32 devices in a mesh: bricks: 32 (over z, y, x, core).
Axes of the slice: x: 2, y: 2, z: 4, core: 2. Of those that a mesh axis runs over, the one named last changes fastest.
Arguments:
- voxels: bfloat16 [192, 64, 512], P('bricks'), may hold values from -6 to 6
- kernel: bfloat16 [64, 8, 3, 3, 3], replicated, may hold values from -0.4375 to 0.4375
- bias: float32 [64], replicated, may hold values from -3 to 3
- cortex: int32 [192, 512], P('bricks'), may hold values 0 or 1
- slot_to_brick: int32 [192], P('bricks'), may hold values from -1 to 95, as said below
- neighbors: int32 [192, 6], P('bricks'), may hold values from -1 to 191, as said below
- cotangent: bfloat16 [192, 64, 512], P('bricks'), may hold values from -6 to 6
Outputs:
- activated: bfloat16 [192, 64, 512], P('bricks')
- input_grad: bfloat16 [192, 64, 512], P('bricks')
- kernel_grad: float32 [64, 8, 3, 3, 3], replicated
- bias_grad: float32 [64], replicated
The draws below stay inside these ranges and needn't reach their ends.
Inputs may be any that keep to these rules, and one draw needn't show every extreme that they name: `slot_to_brick`: the bricks 0 to 95 form a tube of 2 x 2 bricks in cross-section along the first dimension, brick (p, q, r) numbered (p 2 + q) 2 + r. Each device holds a run of consecutive bricks in its first slots, in order, the runs following device order; a device holds 2 to 6 bricks, some device exactly 6; its other slots hold -1. `neighbors`: the slot index of the brick across each face of the slot's brick in that tube, -1 outside the tube and for empty slots; the relation is symmetric. A brick across a face of the first dimension lies on a device at most 2 away, across the other faces at most 1 away, and both distances occur.
All inputs are finite; a program needn't handle non-finite values. No bound on the sum of `cortex` on one device may be relied on, other than what follows from the above.
Results may differ from the reference program's by a relative error of at most 0.0075.
Values may be sent and summed in bfloat16 or wider, within the bound.
No kernel may reach another device: no remote copies, remote signals or barrier semaphores. Data moves between devices by JAX's collectives and lax.ppermute only.
A program may use at most 128 MiB of HBM per device.

```python
import jax
import jax.numpy as jnp
from jax import lax

CHANNEL_COUNT = 64
GROUPS = 8
GC = 8
E = 8
SLOTS = 6
BRICK_VOXELS = 512
TOTAL_SLOTS = 192
NBRICK = 96
N_BRICKS = 32


def deal_bricks(key):
    base_key = jax.random.fold_in(key, 1234)
    group_count = N_BRICKS // 4
    kinds = jax.random.randint(jax.random.fold_in(base_key, 1), (group_count,), 0, 3)
    kinds = kinds.at[0].set(0)
    neighbor_patterns = jnp.array([[6, 2, 2, 2], [4, 4, 2, 2], [3, 3, 3, 3]], dtype=jnp.int32)
    chosen = neighbor_patterns[kinds]
    sub_keys = jax.random.split(jax.random.fold_in(base_key, 2), group_count)
    orders = jax.vmap(lambda sub_key: jax.random.permutation(sub_key, 4))(sub_keys)
    counts = jnp.take_along_axis(chosen, orders, axis=1).reshape(-1).astype(jnp.int32)
    starts = (jnp.cumsum(counts) - counts).astype(jnp.int32)
    positions = jnp.arange(SLOTS, dtype=jnp.int32)
    held = jnp.where(positions[None, :] < counts[:, None], starts[:, None] + positions[None, :], -1)
    return (held.reshape(-1).astype(jnp.int32), starts)


def draw_slot_to_brick(key, part):
    return deal_bricks(key)[0]


def draw_neighbors(key, part):
    held, starts = deal_bricks(key)
    tube_len = NBRICK // 4
    safe = jnp.maximum(held, 0)
    along = safe // 4
    second = safe // 2 % 2
    third = safe % 2
    candidate = jnp.stack([safe - 4, safe + 4, safe - 2, safe + 2, safe - 1, safe + 1], axis=1)
    valid = jnp.stack([along > 0, along < tube_len - 1, second == 1, second == 0, third == 1, third == 0], axis=1)
    valid = valid & (held >= 0)[:, None]
    target = jnp.where(valid, candidate, 0)
    owner = jnp.sum((starts[None, None, :] <= target[:, :, None]).astype(jnp.int32), axis=2) - 1
    slot_index = owner * SLOTS + target - starts[owner]
    return jnp.where(valid, slot_index, -1).astype(jnp.int32)


def plant(result, key, least, top_value):
    spot = [jax.random.randint(jax.random.fold_in(key, axis), (), 0, length) for axis, length in enumerate(result.shape)]
    main_axis = result.shape.index(max(result.shape))
    neighbour = spot[:main_axis] + [(spot[main_axis] + 1) % result.shape[main_axis]] + spot[main_axis + 1:]
    return result.at[tuple(spot)].set(least).at[tuple(neighbour)].set(top_value)


def shard_levels(key, dims, cuts, low, largest):
    level = 1.0
    for dim, blocks in cuts:
        heights = jax.random.uniform(jax.random.fold_in(jax.random.fold_in(key, 6), dim), (blocks,), jnp.float32, low / len(cuts), largest / len(cuts))
        level = level * jnp.repeat(jnp.exp(heights), dims[dim] // blocks).reshape((-1,) + (1,) * (len(dims) - 1 - dim))
    return level


def noise(key, dims, spread, limit, cuts=(), kind=jnp.bfloat16):
    values = jax.random.normal(key, dims, jnp.float32) * spread
    if len(cuts) > 0:
        values = shard_levels(key, dims, cuts, -0.22, 0.18) * values
    return jnp.clip(values, min=-limit, max=limit).astype(kind)


def setup_inputs(seed: int = 0) -> dict:
    arg_keys = jax.random.split(jax.random.key(seed), 8)
    voxels = noise(arg_keys[0], (TOTAL_SLOTS, CHANNEL_COUNT, BRICK_VOXELS), 1.0, 6.0, ((0, 32),))
    kernel = noise(arg_keys[1], (CHANNEL_COUNT, GC, 3, 3, 3), (GC * 27) ** -0.5, 0.4375)
    bias = noise(arg_keys[2], (CHANNEL_COUNT,), 0.5, 3.0, (), jnp.float32)
    cortex = plant((jax.random.randint(arg_keys[3], (TOTAL_SLOTS, BRICK_VOXELS), 0, 3) < 2).astype(jnp.int32), jax.random.fold_in(arg_keys[3], 1), 0, 1)
    slot_to_brick = draw_slot_to_brick(jax.random.fold_in(arg_keys[7], 71), 0)
    neighbors = draw_neighbors(jax.random.fold_in(arg_keys[7], 71), 0)
    cotangent = noise(arg_keys[6], (TOTAL_SLOTS, CHANNEL_COUNT, BRICK_VOXELS), 1.0, 6.0, ((0, 32),))
    return dict(voxels=voxels, kernel=kernel, bias=bias, cortex=cortex, slot_to_brick=slot_to_brick, neighbors=neighbors, cotangent=cotangent)


def follow(link_table, slot_index, facet_position):
    return jnp.where(slot_index >= 0, link_table[jnp.maximum(slot_index, 0), facet_position], -1)

def padded_brick(whole_field, link_table, slot_index):
    edge_len = whole_field.shape[2]
    chosen = {-1: slice(edge_len - 1, edge_len), 0: slice(0, edge_len), 1: slice(0, 1)}
    layers = []
    for step_x in (-1, 0, 1):
        columns = []
        for step_y in (-1, 0, 1):
            entries = []
            for step_z in (-1, 0, 1):
                target = slot_index
                if step_z != 0:
                    target = follow(link_table, target, 4 if step_z < 0 else 5)
                if step_y != 0:
                    target = follow(link_table, target, 2 if step_y < 0 else 3)
                if step_x != 0:
                    target = follow(link_table, target, 0 if step_x < 0 else 1)
                brick_data = whole_field[jnp.maximum(target, 0)]
                window = brick_data[:, chosen[step_x], chosen[step_y], chosen[step_z]]
                entries.append(jnp.where(target >= 0, window, jnp.zeros_like(window)))
            columns.append(jnp.concatenate(entries, axis=3))
        layers.append(jnp.concatenate(columns, axis=2))
    return jnp.concatenate(layers, axis=1)

def grouped(inputs, weights):
    return lax.conv_general_dilated(inputs, weights, (1, 1, 1), 'VALID', dimension_numbers=('NCDHW', 'OIDHW', 'NCDHW'), feature_group_count=GROUPS, precision=lax.Precision.HIGHEST)

def reference(voxels, kernel, bias, cortex, slot_to_brick, neighbors, cotangent):
    slot_count = voxels.shape[0]
    cube = (slot_count, CHANNEL_COUNT, E, E, E)
    fields = voxels.reshape(cube)
    upstream = cotangent.reshape(cube)
    occupied = (slot_to_brick >= 0).astype(jnp.int32)
    keeper = (cortex.reshape(slot_count, E, E, E) * occupied[:, None, None, None]).astype(jnp.float32)
    forward_weights = kernel.astype(jnp.float32)
    six_dim = forward_weights.reshape(GROUPS, GC, GC, 3, 3, 3)
    flipped = jnp.transpose(six_dim, (0, 2, 1, 3, 4, 5))[:, :, :, ::-1, ::-1, ::-1].reshape(CHANNEL_COUNT, GC, 3, 3, 3)
    indices = jnp.arange(slot_count, dtype=jnp.int32)

    def forward_slot(slot_index):
        padded = padded_brick(fields, neighbors, slot_index).astype(jnp.float32)
        pre = grouped(padded[None], forward_weights)[0] + bias[:, None, None, None]
        keep_slot = keeper[slot_index][None]
        sigma = jax.nn.sigmoid(pre)
        activated = (pre * sigma * keep_slot).astype(jnp.bfloat16)
        slope = sigma * (1.0 + pre * (1.0 - sigma))
        dpre = (upstream[slot_index].astype(jnp.float32) * keep_slot * slope).astype(jnp.bfloat16)
        return (activated, dpre)
    activated, dpre_all = lax.map(forward_slot, indices)

    def backward_slot(carry, slot_index):
        kernel_sum, bias_sum = carry
        padded = padded_brick(fields, neighbors, slot_index).astype(jnp.float32)
        grad_pad = padded_brick(dpre_all, neighbors, slot_index).astype(jnp.float32)
        input_grad = grouped(grad_pad[None], flipped)[0].astype(jnp.bfloat16)
        term = dpre_all[slot_index].astype(jnp.float32)
        output_bricks, pullback = jax.vjp(lambda weights_in: grouped(padded[None], weights_in), forward_weights)
        kernel_term = pullback(term[None])[0]
        return ((kernel_sum + kernel_term, bias_sum + lax.optimization_barrier(jnp.sum(term, axis=(1, 2, 3)))), input_grad)
    start = (jnp.zeros_like(forward_weights), jnp.zeros((CHANNEL_COUNT,), jnp.float32))
    totals, input_grad = lax.scan(backward_slot, start, indices)
    return (activated.reshape(slot_count, CHANNEL_COUNT, BRICK_VOXELS), input_grad.reshape(slot_count, CHANNEL_COUNT, BRICK_VOXELS), totals[0], totals[1])
```

```python
import jax
import jax.numpy as jnp
import numpy as np
from jax import lax
from jax.sharding import PartitionSpec as P

CHANNEL_COUNT = 64
GROUPS = 8
GC = 8
E = 8


def passed_along(block, axis, distance):
    devices = range(lax.axis_size(axis))
    route = [(i - distance, i) for i in devices if i - distance in devices]
    return lax.ppermute(block, axis, route)


def layer_of(array_in, axis_pos, which):
    index_list = [slice(None), slice(None), slice(None)]
    index_list[axis_pos] = which
    return array_in[tuple(index_list)]


def static_tables(grid_shape, axis_pos):
    count = int(np.prod(grid_shape))
    old_index = np.arange(count).reshape(grid_shape)
    lower = layer_of(old_index, axis_pos, 0).ravel()
    upper = layer_of(old_index, axis_pos, grid_shape[axis_pos] - 1).ravel()
    facet = lower.shape[0]
    grown = list(grid_shape)
    grown[axis_pos] = grown[axis_pos] + 2
    grown_count = int(np.prod(grown))
    new_index = np.arange(grown_count).reshape(grown)
    middle = layer_of(new_index, axis_pos, slice(1, grid_shape[axis_pos] + 1)).ravel()
    low_pos = layer_of(new_index, axis_pos, 0).ravel()
    high_pos = layer_of(new_index, axis_pos, grown[axis_pos] - 1).ravel()
    facet_ids = np.arange(facet)
    select = np.zeros((count, 2 * facet), np.float32)
    select[lower, facet_ids] = 1.0
    select[upper, facet + facet_ids] = 1.0
    place_mid = np.zeros((count, grown_count), np.float32)
    place_mid[np.arange(count), middle] = 1.0
    place_low = np.zeros((facet, grown_count), np.float32)
    place_low[facet_ids, low_pos] = 1.0
    place_high = np.zeros((facet, grown_count), np.float32)
    place_high[facet_ids, high_pos] = 1.0
    return (tuple(grown), facet, select, place_mid, place_low, place_high)


def place(values, table):
    return jnp.einsum(
        "scn,nm->scm", values, jnp.asarray(table, jnp.bfloat16), preferred_element_type=jnp.float32
    )


def extend(field_flat, grid_shape, axis_pos, home, within, offsets):
    grown, facet, select, place_mid, place_low, place_high = static_tables(grid_shape, axis_pos)
    slot_count = field_flat.shape[0]
    both_layers = (
        place(field_flat, select).astype(jnp.bfloat16).reshape(slot_count, CHANNEL_COUNT, 2, facet)
    )
    layers = jnp.transpose(both_layers, (0, 2, 1, 3))
    if axis_pos == 0:
        packed = layers.reshape(slot_count * 2 * CHANNEL_COUNT * facet // 128, 128)
        stacked = lax.all_gather(packed, "bricks").reshape((-1,) + layers.shape)[:, :, ::-1]
        count = lax.axis_size("bricks")
        reach_list = jnp.arange(count, dtype=jnp.int32) - lax.axis_index("bricks")
    else:
        sources = [layers]
        for offset in offsets:
            sources.append(passed_along(layers, "bricks", -offset))
        stacked = jnp.stack(sources, axis=0)[:, :, ::-1]
        reach_list = jnp.array((0,) + tuple(offsets), dtype=jnp.int32)
    slot_ids = jnp.arange(slot_count, dtype=jnp.int32)
    picks = (home[:, :, None, None] == reach_list[None, None, :, None]) & (
        within[:, :, None, None] == slot_ids[None, None, None, :]
    )
    halos = jnp.einsum(
        "sukt,ktucr->sucr", picks.astype(jnp.bfloat16), stacked, preferred_element_type=jnp.float32
    ).astype(jnp.bfloat16)
    lower_halo = halos[:, 0]
    upper_halo = halos[:, 1]
    grown_flat = (
        place(field_flat, place_mid) + place(lower_halo, place_low) + place(upper_halo, place_high)
    )
    return (grown_flat.astype(jnp.bfloat16), grown)


def pad_field(field_flat, home, within):
    padded = field_flat
    grid_shape = (E, E, E)
    for dim_pos in range(3):
        offsets = (-1, 1)
        padded, grid_shape = extend(
            padded,
            grid_shape,
            dim_pos,
            home[:, 2 * dim_pos : 2 * dim_pos + 2],
            within[:, 2 * dim_pos : 2 * dim_pos + 2],
            offsets,
        )
    return padded


def flip_kernel(kernel):
    six_dim = kernel.reshape(GROUPS, GC, GC, 3, 3, 3)
    return jnp.transpose(six_dim, (0, 2, 1, 3, 4, 5))[:, :, :, ::-1, ::-1, ::-1].reshape(
        CHANNEL_COUNT, GC, 3, 3, 3
    )


def wide_length():
    side = E + 2
    return (E - 1) * side * side + (E - 1) * side + E


def wide_table():
    side = E + 2
    voxel_ids = np.arange(E * E * E)
    positions = voxel_ids // (E * E) * side * side + voxel_ids // E % E * side + voxel_ids % E
    table = np.zeros((wide_length(), E * E * E), np.float32)
    table[positions, voxel_ids] = 1.0
    return table


def tap_stack(padded_flat):
    full_len = padded_flat.shape[2]
    return jnp.stack(
        [padded_flat[:, :, step_c : step_c + full_len - 2] for step_c in range(3)], axis=1
    )


def convolve(tapped, weights):
    slot_count = tapped.shape[0]
    side = E + 2
    span = wide_length()
    in_count = weights.shape[1]
    group_count = CHANNEL_COUNT // in_count
    view = tapped.reshape(slot_count, 3, group_count, in_count, tapped.shape[3])
    shaped = weights.reshape(group_count, CHANNEL_COUNT // group_count, in_count, 3, 3, 3)
    running = jnp.zeros((slot_count, group_count, CHANNEL_COUNT // group_count, span), jnp.float32)
    for step_a in range(3):
        for step_b in range(3):
            tap_base = step_a * side * side + step_b * side
            window = view[:, :, :, :, tap_base : tap_base + span]
            running = running + jnp.einsum(
                "scgil,goic->sgol",
                window,
                shaped[:, :, :, step_a, step_b, :],
                preferred_element_type=jnp.float32,
            )
    return running.reshape(slot_count, CHANNEL_COUNT, span)


def extract(wide_values, table):
    return jnp.einsum(
        "scl,lv->scv",
        wide_values,
        table,
        precision=lax.Precision.HIGHEST,
        preferred_element_type=jnp.float32,
    )


def shards(voxels, kernel, bias, cortex, slot_to_brick, neighbors, cotangent):
    slot_count = voxels.shape[0]
    side = E + 2
    span = wide_length()
    device = lax.axis_index("bricks")
    linked = neighbors >= 0
    home = jnp.where(linked, neighbors // slot_count - device, 99)
    within = jnp.where(linked, neighbors % slot_count, 0)
    occupied = (slot_to_brick >= 0).astype(jnp.int32)
    keeper = (cortex * occupied[:, None]).astype(jnp.float32)[:, None, :]
    table_np = wide_table()
    table_exact = jnp.asarray(table_np, jnp.float32)
    table_half = jnp.asarray(table_np, jnp.bfloat16)
    backward_kernel = flip_kernel(kernel)
    padded = pad_field(voxels, home, within)
    tapped = tap_stack(padded)
    pre = extract(convolve(tapped, kernel), table_exact) + bias[None, :, None]
    sigma = jax.nn.sigmoid(pre)
    activated = (pre * sigma * keeper).astype(jnp.bfloat16)
    slope = sigma * (1.0 + pre * (1.0 - sigma))
    dpre = (cotangent.astype(jnp.float32) * keeper * slope).astype(jnp.bfloat16)
    grad_pad = pad_field(dpre, home, within)
    input_grad = extract(convolve(tap_stack(grad_pad), backward_kernel), table_exact).astype(
        jnp.bfloat16
    )
    dwide = jnp.einsum("scv,lv->scl", dpre, table_half, preferred_element_type=jnp.float32).astype(
        jnp.bfloat16
    )
    grad_groups = dwide.reshape(slot_count, GROUPS, GC, span)
    view = tapped.reshape(slot_count, 3, GROUPS, GC, tapped.shape[3])
    tap_terms = []
    for step_a in range(3):
        for step_b in range(3):
            tap_base = step_a * side * side + step_b * side
            window = view[:, :, :, :, tap_base : tap_base + span]
            tap_terms.append(
                jnp.einsum(
                    "sgol,scgil->goic", grad_groups, window, preferred_element_type=jnp.float32
                )
            )
    stacked_terms = jnp.stack(tap_terms, axis=0).reshape(3, 3, GROUPS, GC, GC, 3)
    device_kernel = jnp.transpose(stacked_terms, (2, 3, 4, 0, 1, 5)).reshape(
        CHANNEL_COUNT, GC, 3, 3, 3
    )
    bias_local = jnp.sum(dpre.astype(jnp.float32), axis=(0, 2))
    flat = jnp.concatenate(
        [
            device_kernel.reshape(CHANNEL_COUNT * 27 * GC // 128, 128),
            jnp.pad(bias_local, (0, 64)).reshape(1, 128),
            jnp.zeros((3, 128), jnp.float32),
        ],
        axis=0,
    )
    total = jnp.sum(lax.all_gather(flat, "bricks"), axis=0)
    kernel_grad = total[: CHANNEL_COUNT * 27 * GC // 128].reshape(CHANNEL_COUNT, GC, 3, 3, 3)
    bias_grad = total[CHANNEL_COUNT * 27 * GC // 128, :CHANNEL_COUNT]
    return (activated, input_grad, kernel_grad, bias_grad)


def solution(mesh):
    return jax.shard_map(
        shards,
        mesh=mesh,
        in_specs=(
            P("bricks", None, None),
            P(),
            P(),
            P("bricks", None),
            P("bricks"),
            P("bricks", None),
            P("bricks", None, None),
        ),
        out_specs=(P("bricks", None, None), P("bricks", None, None), P(), P()),
        check_vma=False,
    )
```

```python
import functools

import jax
import jax.numpy as jnp
import numpy as np
from jax import lax
from jax.experimental import pallas as pl
from jax.experimental.pallas import tpu as pltpu
from jax.sharding import PartitionSpec as P

CH = 64
GC = 8
TILE = 128
NEAR = 7
EDGE = 3
HEAD = 16
SUM_ROWS = 160
BF = jnp.bfloat16
F32 = jnp.float32


@functools.cache
def tables():
    strips = np.zeros((4, 512, TILE), np.float32)
    spread = np.zeros((384, 4 * TILE), np.float32)
    ends = np.zeros((4, 384, TILE), np.float32)
    shifts = np.zeros((4, 256, 9 * TILE), np.float32)
    for half in range(2):
        for xx in range(4):
            for w in range(8):
                i, xp = 2 * half + xx // 2, xx % 2
                spread[half * 64 + xx * 8 + w, i * TILE + xp * 8 + w] = 1
                spread[128 + half * 64 + 32 + xx * 8 + w, i * TILE + 32 + xp * 8 + w] = 1
                spread[256 + half * 64 + xx * 8 + w, i * TILE + 64 + xp * 8 + w] = 1
    for t in range(4):
        q, r = t // 2, t % 2
        own_y, own_z = (0 if q else 7), (0 if r else 7)
        far_y, far_z = 7 - own_y, 7 - own_z
        for half in range(2):
            for xx in range(4):
                for w in range(8):
                    plane = (4 * half + xx) * 64
                    strips[t, plane + own_y * 8 + w, half * 64 + xx * 8 + w] = 1
                    strips[t, plane + w * 8 + own_z, half * 64 + 32 + xx * 8 + w] = 1
        for xp in range(2):
            for w in range(8):
                ends[t, xp * 64 + far_y * 8 + w, xp * 8 + w] = 1
                ends[t, 128 + xp * 64 + w * 8 + far_z, 32 + xp * 8 + w] = 1
                ends[t, 256 + xp * 64 + far_y * 8 + w, 64 + xp * 8 + w] = 1
        out_y, out_z = (-1 if q else 8), (-1 if r else 8)
        for b in range(3):
            for c in range(3):
                for xp in range(2):
                    for y in range(8):
                        for z in range(8):
                            yy, zz = y + b - 1, z + c - 1
                            in_y, in_z = 0 <= yy < 8, 0 <= zz < 8
                            if in_y and in_z:
                                k = xp * 64 + yy * 8 + zz
                            elif in_z and yy == out_y:
                                k = 128 + xp * 8 + zz
                            elif in_y and zz == out_z:
                                k = 160 + xp * 8 + yy
                            elif yy == out_y and zz == out_z:
                                k = 192 + xp * 8 + far_z
                            else:
                                continue
                            shifts[t, k, (b * 3 + c) * TILE + xp * 64 + y * 8 + z] = 1
    return strips, spread, ends, shifts


def left_half(shape):
    return lax.broadcasted_iota(jnp.int32, shape, len(shape) - 1) % TILE < 64


def join_halves(left, right):
    mixed = jnp.where(left_half(left.shape), left.astype(F32), right.astype(F32))
    return mixed.astype(left.dtype)


def dot(a, b):
    return jnp.dot(a, b, preferred_element_type=F32)


def count_own(slot_ref):
    total = jnp.int32(0)
    for s in range(slot_ref.shape[0]):
        total = total + (slot_ref[s] >= 0).astype(jnp.int32)
    return total


def count_sent(head):
    return jnp.max(head.astype(F32)).astype(jnp.int32)


def kind_of(brick):
    return jnp.maximum(brick, 0) & 3


def pack_bricks(slot_ref, field_ref, strips_ref, msg_ref):
    slots = field_ref.shape[0]
    for s in range(slots):
        table = strips_ref[kind_of(slot_ref[s])]
        row = s * 2 * CH
        msg_ref[row : row + CH, :] = dot(field_ref[s], table).astype(BF)
        msg_ref[row + CH : row + 2 * CH, :] = join_halves(
            field_ref[s, :, 0:TILE], field_ref[s, :, 3 * TILE : 4 * TILE]
        )
    row = slots * 2 * CH
    count = count_own(slot_ref).astype(F32)
    msg_ref[row : row + HEAD, :] = jnp.full((HEAD, TILE), count, F32).astype(BF)


def pack_kernel(slot_ref, field_ref, strips_ref, msg_ref):
    pack_bricks(slot_ref, field_ref, strips_ref, msg_ref)


def route_body(slot_ref, own_ref, mate_ref, near_ref, far_ref, box):
    slots = slot_ref.shape[0]
    odd = (lax.axis_index("bricks") & 1) == 1
    mine = count_own(slot_ref)
    head = slots * 2 * CH
    other = count_sent(mate_ref[head : head + HEAD, :])
    for s in range(2 * slots):
        box[s] = own_ref[s * CH : (s + 1) * CH, :]
        box[2 * slots + s] = mate_ref[s * CH : (s + 1) * CH, :]
    for j in range(NEAR):
        up = jnp.where(j < mine, mine - 1 - j, slots + other - 1 - (j - mine))
        down = jnp.where(j < mine, j, slots + j - mine)
        at = jnp.clip(jnp.where(odd, up, down), 0, 2 * slots - 1)
        near_ref[j * CH : (j + 1) * CH, :] = box[2 * at + 1]
        if j < EDGE:
            near_ref[(NEAR + j) * CH : (NEAR + j + 1) * CH, :] = box[2 * at]
            far_ref[j * CH : (j + 1) * CH, :] = box[2 * at + 1]
    row = (NEAR + EDGE) * CH
    both = (mine + other).astype(F32)
    near_ref[row : row + HEAD, :] = jnp.full((HEAD, TILE), both, F32).astype(BF)


def route_kernel(slot_ref, own_ref, mate_ref, near_ref, far_ref, box):
    route_body(slot_ref, own_ref, mate_ref, near_ref, far_ref, box)


def route_sum_kernel(slot_ref, own_ref, mate_ref, near_ref, far_ref, sum_ref, box):
    route_body(slot_ref, own_ref, mate_ref, near_ref, far_ref, box)
    high = slot_ref.shape[0] * 2 * CH + HEAD
    low = high + SUM_ROWS
    parts = []
    for ref in (own_ref, mate_ref):
        parts.append(
            ref[high : high + SUM_ROWS, :].astype(F32) + ref[low : low + SUM_ROWS, :].astype(F32)
        )
    sum_ref[...] = parts[0] + parts[1]


def weight_kernel(taps_ref, forward_ref, backward_ref, work):
    values = taps_ref[...].astype(F32)
    lanes = lax.broadcasted_iota(jnp.int32, (GC, CH), 1) // GC

    def block(tap):
        tile = values[tap * GC : (tap + 1) * GC, :]
        return jnp.concatenate([jnp.where(lanes == g, tile, 0.0) for g in range(CH // GC)], axis=0)

    work[...] = jnp.zeros_like(work)
    for bc in range(9):
        rows = slice(bc * CH, (bc + 1) * CH)
        work[rows, 0:TILE] = jnp.concatenate([block(bc), block(9 + bc)], axis=1)
        work[rows, TILE : TILE + CH] = block(18 + bc)
    turned = work[...].T
    forward_ref[...] = turned[0 : 3 * CH, 0 : 9 * CH].astype(BF)
    for a in range(3):
        rows = slice(a * CH, (a + 1) * CH)
        base = (2 - a) * 9 + 8
        for bc in range(0, 8, 2):
            pair = jnp.concatenate([block(base - bc), block(base - bc - 1)], axis=1)
            backward_ref[rows, bc * CH : (bc + 2) * CH] = pair.astype(BF)
        backward_ref[rows, 8 * CH : 9 * CH] = block(base - 8).astype(BF)


def make_finder(slot_ref, mate_ref, first_ref, second_ref, first_far_ref, second_far_ref, planes, strips):
    slots = slot_ref.shape[0]
    odd = (lax.axis_index("bricks") & 1) == 1
    base = slot_ref[0]
    mine = count_own(slot_ref)
    head = slots * 2 * CH
    other = count_sent(mate_ref[head : head + HEAD, :])
    row = (NEAR + EDGE) * CH
    counts = [count_sent(ref[row : row + HEAD, :]) for ref in (first_ref, second_ref)]
    for s in range(slots):
        strips[slots + s] = mate_ref[s * 2 * CH : s * 2 * CH + CH, :]
        planes[slots + s] = mate_ref[s * 2 * CH + CH : (s + 1) * 2 * CH, :]
    for side, (near, far) in enumerate(((first_ref, first_far_ref), (second_ref, second_far_ref))):
        for j in range(NEAR):
            planes[2 * slots + side * NEAR + j] = near[j * CH : (j + 1) * CH, :]
        for j in range(EDGE):
            strips[2 * slots + side * EDGE + j] = near[(NEAR + j) * CH : (NEAR + j + 1) * CH, :]
            planes[2 * slots + 2 * NEAR + side * EDGE + j] = far[j * CH : (j + 1) * CH, :]
    nothing = 2 * slots + 2 * NEAR + 2 * EDGE
    planes[nothing] = jnp.zeros((CH, TILE), BF)
    low_side = odd.astype(jnp.int32)
    high_side = 1 - low_side
    low_count = jnp.where(odd, counts[1], counts[0])
    high_count = jnp.where(odd, counts[0], counts[1])
    mate_first = jnp.where(odd, base - other, base + mine)
    chip_low = jnp.where(odd, base - other, base)
    chip_high = jnp.where(odd, base + mine, base + mine + other)

    def on_chip(brick):
        own = (brick >= base) & (brick < base + mine)
        return jnp.where(own, brick - base, slots + brick - mate_first)

    def find_strip(brick):
        low = 2 * slots + low_side * EDGE + (chip_low - 1 - brick)
        high = 2 * slots + high_side * EDGE + (brick - chip_high)
        at = jnp.where(brick < chip_low, low, jnp.where(brick >= chip_high, high, on_chip(brick)))
        return jnp.clip(at, 0, 2 * slots + 2 * EDGE - 1)

    def outside(distance, count, side):
        near = 2 * slots + side * NEAR + distance
        far = 2 * slots + 2 * NEAR + side * EDGE + distance - count
        return jnp.where(distance < count, near, far)

    def find_plane(brick, exists):
        low = outside(chip_low - 1 - brick, low_count, low_side)
        high = outside(brick - chip_high, high_count, high_side)
        at = jnp.where(brick < chip_low, low, jnp.where(brick >= chip_high, high, on_chip(brick)))
        return jnp.clip(jnp.where(exists, at, nothing), 0, nothing)

    return base, mine, find_strip, find_plane


def convolve_brick(
    s, base, find_strip, find_plane, link_ref, field_ref, planes, strips,
    spread_ref, ends_ref, shifts_ref, weight_ref, mixed, taps, sums,
):
    brick = base + s
    kind = brick & 3
    step_y = 2 - 2 * (kind & 2)
    step_z = 1 - 2 * (kind & 1)
    sides = (brick + step_y, brick + step_z, brick + step_y + step_z)
    has_low = link_ref[s, 0] >= 0
    has_high = link_ref[s, 1] >= 0

    def outer(near):
        high = planes[find_plane(near + 4, has_high)]
        low = planes[find_plane(near - 4, has_low)]
        return join_halves(high, low)

    beside = jnp.concatenate([strips[find_strip(m)] for m in sides], axis=1)
    halo = dot(beside, spread_ref[...]).astype(BF)
    outer_beside = jnp.concatenate([outer(m) for m in sides], axis=1)
    for i in range(4):
        rows = slice(i * CH, (i + 1) * CH)
        mixed[rows, 0:TILE] = field_ref[s, :, i * TILE : (i + 1) * TILE]
        mixed[rows, TILE:] = halo[:, i * TILE : (i + 1) * TILE]
    mixed[4 * CH :, 0:TILE] = outer(brick)
    mixed[4 * CH :, TILE:] = dot(outer_beside, ends_ref[kind]).astype(BF)
    for bc in range(0, 9, 2):
        wide = min(2, 9 - bc)
        part = dot(mixed[...], shifts_ref[kind, :, bc * TILE : (bc + wide) * TILE]).astype(BF)
        for e in range(wide):
            for i in range(5):
                taps[(bc + e) * CH : (bc + e + 1) * CH, i * TILE : (i + 1) * TILE] = part[
                    i * CH : (i + 1) * CH, e * TILE : (e + 1) * TILE
                ]
    sums[...] = dot(weight_ref[...], taps[0 : 9 * CH, :])
    turned = []
    for a in (0, 2):
        rows = slice(a * CH, (a + 1) * CH)
        turned.append(
            [pltpu.roll(sums[rows, i * TILE : (i + 1) * TILE], 64, 1) for i in range(5)]
        )
    left = left_half((CH, TILE))
    tiles = []
    for i in range(4):
        lower = jnp.where(left, turned[0][(i - 1) % 5], turned[0][i])
        upper = jnp.where(left, turned[1][i], turned[1][i + 1])
        tiles.append(sums[CH : 2 * CH, i * TILE : (i + 1) * TILE] + lower + upper)
    return tiles


def forward_kernel(
    slot_ref, link_ref, field_ref, own_ref, mate_ref, first_ref, second_ref, first_far_ref,
    second_far_ref, weight_ref, bias_ref, cortex_ref, upstream_ref, strips_ref, spread_ref,
    ends_ref, shifts_ref, out_ref, dpre_ref, msg_ref,
    planes, strips, mixed, taps, sums, spots, grads, keeps,
):
    slots = field_ref.shape[0]
    base, mine, find_strip, find_plane = make_finder(
        slot_ref, mate_ref, first_ref, second_ref, first_far_ref, second_far_ref, planes, strips
    )
    for s in range(slots):
        strips[s] = own_ref[s * 2 * CH : s * 2 * CH + CH, :]
        planes[s] = own_ref[s * 2 * CH + CH : (s + 1) * 2 * CH, :]
        keeps[s] = jnp.broadcast_to(cortex_ref[s : s + 1, :].astype(F32), (8, 512))
    taps[9 * CH :, :] = jnp.ones((HEAD, 5 * TILE), BF)
    grads[...] = jnp.zeros_like(grads)
    for s in range(slots):

        @pl.when(s >= mine)
        def _():
            out_ref[s] = jnp.zeros((CH, 512), BF)
            dpre_ref[s] = jnp.zeros((CH, 512), BF)

    square = (CH, CH)
    diagonal = lax.broadcasted_iota(jnp.int32, square, 0) == lax.broadcasted_iota(jnp.int32, square, 1)
    bias = jnp.sum(jnp.where(diagonal, bias_ref[...], 0.0), axis=1, keepdims=True)
    left = left_half((CH, TILE))
    zero = jnp.zeros((CH, TILE), F32)

    def one_brick(s, carry):
        tiles = convolve_brick(
            s, base, find_strip, find_plane, link_ref, field_ref, planes, strips,
            spread_ref, ends_ref, shifts_ref, weight_ref, mixed, taps, sums,
        )
        turned = []
        for i in range(4):
            lanes = slice(i * TILE, (i + 1) * TILE)
            pre = tiles[i] + bias
            keep = keeps[s, 0:1, lanes]
            sigma = 1.0 / (1.0 + jnp.exp(-pre))
            out_ref[s, :, lanes] = (pre * sigma * keep).astype(BF)
            slope = sigma * (1.0 + pre * (1.0 - sigma))
            dpre = (upstream_ref[s, :, lanes].astype(F32) * keep * slope).astype(BF)
            dpre_ref[s, :, lanes] = dpre
            spots[CH : 2 * CH, lanes] = dpre
            turned.append(pltpu.roll(dpre.astype(F32), 64, 1))
        spots[CH : 2 * CH, 4 * TILE :] = jnp.zeros((CH, TILE), BF)
        turned.append(zero)
        for i in range(4):
            lanes = slice(i * TILE, (i + 1) * TILE)
            spots[0:CH, lanes] = jnp.where(left, turned[i], turned[i + 1]).astype(BF)
            before = turned[i - 1] if i else zero
            spots[2 * CH :, lanes] = jnp.where(left, before, turned[i]).astype(BF)
        spots[0:CH, 4 * TILE :] = jnp.where(left, 0.0, turned[0]).astype(BF)
        spots[2 * CH :, 4 * TILE :] = jnp.where(left, turned[3], 0.0).astype(BF)
        grads[...] += lax.dot_general(
            taps[...], spots[...], (((1,), (1,)), ((), ())), preferred_element_type=F32
        )
        return carry

    lax.fori_loop(0, mine, one_brick, 0)

    pack_bricks(slot_ref, dpre_ref, strips_ref, msg_ref)
    high = slots * 2 * CH + HEAD
    low = high + SUM_ROWS
    group = lax.broadcasted_iota(jnp.int32, (GC, TILE), 1) % CH // GC
    for half, lanes in enumerate((slice(0, TILE), slice(TILE, TILE + CH))):
        group_here = group[:, : lanes.stop - lanes.start]
        rows = []
        for bc in range(9):
            total = jnp.zeros(group_here.shape, F32)
            for g in range(CH // GC):
                at = bc * CH + g * GC
                total = total + jnp.where(group_here == g, grads[at : at + GC, lanes], 0.0)
            rows.append(total)
        rows.append(grads[9 * CH : 9 * CH + GC, lanes])
        full = jnp.concatenate(rows, axis=0)
        if full.shape[1] < TILE:
            full = jnp.concatenate([full, jnp.zeros((10 * GC, TILE - full.shape[1]), F32)], axis=1)
        rounded = full.astype(BF)
        at = half * 10 * GC
        msg_ref[high + at : high + at + 10 * GC, :] = rounded
        msg_ref[low + at : low + at + 10 * GC, :] = (full - rounded.astype(F32)).astype(BF)


def backward_kernel(
    slot_ref, link_ref, field_ref, own_ref, mate_ref, first_ref, second_ref, first_far_ref,
    second_far_ref, weight_ref, spread_ref, ends_ref, shifts_ref, out_ref,
    planes, strips, mixed, taps, sums,
):
    slots = field_ref.shape[0]
    base, mine, find_strip, find_plane = make_finder(
        slot_ref, mate_ref, first_ref, second_ref, first_far_ref, second_far_ref, planes, strips
    )
    for s in range(slots):
        strips[s] = own_ref[s * 2 * CH : s * 2 * CH + CH, :]
        planes[s] = own_ref[s * 2 * CH + CH : (s + 1) * 2 * CH, :]

        @pl.when(s >= mine)
        def _():
            out_ref[s] = jnp.zeros((CH, 512), BF)

    def one_brick(s, carry):
        tiles = convolve_brick(
            s, base, find_strip, find_plane, link_ref, field_ref, planes, strips,
            spread_ref, ends_ref, shifts_ref, weight_ref, mixed, taps, sums,
        )
        for i in range(4):
            out_ref[s, :, i * TILE : (i + 1) * TILE] = tiles[i].astype(BF)
        return carry

    lax.fori_loop(0, mine, one_brick, 0)


def finish_kernel(a_ref, b_ref, kernel_ref, bias_ref):
    first = a_ref[0 : 10 * GC, :] + b_ref[0 : 10 * GC, :]
    second = a_ref[10 * GC :, :] + b_ref[10 * GC :, :]
    turned = pltpu.roll(first, 64, 1)
    for a, part in enumerate((first, turned, second)):
        kernel_ref[a * 9 * GC : (a + 1) * 9 * GC, :] = part[0 : 9 * GC, 0:CH]
    bias_ref[...] = turned[9 * GC : 9 * GC + 1, 0:CH]


VMEM = pl.BlockSpec(memory_space=pltpu.VMEM)
SMEM = pl.BlockSpec(memory_space=pltpu.SMEM)


def call(kernel, ins, outs, scratch=(), flops=0, size=400000):
    return pl.pallas_call(
        kernel,
        in_specs=ins,
        out_specs=tuple(VMEM for _ in outs),
        out_shape=tuple(outs),
        scratch_shapes=list(scratch),
        compiler_params=pltpu.CompilerParams(vmem_limit_bytes=40 * 2**20),
        cost_estimate=pl.CostEstimate(flops=flops, bytes_accessed=size, transcendentals=0),
    )


def sent(block, route):
    return lax.ppermute(block, "bricks", route)


def shards(voxels, kernel, bias, cortex, slot_to_brick, neighbors, cotangent):
    slots = voxels.shape[0]
    devices = lax.axis_size("bricks")
    strips, spread, ends, shifts = (jnp.asarray(t, BF) for t in tables())
    shape = jax.ShapeDtypeStruct
    pack_rows = slots * 2 * CH + HEAD
    near_shape = shape(((NEAR + EDGE) * CH + HEAD, TILE), BF)
    far_shape = shape((EDGE * CH, TILE), BF)

    def routes(near, far):
        out = []
        for chips, which in ((1, near), (1, near), (2, far), (2, far)):
            further = len(out) % 2
            pairs = []
            for d in range(devices):
                to = d + 2 * chips - 1 + further if d % 2 else d - 2 * chips + 1 - further
                if 0 <= to < devices:
                    pairs.append((d, to))
            out.append(sent(which, pairs))
        return out

    def swapped(block, mask):
        return sent(block, [(d, d ^ mask) for d in range(devices)])

    box = [pltpu.VMEM((4 * slots, CH, TILE), BF)]
    work = [
        pltpu.VMEM((2 * slots + 2 * NEAR + 2 * EDGE + 1, CH, TILE), BF),
        pltpu.VMEM((2 * slots + 2 * EDGE, CH, TILE), BF),
        pltpu.VMEM((5 * CH, 2 * TILE), BF),
        pltpu.VMEM((9 * CH + HEAD, 5 * TILE), BF),
        pltpu.VMEM((3 * CH, 5 * TILE), F32),
    ]
    field = shape(voxels.shape, BF)

    (own,) = call(pack_kernel, [SMEM, VMEM, VMEM], [shape((pack_rows, TILE), BF)])(
        slot_to_brick, voxels, strips
    )
    mate = swapped(own, 1)
    weight_shape = shape((3 * CH, 9 * CH), BF)
    taps = jnp.transpose(kernel, (2, 3, 4, 1, 0)).reshape(27 * GC, CH)
    forward, backward = call(
        weight_kernel, [VMEM], [weight_shape] * 2, [pltpu.VMEM((640, 256), F32)]
    )(taps)
    near, far = call(route_kernel, [SMEM, VMEM, VMEM], [near_shape, far_shape], box)(
        slot_to_brick, own, mate
    )
    received = routes(near, far)
    activated, dpre, own = call(
        forward_kernel,
        [SMEM, SMEM] + [VMEM] * 15,
        [field, field, shape((pack_rows + 2 * SUM_ROWS, TILE), BF)],
        work
        + [
            pltpu.VMEM((3 * CH, 5 * TILE), BF),
            pltpu.VMEM((9 * CH + HEAD, 3 * CH), F32),
            pltpu.VMEM((slots, 8, 512), F32),
        ],
        flops=4 * 10**9,
    )(
        slot_to_brick, neighbors, voxels, own, mate, *received, forward, bias.reshape(1, CH),
        cortex, cotangent, strips, spread, ends, shifts,
    )
    mate = swapped(own, 1)
    near, far, total = call(
        route_sum_kernel,
        [SMEM, VMEM, VMEM],
        [near_shape, far_shape, shape((SUM_ROWS, TILE), F32)],
        box,
    )(slot_to_brick, own, mate)
    masks = [2**p for p in range(1, devices.bit_length() - 1)]
    for mask in masks[:-1]:
        total = total + swapped(total, mask)
    other = swapped(total, masks[-1])
    received = routes(near, far)
    (input_grad,) = call(
        backward_kernel, [SMEM, SMEM] + [VMEM] * 11, [field], work, flops=2 * 10**9
    )(
        slot_to_brick, neighbors, dpre, own, mate, *received, backward, spread, ends, shifts
    )
    kernel_sum, bias_sum = call(
        finish_kernel, [VMEM, VMEM], [shape((27 * GC, CH), F32), shape((1, CH), F32)]
    )(total, other)
    kernel_grad = jnp.transpose(kernel_sum.reshape(3, 3, 3, GC, CH), (4, 3, 0, 1, 2))
    return (activated, input_grad, kernel_grad, bias_sum.reshape(CH))


def solution(mesh):
    devices = mesh.shape["bricks"]
    assert devices & (devices - 1) == 0
    return jax.shard_map(
        shards,
        mesh=mesh,
        in_specs=(
            P("bricks", None, None),
            P(),
            P(),
            P("bricks", None),
            P("bricks"),
            P("bricks", None),
            P("bricks", None, None),
        ),
        out_specs=(P("bricks", None, None), P("bricks", None, None), P(), P()),
        check_vma=False,
    )
```

```python
import functools

import jax
import jax.numpy as jnp
import numpy as np
from jax import lax
from jax.experimental import pallas as pl
from jax.experimental.pallas import tpu as pltpu
from jax.sharding import PartitionSpec as P

CH = 64
GC = 8
TILE = 128
NEAR = 7
EDGE = 3
HEAD = 16
SUM_ROWS = 160
BF = jnp.bfloat16
F32 = jnp.float32


@functools.cache
def tables():
    strips = np.zeros((4, 512, TILE), np.float32)
    spread = np.zeros((384, 4 * TILE), np.float32)
    ends = np.zeros((4, 384, TILE), np.float32)
    shifts = np.zeros((4, 256, 9 * TILE), np.float32)
    for half in range(2):
        for xx in range(4):
            for w in range(8):
                i, xp = 2 * half + xx // 2, xx % 2
                spread[half * 64 + xx * 8 + w, i * TILE + xp * 8 + w] = 1
                spread[128 + half * 64 + 32 + xx * 8 + w, i * TILE + 32 + xp * 8 + w] = 1
                spread[256 + half * 64 + xx * 8 + w, i * TILE + 64 + xp * 8 + w] = 1
    for t in range(4):
        q, r = t // 2, t % 2
        own_y, own_z = (0 if q else 7), (0 if r else 7)
        far_y, far_z = 7 - own_y, 7 - own_z
        for half in range(2):
            for xx in range(4):
                for w in range(8):
                    plane = (4 * half + xx) * 64
                    strips[t, plane + own_y * 8 + w, half * 64 + xx * 8 + w] = 1
                    strips[t, plane + w * 8 + own_z, half * 64 + 32 + xx * 8 + w] = 1
        for xp in range(2):
            for w in range(8):
                ends[t, xp * 64 + far_y * 8 + w, xp * 8 + w] = 1
                ends[t, 128 + xp * 64 + w * 8 + far_z, 32 + xp * 8 + w] = 1
                ends[t, 256 + xp * 64 + far_y * 8 + w, 64 + xp * 8 + w] = 1
        out_y, out_z = (-1 if q else 8), (-1 if r else 8)
        for b in range(3):
            for c in range(3):
                for xp in range(2):
                    for y in range(8):
                        for z in range(8):
                            yy, zz = y + b - 1, z + c - 1
                            in_y, in_z = 0 <= yy < 8, 0 <= zz < 8
                            if in_y and in_z:
                                k = xp * 64 + yy * 8 + zz
                            elif in_z and yy == out_y:
                                k = 128 + xp * 8 + zz
                            elif in_y and zz == out_z:
                                k = 160 + xp * 8 + yy
                            elif yy == out_y and zz == out_z:
                                k = 192 + xp * 8 + far_z
                            else:
                                continue
                            shifts[t, k, (b * 3 + c) * TILE + xp * 64 + y * 8 + z] = 1
    return strips, spread, ends, shifts


def left_half(shape):
    return lax.broadcasted_iota(jnp.int32, shape, len(shape) - 1) % TILE < 64


def join_halves(left, right):
    mixed = jnp.where(left_half(left.shape), left.astype(F32), right.astype(F32))
    return mixed.astype(left.dtype)


def dot(a, b):
    return jnp.dot(a, b, preferred_element_type=F32)


def count_own(slot_ref):
    total = jnp.int32(0)
    for s in range(slot_ref.shape[0]):
        total = total + (slot_ref[s] >= 0).astype(jnp.int32)
    return total


def count_sent(head):
    return jnp.max(head.astype(F32)).astype(jnp.int32)


def kind_of(brick):
    return jnp.maximum(brick, 0) & 3


def pack_bricks(slot_ref, field_ref, strips_ref, msg_ref):
    slots = field_ref.shape[0]
    for s in range(slots):
        table = strips_ref[kind_of(slot_ref[s])]
        row = s * 2 * CH
        msg_ref[row : row + CH, :] = dot(field_ref[s], table).astype(BF)
        msg_ref[row + CH : row + 2 * CH, :] = join_halves(
            field_ref[s, :, 0:TILE], field_ref[s, :, 3 * TILE : 4 * TILE]
        )
    row = slots * 2 * CH
    count = count_own(slot_ref).astype(F32)
    msg_ref[row : row + HEAD, :] = jnp.full((HEAD, TILE), count, F32).astype(BF)


def bring(pairs, sems):
    copies = [pltpu.make_async_copy(a, b, sems.at[i]) for i, (a, b) in enumerate(pairs)]
    for copy in copies:
        copy.start()
    return copies


def pack_kernel(slot_hbm, field_hbm, strips_hbm, msg_ref, field_ref, strips_ref, slot_ref, sems):
    pairs = ((slot_hbm, slot_ref), (field_hbm, field_ref), (strips_hbm, strips_ref))
    for copy in bring(pairs, sems):
        copy.wait()
    pack_bricks(slot_ref, field_ref, strips_ref, msg_ref)


def route_body(slots, own_ref, mate_ref, near_ref, far_ref, box):
    odd = (lax.axis_index("bricks") & 1) == 1
    head = slots * 2 * CH
    mine = count_sent(own_ref[head : head + HEAD, :])
    other = count_sent(mate_ref[head : head + HEAD, :])
    for s in range(2 * slots):
        box[s] = own_ref[s * CH : (s + 1) * CH, :]
        box[2 * slots + s] = mate_ref[s * CH : (s + 1) * CH, :]
    for j in range(NEAR):
        up = jnp.where(j < mine, mine - 1 - j, slots + other - 1 - (j - mine))
        down = jnp.where(j < mine, j, slots + j - mine)
        at = jnp.clip(jnp.where(odd, up, down), 0, 2 * slots - 1)
        near_ref[j * CH : (j + 1) * CH, :] = box[2 * at + 1]
        if j < EDGE:
            near_ref[(NEAR + j) * CH : (NEAR + j + 1) * CH, :] = box[2 * at]
            far_ref[j * CH : (j + 1) * CH, :] = box[2 * at + 1]
    row = (NEAR + EDGE) * CH
    both = (mine + other).astype(F32)
    near_ref[row : row + HEAD, :] = jnp.full((HEAD, TILE), both, F32).astype(BF)


def route_kernel(slots, own_ref, mate_ref, near_ref, far_ref, box):
    route_body(slots, own_ref, mate_ref, near_ref, far_ref, box)


def route_sum_kernel(slots, own_ref, mate_ref, near_ref, far_ref, sum_ref, box):
    route_body(slots, own_ref, mate_ref, near_ref, far_ref, box)
    high = slots * 2 * CH + HEAD
    low = high + SUM_ROWS
    parts = []
    for ref in (own_ref, mate_ref):
        parts.append(
            ref[high : high + SUM_ROWS, :].astype(F32) + ref[low : low + SUM_ROWS, :].astype(F32)
        )
    sum_ref[...] = parts[0] + parts[1]


def weight_kernel(count, *refs):
    taps_hbm, sources = refs[0], refs[1 : count + 1]
    forward_ref, backward_ref = refs[count + 1 : count + 3]
    places = refs[count + 3 : 2 * count + 3]
    taps_ref, work, sems = refs[2 * count + 3 :]
    copies = bring(((taps_hbm, taps_ref),) + tuple(zip(sources, places)), sems)
    copies[0].wait()
    values = taps_ref[...].astype(F32)
    lanes = lax.broadcasted_iota(jnp.int32, (GC, CH), 1) // GC

    def block(tap):
        tile = values[tap * GC : (tap + 1) * GC, :]
        return jnp.concatenate([jnp.where(lanes == g, tile, 0.0) for g in range(CH // GC)], axis=0)

    work[...] = jnp.zeros_like(work)
    for bc in range(9):
        rows = slice(bc * CH, (bc + 1) * CH)
        work[rows, 0:TILE] = jnp.concatenate([block(bc), block(9 + bc)], axis=1)
        work[rows, TILE : TILE + CH] = block(18 + bc)
    turned = work[...].T
    forward_ref[...] = turned[0 : 3 * CH, 0 : 9 * CH].astype(BF)
    for a in range(3):
        rows = slice(a * CH, (a + 1) * CH)
        base = (2 - a) * 9 + 8
        for bc in range(0, 8, 2):
            pair = jnp.concatenate([block(base - bc), block(base - bc - 1)], axis=1)
            backward_ref[rows, bc * CH : (bc + 2) * CH] = pair.astype(BF)
        backward_ref[rows, 8 * CH : 9 * CH] = block(base - 8).astype(BF)
    for copy in copies[1:]:
        copy.wait()


def make_finder(
    slot_hbm, link_hbm, own_ref, mate_ref, first_ref, second_ref, first_far_ref, second_far_ref,
    planes, strips, slot_ref, link_ref, sems,
):
    copies = bring(((slot_hbm, slot_ref), (link_hbm, link_ref)), sems)
    slots = slot_ref.shape[0]
    odd = (lax.axis_index("bricks") & 1) == 1
    head = slots * 2 * CH
    mine = count_sent(own_ref[head : head + HEAD, :])
    other = count_sent(mate_ref[head : head + HEAD, :])
    row = (NEAR + EDGE) * CH
    counts = [count_sent(ref[row : row + HEAD, :]) for ref in (first_ref, second_ref)]
    for k, ref in enumerate((own_ref, mate_ref)):
        for s in range(slots):
            strips[k * slots + s] = ref[s * 2 * CH : s * 2 * CH + CH, :]
            planes[k * slots + s] = ref[s * 2 * CH + CH : (s + 1) * 2 * CH, :]
    for side, (near, far) in enumerate(((first_ref, first_far_ref), (second_ref, second_far_ref))):
        for j in range(NEAR):
            planes[2 * slots + side * NEAR + j] = near[j * CH : (j + 1) * CH, :]
        for j in range(EDGE):
            strips[2 * slots + side * EDGE + j] = near[(NEAR + j) * CH : (NEAR + j + 1) * CH, :]
            planes[2 * slots + 2 * NEAR + side * EDGE + j] = far[j * CH : (j + 1) * CH, :]
    nothing = 2 * slots + 2 * NEAR + 2 * EDGE
    planes[nothing] = jnp.zeros((CH, TILE), BF)
    for copy in copies:
        copy.wait()
    base = slot_ref[0]
    low_side = odd.astype(jnp.int32)
    high_side = 1 - low_side
    low_count = jnp.where(odd, counts[1], counts[0])
    high_count = jnp.where(odd, counts[0], counts[1])
    mate_first = jnp.where(odd, base - other, base + mine)
    chip_low = jnp.where(odd, base - other, base)
    chip_high = jnp.where(odd, base + mine, base + mine + other)

    def on_chip(brick):
        own = (brick >= base) & (brick < base + mine)
        return jnp.where(own, brick - base, slots + brick - mate_first)

    def find_strip(brick):
        low = 2 * slots + low_side * EDGE + (chip_low - 1 - brick)
        high = 2 * slots + high_side * EDGE + (brick - chip_high)
        at = jnp.where(brick < chip_low, low, jnp.where(brick >= chip_high, high, on_chip(brick)))
        return jnp.clip(at, 0, 2 * slots + 2 * EDGE - 1)

    def outside(distance, count, side):
        near = 2 * slots + side * NEAR + distance
        far = 2 * slots + 2 * NEAR + side * EDGE + distance - count
        return jnp.where(distance < count, near, far)

    def find_plane(brick, exists):
        low = outside(chip_low - 1 - brick, low_count, low_side)
        high = outside(brick - chip_high, high_count, high_side)
        at = jnp.where(brick < chip_low, low, jnp.where(brick >= chip_high, high, on_chip(brick)))
        return jnp.clip(jnp.where(exists, at, nothing), 0, nothing)

    return base, mine, find_strip, find_plane


def convolve_brick(
    s, base, find_strip, find_plane, link_ref, field_ref, planes, strips,
    spread_ref, ends_ref, shifts_ref, weight_ref, mixed, taps, sums,
):
    brick = base + s
    kind = brick & 3
    step_y = 2 - 2 * (kind & 2)
    step_z = 1 - 2 * (kind & 1)
    sides = (brick + step_y, brick + step_z, brick + step_y + step_z)
    has_low = link_ref[s, 0] >= 0
    has_high = link_ref[s, 1] >= 0

    def outer(near):
        high = planes[find_plane(near + 4, has_high)]
        low = planes[find_plane(near - 4, has_low)]
        return join_halves(high, low)

    beside = jnp.concatenate([strips[find_strip(m)] for m in sides], axis=1)
    halo = dot(beside, spread_ref[...]).astype(BF)
    outer_beside = jnp.concatenate([outer(m) for m in sides], axis=1)
    for i in range(4):
        rows = slice(i * CH, (i + 1) * CH)
        mixed[rows, 0:TILE] = field_ref[s, :, i * TILE : (i + 1) * TILE]
        mixed[rows, TILE:] = halo[:, i * TILE : (i + 1) * TILE]
    mixed[4 * CH :, 0:TILE] = outer(brick)
    mixed[4 * CH :, TILE:] = dot(outer_beside, ends_ref[kind]).astype(BF)
    for bc in range(0, 9, 2):
        wide = min(2, 9 - bc)
        part = dot(mixed[...], shifts_ref[kind, :, bc * TILE : (bc + wide) * TILE]).astype(BF)
        for e in range(wide):
            for i in range(5):
                taps[(bc + e) * CH : (bc + e + 1) * CH, i * TILE : (i + 1) * TILE] = part[
                    i * CH : (i + 1) * CH, e * TILE : (e + 1) * TILE
                ]
    sums[...] = dot(weight_ref[...], taps[0 : 9 * CH, :])
    turned = []
    for a in (0, 2):
        rows = slice(a * CH, (a + 1) * CH)
        turned.append(
            [pltpu.roll(sums[rows, i * TILE : (i + 1) * TILE], 64, 1) for i in range(5)]
        )
    left = left_half((CH, TILE))
    tiles = []
    for i in range(4):
        lower = jnp.where(left, turned[0][(i - 1) % 5], turned[0][i])
        upper = jnp.where(left, turned[1][i], turned[1][i + 1])
        tiles.append(sums[CH : 2 * CH, i * TILE : (i + 1) * TILE] + lower + upper)
    return tiles


def forward_kernel(
    slot_hbm, link_hbm, field_ref, own_ref, mate_ref, first_ref, second_ref, first_far_ref,
    second_far_ref, weight_ref, bias_ref, cortex_ref, upstream_ref, strips_ref, spread_ref,
    ends_ref, shifts_ref, out_ref, dpre_ref, msg_ref,
    planes, strips, mixed, taps, sums, slot_ref, link_ref, sems, spots, grads, keeps,
):
    slots = field_ref.shape[0]
    base, mine, find_strip, find_plane = make_finder(
        slot_hbm, link_hbm, own_ref, mate_ref, first_ref, second_ref, first_far_ref, second_far_ref,
        planes, strips, slot_ref, link_ref, sems,
    )
    for s in range(slots):
        keeps[s] = jnp.broadcast_to(cortex_ref[s : s + 1, :].astype(F32), (8, 512))
    taps[9 * CH :, :] = jnp.ones((HEAD, 5 * TILE), BF)
    grads[...] = jnp.zeros_like(grads)
    for s in range(slots):

        @pl.when(s >= mine)
        def _():
            out_ref[s] = jnp.zeros((CH, 512), BF)
            dpre_ref[s] = jnp.zeros((CH, 512), BF)

    square = (CH, CH)
    diagonal = lax.broadcasted_iota(jnp.int32, square, 0) == lax.broadcasted_iota(jnp.int32, square, 1)
    bias = jnp.sum(jnp.where(diagonal, bias_ref[...], 0.0), axis=1, keepdims=True)
    left = left_half((CH, TILE))
    zero = jnp.zeros((CH, TILE), F32)

    def one_brick(s, carry):
        tiles = convolve_brick(
            s, base, find_strip, find_plane, link_ref, field_ref, planes, strips,
            spread_ref, ends_ref, shifts_ref, weight_ref, mixed, taps, sums,
        )
        turned = []
        for i in range(4):
            lanes = slice(i * TILE, (i + 1) * TILE)
            pre = tiles[i] + bias
            keep = keeps[s, 0:1, lanes]
            sigma = 1.0 / (1.0 + jnp.exp(-pre))
            out_ref[s, :, lanes] = (pre * sigma * keep).astype(BF)
            slope = sigma * (1.0 + pre * (1.0 - sigma))
            dpre = (upstream_ref[s, :, lanes].astype(F32) * keep * slope).astype(BF)
            dpre_ref[s, :, lanes] = dpre
            spots[CH : 2 * CH, lanes] = dpre
            turned.append(pltpu.roll(dpre.astype(F32), 64, 1))
        spots[CH : 2 * CH, 4 * TILE :] = jnp.zeros((CH, TILE), BF)
        turned.append(zero)
        for i in range(4):
            lanes = slice(i * TILE, (i + 1) * TILE)
            spots[0:CH, lanes] = jnp.where(left, turned[i], turned[i + 1]).astype(BF)
            before = turned[i - 1] if i else zero
            spots[2 * CH :, lanes] = jnp.where(left, before, turned[i]).astype(BF)
        spots[0:CH, 4 * TILE :] = jnp.where(left, 0.0, turned[0]).astype(BF)
        spots[2 * CH :, 4 * TILE :] = jnp.where(left, turned[3], 0.0).astype(BF)
        grads[...] += lax.dot_general(
            taps[...], spots[...], (((1,), (1,)), ((), ())), preferred_element_type=F32
        )
        return carry

    lax.fori_loop(0, mine, one_brick, 0)

    pack_bricks(slot_ref, dpre_ref, strips_ref, msg_ref)
    high = slots * 2 * CH + HEAD
    low = high + SUM_ROWS
    group = lax.broadcasted_iota(jnp.int32, (GC, TILE), 1) % CH // GC
    for half, lanes in enumerate((slice(0, TILE), slice(TILE, TILE + CH))):
        group_here = group[:, : lanes.stop - lanes.start]
        rows = []
        for bc in range(9):
            total = jnp.zeros(group_here.shape, F32)
            for g in range(CH // GC):
                at = bc * CH + g * GC
                total = total + jnp.where(group_here == g, grads[at : at + GC, lanes], 0.0)
            rows.append(total)
        rows.append(grads[9 * CH : 9 * CH + GC, lanes])
        full = jnp.concatenate(rows, axis=0)
        if full.shape[1] < TILE:
            full = jnp.concatenate([full, jnp.zeros((10 * GC, TILE - full.shape[1]), F32)], axis=1)
        rounded = full.astype(BF)
        at = half * 10 * GC
        msg_ref[high + at : high + at + 10 * GC, :] = rounded
        msg_ref[low + at : low + at + 10 * GC, :] = (full - rounded.astype(F32)).astype(BF)


def backward_kernel(part, *refs):
    if part:
        refs, last_ref = refs[:13] + refs[14:], refs[13]
        field_ref, own_ref, out_ref = refs[2], refs[3], refs[13]
        slots = field_ref.shape[0]
        head = slots * 2 * CH
        half = count_sent(own_ref[head : head + HEAD, :]) // 2
        for s in range(slots):

            @pl.when(s < half)
            def _():
                out_ref[s] = last_ref[s]

    backward_body(part, *refs)


def backward_body(
    part, slot_hbm, link_hbm, field_ref, own_ref, mate_ref, first_ref, second_ref, first_far_ref,
    second_far_ref, weight_ref, spread_ref, ends_ref, shifts_ref, out_ref,
    planes, strips, mixed, taps, sums, slot_ref, link_ref, sems,
):
    slots = field_ref.shape[0]
    base, mine, find_strip, find_plane = make_finder(
        slot_hbm, link_hbm, own_ref, mate_ref, first_ref, second_ref, first_far_ref, second_far_ref,
        planes, strips, slot_ref, link_ref, sems,
    )
    if part == 1:
        for s in range(slots):

            @pl.when(s >= mine)
            def _():
                out_ref[s] = jnp.zeros((CH, 512), BF)

    def one_brick(s, carry):
        tiles = convolve_brick(
            s, base, find_strip, find_plane, link_ref, field_ref, planes, strips,
            spread_ref, ends_ref, shifts_ref, weight_ref, mixed, taps, sums,
        )
        for i in range(4):
            out_ref[s, :, i * TILE : (i + 1) * TILE] = tiles[i].astype(BF)
        return carry

    half = mine // 2
    lax.fori_loop(half * part, mine if part else half, one_brick, 0)


def finish_kernel(a_ref, b_ref, kernel_ref, bias_ref):
    first = a_ref[0 : 10 * GC, :] + b_ref[0 : 10 * GC, :]
    second = a_ref[10 * GC :, :] + b_ref[10 * GC :, :]
    turned = pltpu.roll(first, 64, 1)
    for a, part in enumerate((first, turned, second)):
        kernel_ref[a * 9 * GC : (a + 1) * 9 * GC, :] = part[0 : 9 * GC, 0:CH]
    bias_ref[...] = turned[9 * GC : 9 * GC + 1, 0:CH]


VMEM = pl.BlockSpec(memory_space=pltpu.VMEM)
HBM = pl.BlockSpec(memory_space=pltpu.HBM)


def call(kernel, ins, outs, scratch=(), flops=0, size=400000):
    return pl.pallas_call(
        kernel,
        in_specs=ins,
        out_specs=tuple(VMEM for _ in outs),
        out_shape=tuple(outs),
        scratch_shapes=list(scratch),
        compiler_params=pltpu.CompilerParams(vmem_limit_bytes=24 * 2**20),
        cost_estimate=pl.CostEstimate(flops=flops, bytes_accessed=size, transcendentals=0),
    )


def sent(block, route):
    return lax.ppermute(block, "bricks", route)


def shards(voxels, kernel, bias, cortex, slot_to_brick, neighbors, cotangent):
    slots = voxels.shape[0]
    devices = lax.axis_size("bricks")
    strips, spread, ends, shifts = (jnp.asarray(t, BF) for t in tables())
    shape = jax.ShapeDtypeStruct
    pack_rows = slots * 2 * CH + HEAD
    near_shape = shape(((NEAR + EDGE) * CH + HEAD, TILE), BF)
    far_shape = shape((EDGE * CH, TILE), BF)

    def routed(block, chips):
        pairs = []
        for d in range(devices):
            to = d + 2 * chips - 1 if d % 2 else d - 2 * chips + 1
            if 0 <= to < devices:
                pairs.append((d, to))
        return sent(block, pairs)

    def swapped(block, mask):
        return sent(block, [(d, d ^ mask) for d in range(devices)])

    box = [pltpu.VMEM((4 * slots, CH, TILE), BF)]
    work = [
        pltpu.VMEM((2 * slots + 2 * NEAR + 2 * EDGE + 1, CH, TILE), BF),
        pltpu.VMEM((2 * slots + 2 * EDGE, CH, TILE), BF),
        pltpu.VMEM((5 * CH, 2 * TILE), BF),
        pltpu.VMEM((9 * CH + HEAD, 5 * TILE), BF),
        pltpu.VMEM((3 * CH, 5 * TILE), F32),
        pltpu.SMEM(slot_to_brick.shape, jnp.int32),
        pltpu.SMEM(neighbors.shape, jnp.int32),
        pltpu.SemaphoreType.DMA((2,)),
    ]
    field = shape(voxels.shape, BF)

    own, voxels, strips = call(
        pack_kernel,
        [HBM] * 3,
        [shape((pack_rows, TILE), BF), field, shape(strips.shape, BF)],
        [pltpu.SMEM(slot_to_brick.shape, jnp.int32), pltpu.SemaphoreType.DMA((3,))],
    )(slot_to_brick, voxels, strips)
    mate = swapped(own, 1)
    weight_shape = shape((3 * CH, 9 * CH), BF)
    taps = jnp.transpose(kernel, (2, 3, 4, 1, 0)).reshape(27 * GC, CH)
    later = (cotangent, cortex, bias.reshape(1, CH), spread, ends, shifts)
    staged = call(
        functools.partial(weight_kernel, len(later)),
        [HBM] * (1 + len(later)),
        [weight_shape] * 2 + [shape(a.shape, a.dtype) for a in later],
        [
            pltpu.VMEM(taps.shape, BF),
            pltpu.VMEM((640, 256), F32),
            pltpu.SemaphoreType.DMA((1 + len(later),)),
        ],
        size=5 * 10**6,
    )(taps, *later)
    near, far = call(
        functools.partial(route_kernel, slots), [VMEM, VMEM], [near_shape, far_shape], box
    )(own, mate)
    near, far = routed(near, 1), routed(far, 2)
    near, far, staged = lax.optimization_barrier((near, far, staged))
    forward, backward, cotangent, cortex, bias, spread, ends, shifts = staged
    received = (near, swapped(near, 1), far, swapped(far, 1))
    activated, dpre, own = call(
        forward_kernel,
        [HBM, HBM] + [VMEM] * 15,
        [field, field, shape((pack_rows + 2 * SUM_ROWS, TILE), BF)],
        work
        + [
            pltpu.VMEM((3 * CH, 5 * TILE), BF),
            pltpu.VMEM((9 * CH + HEAD, 3 * CH), F32),
            pltpu.VMEM((slots, 8, 512), F32),
        ],
        flops=4 * 10**9,
    )(
        slot_to_brick, neighbors, voxels, own, mate, *received, forward, bias,
        cortex, cotangent, strips, spread, ends, shifts,
    )
    mate = swapped(own, 1)
    near, far, total = call(
        functools.partial(route_sum_kernel, slots),
        [VMEM, VMEM],
        [near_shape, far_shape, shape((SUM_ROWS, TILE), F32)],
        box,
    )(own, mate)
    state = dict(near=near, far=far)

    def send_halos():
        state.update(near=routed(state["near"], 1), far=routed(state["far"], 2))

    def tell_mate():
        near, far = state["near"], state["far"]
        state.update(second=swapped(near, 1), second_far=swapped(far, 1))

    def half_backward(part):
        last = [state["grad"]] if part else []
        (state["grad"],) = call(
            functools.partial(backward_kernel, part),
            [HBM, HBM] + [VMEM] * (11 + part),
            [field],
            work,
            flops=10**9,
        )(
            slot_to_brick, neighbors, dpre, own, mate, state["near"], state["second"],
            state["far"], state["second_far"], backward, spread, ends, shifts, *last,
        )

    beside = [send_halos, tell_mate, lambda: half_backward(0), lambda: half_backward(1)]
    masks = [2**p for p in range(1, devices.bit_length() - 1)]
    for mask in masks:
        other = swapped(total, mask)
        if beside:
            beside.pop(0)()
        if mask != masks[-1]:
            total, other, state = lax.optimization_barrier((total, other, state))
            total = total + other
    for task in beside:
        task()
    input_grad = state["grad"]
    kernel_sum, bias_sum = call(
        finish_kernel, [VMEM, VMEM], [shape((27 * GC, CH), F32), shape((1, CH), F32)]
    )(total, other)
    kernel_grad = jnp.transpose(kernel_sum.reshape(3, 3, 3, GC, CH), (4, 3, 0, 1, 2))
    return (activated, input_grad, kernel_grad, bias_sum.reshape(CH))


def solution(mesh):
    devices = mesh.shape["bricks"]
    assert devices & (devices - 1) == 0
    return jax.shard_map(
        shards,
        mesh=mesh,
        in_specs=(
            P("bricks", None, None),
            P(),
            P(),
            P("bricks", None),
            P("bricks"),
            P("bricks", None),
            P("bricks", None, None),
        ),
        out_specs=(P("bricks", None, None), P("bricks", None, None), P(), P()),
        check_vma=False,
    )
```

```python
import functools

import jax
import jax.numpy as jnp
import numpy as np
from jax import lax
from jax.experimental import pallas as pl
from jax.experimental.pallas import tpu as pltpu
from jax.sharding import PartitionSpec as P

CH = 64
GC = 8
TILE = 128
NEAR = 7
EDGE = 3
BUSY = 10**10
HEAD = 16
SUM_ROWS = 160
BF = jnp.bfloat16
F32 = jnp.float32


@functools.cache
def tables():
    strips = np.zeros((4, 512, TILE), np.float32)
    spread = np.zeros((384, 4 * TILE), np.float32)
    ends = np.zeros((4, 384, TILE), np.float32)
    shifts = np.zeros((4, 256, 9 * TILE), np.float32)
    for half in range(2):
        for xx in range(4):
            for w in range(8):
                i, xp = 2 * half + xx // 2, xx % 2
                spread[half * 64 + xx * 8 + w, i * TILE + xp * 8 + w] = 1
                spread[128 + half * 64 + 32 + xx * 8 + w, i * TILE + 32 + xp * 8 + w] = 1
                spread[256 + half * 64 + xx * 8 + w, i * TILE + 64 + xp * 8 + w] = 1
    for t in range(4):
        q, r = t // 2, t % 2
        own_y, own_z = (0 if q else 7), (0 if r else 7)
        far_y, far_z = 7 - own_y, 7 - own_z
        for half in range(2):
            for xx in range(4):
                for w in range(8):
                    plane = (4 * half + xx) * 64
                    strips[t, plane + own_y * 8 + w, half * 64 + xx * 8 + w] = 1
                    strips[t, plane + w * 8 + own_z, half * 64 + 32 + xx * 8 + w] = 1
        for xp in range(2):
            for w in range(8):
                ends[t, xp * 64 + far_y * 8 + w, xp * 8 + w] = 1
                ends[t, 128 + xp * 64 + w * 8 + far_z, 32 + xp * 8 + w] = 1
                ends[t, 256 + xp * 64 + far_y * 8 + w, 64 + xp * 8 + w] = 1
        out_y, out_z = (-1 if q else 8), (-1 if r else 8)
        for b in range(3):
            for c in range(3):
                for xp in range(2):
                    for y in range(8):
                        for z in range(8):
                            yy, zz = y + b - 1, z + c - 1
                            in_y, in_z = 0 <= yy < 8, 0 <= zz < 8
                            if in_y and in_z:
                                k = xp * 64 + yy * 8 + zz
                            elif in_z and yy == out_y:
                                k = 128 + xp * 8 + zz
                            elif in_y and zz == out_z:
                                k = 160 + xp * 8 + yy
                            elif yy == out_y and zz == out_z:
                                k = 192 + xp * 8 + far_z
                            else:
                                continue
                            shifts[t, k, (b * 3 + c) * TILE + xp * 64 + y * 8 + z] = 1
    return strips, spread, ends, shifts


def left_half(shape):
    return lax.broadcasted_iota(jnp.int32, shape, len(shape) - 1) % TILE < 64


def join_halves(left, right):
    mixed = jnp.where(left_half(left.shape), left.astype(F32), right.astype(F32))
    return mixed.astype(left.dtype)


def dot(a, b):
    return jnp.dot(a, b, preferred_element_type=F32)


def count_own(slot_ref):
    total = jnp.int32(0)
    for s in range(slot_ref.shape[0]):
        total = total + (slot_ref[s] >= 0).astype(jnp.int32)
    return total


def count_sent(head):
    return jnp.max(head.astype(F32)).astype(jnp.int32)


def kind_of(brick):
    return jnp.maximum(brick, 0) & 3


def pack_bricks(slot_ref, field_ref, strips_ref, msg_ref):
    slots = field_ref.shape[0]
    for s in range(slots):
        table = strips_ref[kind_of(slot_ref[s])]
        row = s * 2 * CH
        msg_ref[row : row + CH, :] = dot(field_ref[s], table).astype(BF)
        msg_ref[row + CH : row + 2 * CH, :] = join_halves(
            field_ref[s, :, 0:TILE], field_ref[s, :, 3 * TILE : 4 * TILE]
        )
    row = slots * 2 * CH
    count = count_own(slot_ref).astype(F32)
    msg_ref[row : row + HEAD, :] = jnp.full((HEAD, TILE), count, F32).astype(BF)


def bring(pairs, sems):
    copies = [pltpu.make_async_copy(a, b, sems.at[i]) for i, (a, b) in enumerate(pairs)]
    for copy in copies:
        copy.start()
    return copies


def pack_kernel(slot_hbm, field_hbm, strips_hbm, msg_ref, field_ref, strips_ref, slot_ref, sems):
    pairs = ((slot_hbm, slot_ref), (field_hbm, field_ref), (strips_hbm, strips_ref))
    for copy in bring(pairs, sems):
        copy.wait()
    pack_bricks(slot_ref, field_ref, strips_ref, msg_ref)


def route_body(slots, own_ref, mate_ref, near_ref, far_ref, box):
    odd = (lax.axis_index("bricks") & 1) == 1
    head = slots * 2 * CH
    mine = count_sent(own_ref[head : head + HEAD, :])
    other = count_sent(mate_ref[head : head + HEAD, :])
    for s in range(2 * slots):
        box[s] = own_ref[s * CH : (s + 1) * CH, :]
        box[2 * slots + s] = mate_ref[s * CH : (s + 1) * CH, :]
    for j in range(NEAR):
        up = jnp.where(j < mine, mine - 1 - j, slots + other - 1 - (j - mine))
        down = jnp.where(j < mine, j, slots + j - mine)
        at = jnp.clip(jnp.where(odd, up, down), 0, 2 * slots - 1)
        near_ref[j * CH : (j + 1) * CH, :] = box[2 * at + 1]
        if j < EDGE:
            near_ref[(NEAR + j) * CH : (NEAR + j + 1) * CH, :] = box[2 * at]
            far_ref[j * CH : (j + 1) * CH, :] = box[2 * at + 1]
    row = (NEAR + EDGE) * CH
    both = (mine + other).astype(F32)
    near_ref[row : row + HEAD, :] = jnp.full((HEAD, TILE), both, F32).astype(BF)


def route_kernel(slots, own_ref, mate_ref, near_ref, far_ref, box):
    route_body(slots, own_ref, mate_ref, near_ref, far_ref, box)


def route_sum_kernel(slots, own_ref, mate_ref, near_ref, far_ref, sum_ref, box):
    route_body(slots, own_ref, mate_ref, near_ref, far_ref, box)
    high = slots * 2 * CH + HEAD
    low = high + SUM_ROWS
    parts = []
    for ref in (own_ref, mate_ref):
        parts.append(
            ref[high : high + SUM_ROWS, :].astype(F32) + ref[low : low + SUM_ROWS, :].astype(F32)
        )
    sum_ref[...] = parts[0] + parts[1]


def weight_kernel(taps_ref, forward_ref, backward_ref, work):
    values = taps_ref[...].astype(F32)
    lanes = lax.broadcasted_iota(jnp.int32, (GC, CH), 1) // GC

    def block(tap):
        tile = values[tap * GC : (tap + 1) * GC, :]
        return jnp.concatenate([jnp.where(lanes == g, tile, 0.0) for g in range(CH // GC)], axis=0)

    work[...] = jnp.zeros_like(work)
    for bc in range(9):
        rows = slice(bc * CH, (bc + 1) * CH)
        work[rows, 0:TILE] = jnp.concatenate([block(bc), block(9 + bc)], axis=1)
        work[rows, TILE : TILE + CH] = block(18 + bc)
    turned = work[...].T
    forward_ref[...] = turned[0 : 3 * CH, 0 : 9 * CH].astype(BF)
    for a in range(3):
        rows = slice(a * CH, (a + 1) * CH)
        base = (2 - a) * 9 + 8
        for bc in range(0, 8, 2):
            pair = jnp.concatenate([block(base - bc), block(base - bc - 1)], axis=1)
            backward_ref[rows, bc * CH : (bc + 2) * CH] = pair.astype(BF)
        backward_ref[rows, 8 * CH : 9 * CH] = block(base - 8).astype(BF)


def make_finder(
    slot_hbm, link_hbm, own_ref, mate_ref, first_ref, second_ref, first_far_ref, second_far_ref,
    planes, strips, slot_ref, link_ref, sems,
):
    copies = bring(((slot_hbm, slot_ref), (link_hbm, link_ref)), sems)
    slots = slot_ref.shape[0]
    odd = (lax.axis_index("bricks") & 1) == 1
    head = slots * 2 * CH
    mine = count_sent(own_ref[head : head + HEAD, :])
    other = count_sent(mate_ref[head : head + HEAD, :])
    row = (NEAR + EDGE) * CH
    counts = [count_sent(ref[row : row + HEAD, :]) for ref in (first_ref, second_ref)]
    for k, ref in enumerate((own_ref, mate_ref)):
        for s in range(slots):
            strips[k * slots + s] = ref[s * 2 * CH : s * 2 * CH + CH, :]
            planes[k * slots + s] = ref[s * 2 * CH + CH : (s + 1) * 2 * CH, :]
    for side, (near, far) in enumerate(((first_ref, first_far_ref), (second_ref, second_far_ref))):
        for j in range(NEAR):
            planes[2 * slots + side * NEAR + j] = near[j * CH : (j + 1) * CH, :]
        for j in range(EDGE):
            strips[2 * slots + side * EDGE + j] = near[(NEAR + j) * CH : (NEAR + j + 1) * CH, :]
            planes[2 * slots + 2 * NEAR + side * EDGE + j] = far[j * CH : (j + 1) * CH, :]
    nothing = 2 * slots + 2 * NEAR + 2 * EDGE
    planes[nothing] = jnp.zeros((CH, TILE), BF)
    for copy in copies:
        copy.wait()
    base = slot_ref[0]
    low_side = odd.astype(jnp.int32)
    high_side = 1 - low_side
    low_count = jnp.where(odd, counts[1], counts[0])
    high_count = jnp.where(odd, counts[0], counts[1])
    mate_first = jnp.where(odd, base - other, base + mine)
    chip_low = jnp.where(odd, base - other, base)
    chip_high = jnp.where(odd, base + mine, base + mine + other)

    def on_chip(brick):
        own = (brick >= base) & (brick < base + mine)
        return jnp.where(own, brick - base, slots + brick - mate_first)

    def find_strip(brick):
        low = 2 * slots + low_side * EDGE + (chip_low - 1 - brick)
        high = 2 * slots + high_side * EDGE + (brick - chip_high)
        at = jnp.where(brick < chip_low, low, jnp.where(brick >= chip_high, high, on_chip(brick)))
        return jnp.clip(at, 0, 2 * slots + 2 * EDGE - 1)

    def outside(distance, count, side):
        near = 2 * slots + side * NEAR + distance
        far = 2 * slots + 2 * NEAR + side * EDGE + distance - count
        return jnp.where(distance < count, near, far)

    def find_plane(brick, exists):
        low = outside(chip_low - 1 - brick, low_count, low_side)
        high = outside(brick - chip_high, high_count, high_side)
        at = jnp.where(brick < chip_low, low, jnp.where(brick >= chip_high, high, on_chip(brick)))
        return jnp.clip(jnp.where(exists, at, nothing), 0, nothing)

    return base, mine, find_strip, find_plane


def convolve_brick(
    s, base, find_strip, find_plane, link_ref, field_ref, planes, strips,
    spread_ref, ends_ref, shifts_ref, weight_ref, mixed, taps, sums,
):
    brick = base + s
    kind = brick & 3
    step_y = 2 - 2 * (kind & 2)
    step_z = 1 - 2 * (kind & 1)
    sides = (brick + step_y, brick + step_z, brick + step_y + step_z)
    has_low = link_ref[s, 0] >= 0
    has_high = link_ref[s, 1] >= 0

    def outer(near):
        high = planes[find_plane(near + 4, has_high)]
        low = planes[find_plane(near - 4, has_low)]
        return join_halves(high, low)

    beside = jnp.concatenate([strips[find_strip(m)] for m in sides], axis=1)
    halo = dot(beside, spread_ref[...]).astype(BF)
    outer_beside = jnp.concatenate([outer(m) for m in sides], axis=1)
    for i in range(4):
        rows = slice(i * CH, (i + 1) * CH)
        mixed[rows, 0:TILE] = field_ref[s, :, i * TILE : (i + 1) * TILE]
        mixed[rows, TILE:] = halo[:, i * TILE : (i + 1) * TILE]
    mixed[4 * CH :, 0:TILE] = outer(brick)
    mixed[4 * CH :, TILE:] = dot(outer_beside, ends_ref[kind]).astype(BF)
    for bc in range(0, 9, 2):
        wide = min(2, 9 - bc)
        part = dot(mixed[...], shifts_ref[kind, :, bc * TILE : (bc + wide) * TILE]).astype(BF)
        for e in range(wide):
            for i in range(5):
                taps[(bc + e) * CH : (bc + e + 1) * CH, i * TILE : (i + 1) * TILE] = part[
                    i * CH : (i + 1) * CH, e * TILE : (e + 1) * TILE
                ]
    sums[...] = dot(weight_ref[...], taps[0 : 9 * CH, :])
    turned = []
    for a in (0, 2):
        rows = slice(a * CH, (a + 1) * CH)
        turned.append(
            [pltpu.roll(sums[rows, i * TILE : (i + 1) * TILE], 64, 1) for i in range(5)]
        )
    left = left_half((CH, TILE))
    tiles = []
    for i in range(4):
        lower = jnp.where(left, turned[0][(i - 1) % 5], turned[0][i])
        upper = jnp.where(left, turned[1][i], turned[1][i + 1])
        tiles.append(sums[CH : 2 * CH, i * TILE : (i + 1) * TILE] + lower + upper)
    return tiles


def forward_kernel(
    slot_hbm, link_hbm, field_ref, own_ref, mate_ref, first_ref, second_ref, first_far_ref,
    second_far_ref, weight_ref, bias_ref, cortex_ref, upstream_ref, strips_ref, spread_ref,
    ends_ref, shifts_ref, out_ref, dpre_ref, msg_ref,
    planes, strips, mixed, taps, sums, slot_ref, link_ref, sems, spots, grads, keeps,
):
    slots = field_ref.shape[0]
    base, mine, find_strip, find_plane = make_finder(
        slot_hbm, link_hbm, own_ref, mate_ref, first_ref, second_ref, first_far_ref, second_far_ref,
        planes, strips, slot_ref, link_ref, sems,
    )
    for s in range(slots):
        keeps[s] = jnp.broadcast_to(cortex_ref[s : s + 1, :].astype(F32), (8, 512))
    taps[9 * CH :, :] = jnp.ones((HEAD, 5 * TILE), BF)
    grads[...] = jnp.zeros_like(grads)
    for s in range(slots):

        @pl.when(s >= mine)
        def _():
            out_ref[s] = jnp.zeros((CH, 512), BF)
            dpre_ref[s] = jnp.zeros((CH, 512), BF)

    square = (CH, CH)
    diagonal = lax.broadcasted_iota(jnp.int32, square, 0) == lax.broadcasted_iota(jnp.int32, square, 1)
    bias = jnp.sum(jnp.where(diagonal, bias_ref[...], 0.0), axis=1, keepdims=True)
    left = left_half((CH, TILE))
    zero = jnp.zeros((CH, TILE), F32)

    def one_brick(s, carry):
        tiles = convolve_brick(
            s, base, find_strip, find_plane, link_ref, field_ref, planes, strips,
            spread_ref, ends_ref, shifts_ref, weight_ref, mixed, taps, sums,
        )
        turned = []
        for i in range(4):
            lanes = slice(i * TILE, (i + 1) * TILE)
            pre = tiles[i] + bias
            keep = keeps[s, 0:1, lanes]
            sigma = 1.0 / (1.0 + jnp.exp(-pre))
            out_ref[s, :, lanes] = (pre * sigma * keep).astype(BF)
            slope = sigma * (1.0 + pre * (1.0 - sigma))
            dpre = (upstream_ref[s, :, lanes].astype(F32) * keep * slope).astype(BF)
            dpre_ref[s, :, lanes] = dpre
            spots[CH : 2 * CH, lanes] = dpre
            turned.append(pltpu.roll(dpre.astype(F32), 64, 1))
        spots[CH : 2 * CH, 4 * TILE :] = jnp.zeros((CH, TILE), BF)
        turned.append(zero)
        for i in range(4):
            lanes = slice(i * TILE, (i + 1) * TILE)
            spots[0:CH, lanes] = jnp.where(left, turned[i], turned[i + 1]).astype(BF)
            before = turned[i - 1] if i else zero
            spots[2 * CH :, lanes] = jnp.where(left, before, turned[i]).astype(BF)
        spots[0:CH, 4 * TILE :] = jnp.where(left, 0.0, turned[0]).astype(BF)
        spots[2 * CH :, 4 * TILE :] = jnp.where(left, turned[3], 0.0).astype(BF)
        grads[...] += lax.dot_general(
            taps[...], spots[...], (((1,), (1,)), ((), ())), preferred_element_type=F32
        )
        return carry

    lax.fori_loop(0, mine, one_brick, 0)

    pack_bricks(slot_ref, dpre_ref, strips_ref, msg_ref)
    high = slots * 2 * CH + HEAD
    low = high + SUM_ROWS
    group = lax.broadcasted_iota(jnp.int32, (GC, TILE), 1) % CH // GC
    for half, lanes in enumerate((slice(0, TILE), slice(TILE, TILE + CH))):
        group_here = group[:, : lanes.stop - lanes.start]
        rows = []
        for bc in range(9):
            total = jnp.zeros(group_here.shape, F32)
            for g in range(CH // GC):
                at = bc * CH + g * GC
                total = total + jnp.where(group_here == g, grads[at : at + GC, lanes], 0.0)
            rows.append(total)
        rows.append(grads[9 * CH : 9 * CH + GC, lanes])
        full = jnp.concatenate(rows, axis=0)
        if full.shape[1] < TILE:
            full = jnp.concatenate([full, jnp.zeros((10 * GC, TILE - full.shape[1]), F32)], axis=1)
        rounded = full.astype(BF)
        at = half * 10 * GC
        msg_ref[high + at : high + at + 10 * GC, :] = rounded
        msg_ref[low + at : low + at + 10 * GC, :] = (full - rounded.astype(F32)).astype(BF)


def backward_kernel(part, *refs):
    if part:
        refs, last_ref = refs[:13] + refs[14:], refs[13]
        field_ref, own_ref, out_ref = refs[2], refs[3], refs[13]
        slots = field_ref.shape[0]
        head = slots * 2 * CH
        half = count_sent(own_ref[head : head + HEAD, :]) // 2
        for s in range(slots):

            @pl.when(s < half)
            def _():
                out_ref[s] = last_ref[s]

    backward_body(part, *refs)


def backward_body(
    part, slot_hbm, link_hbm, field_ref, own_ref, mate_ref, first_ref, second_ref, first_far_ref,
    second_far_ref, weight_ref, spread_ref, ends_ref, shifts_ref, out_ref,
    planes, strips, mixed, taps, sums, slot_ref, link_ref, sems,
):
    slots = field_ref.shape[0]
    base, mine, find_strip, find_plane = make_finder(
        slot_hbm, link_hbm, own_ref, mate_ref, first_ref, second_ref, first_far_ref, second_far_ref,
        planes, strips, slot_ref, link_ref, sems,
    )
    if part == 1:
        for s in range(slots):

            @pl.when(s >= mine)
            def _():
                out_ref[s] = jnp.zeros((CH, 512), BF)

    def one_brick(s, carry):
        tiles = convolve_brick(
            s, base, find_strip, find_plane, link_ref, field_ref, planes, strips,
            spread_ref, ends_ref, shifts_ref, weight_ref, mixed, taps, sums,
        )
        for i in range(4):
            out_ref[s, :, i * TILE : (i + 1) * TILE] = tiles[i].astype(BF)
        return carry

    half = mine // 2
    lax.fori_loop(half * part, mine if part else half, one_brick, 0)


def finish_kernel(a_ref, b_ref, kernel_ref, bias_ref):
    first = a_ref[0 : 10 * GC, :] + b_ref[0 : 10 * GC, :]
    second = a_ref[10 * GC :, :] + b_ref[10 * GC :, :]
    turned = pltpu.roll(first, 64, 1)
    for a, part in enumerate((first, turned, second)):
        kernel_ref[a * 9 * GC : (a + 1) * 9 * GC, :] = part[0 : 9 * GC, 0:CH]
    bias_ref[...] = turned[9 * GC : 9 * GC + 1, 0:CH]


VMEM = pl.BlockSpec(memory_space=pltpu.VMEM)
HBM = pl.BlockSpec(memory_space=pltpu.HBM)


def call(kernel, ins, outs, scratch=(), flops=0, size=400000, limit=24):
    return pl.pallas_call(
        kernel,
        in_specs=ins,
        out_specs=tuple(VMEM for _ in outs),
        out_shape=tuple(outs),
        scratch_shapes=list(scratch),
        compiler_params=pltpu.CompilerParams(vmem_limit_bytes=limit * 2**20),
        cost_estimate=pl.CostEstimate(flops=flops, bytes_accessed=size, transcendentals=0),
    )


def sent(block, route):
    return lax.ppermute(block, "bricks", route)


def shards(voxels, kernel, bias, cortex, slot_to_brick, neighbors, cotangent):
    slots = voxels.shape[0]
    devices = lax.axis_size("bricks")
    strips, spread, ends, shifts = (jnp.asarray(t, BF) for t in tables())
    shape = jax.ShapeDtypeStruct
    pack_rows = slots * 2 * CH + HEAD
    near_shape = shape(((NEAR + EDGE) * CH + HEAD, TILE), BF)
    far_shape = shape((EDGE * CH, TILE), BF)

    def routed(block, chips):
        pairs = []
        for d in range(devices):
            to = d + 2 * chips - 1 if d % 2 else d - 2 * chips + 1
            if 0 <= to < devices:
                pairs.append((d, to))
        return sent(block, pairs)

    def swapped(block, mask):
        return sent(block, [(d, d ^ mask) for d in range(devices)])

    box = [pltpu.VMEM((4 * slots, CH, TILE), BF)]
    work = [
        pltpu.VMEM((2 * slots + 2 * NEAR + 2 * EDGE + 1, CH, TILE), BF),
        pltpu.VMEM((2 * slots + 2 * EDGE, CH, TILE), BF),
        pltpu.VMEM((5 * CH, 2 * TILE), BF),
        pltpu.VMEM((9 * CH + HEAD, 5 * TILE), BF),
        pltpu.VMEM((3 * CH, 5 * TILE), F32),
        pltpu.SMEM(slot_to_brick.shape, jnp.int32),
        pltpu.SMEM(neighbors.shape, jnp.int32),
        pltpu.SemaphoreType.DMA((2,)),
    ]
    field = shape(voxels.shape, BF)

    (own,) = call(
        pack_kernel,
        [HBM] * 3,
        [shape((pack_rows, TILE), BF)],
        [pltpu.VMEM(voxels.shape, BF), pltpu.VMEM(strips.shape, BF), pltpu.SMEM(slot_to_brick.shape, jnp.int32), pltpu.SemaphoreType.DMA((3,))],
        limit=60,
    )(slot_to_brick, voxels, strips)
    mate = swapped(own, 1)
    weight_shape = shape((3 * CH, 9 * CH), BF)
    taps = jnp.transpose(kernel, (2, 3, 4, 1, 0)).reshape(27 * GC, CH)
    staged = call(
        weight_kernel, [VMEM], [weight_shape] * 2, [pltpu.VMEM((640, 256), F32)], flops=BUSY
    )(taps)
    near, far = call(
        functools.partial(route_kernel, slots), [VMEM, VMEM], [near_shape, far_shape], box,
        flops=BUSY,
    )(own, mate)
    near, far = routed(near, 1), routed(far, 2)
    near, far, staged = lax.optimization_barrier((near, far, staged))
    forward, backward = staged
    received = (near, swapped(near, 1), far, swapped(far, 1))
    activated, dpre, own = call(
        forward_kernel,
        [HBM, HBM] + [VMEM] * 15,
        [field, field, shape((pack_rows + 2 * SUM_ROWS, TILE), BF)],
        work
        + [
            pltpu.VMEM((3 * CH, 5 * TILE), BF),
            pltpu.VMEM((9 * CH + HEAD, 3 * CH), F32),
            pltpu.VMEM((slots, 8, 512), F32),
        ],
        flops=4 * 10**9,
    )(
        slot_to_brick, neighbors, voxels, own, mate, *received, forward, bias.reshape(1, CH),
        cortex, cotangent, strips, spread, ends, shifts,
    )
    mate = swapped(own, 1)
    near, far, total = call(
        functools.partial(route_sum_kernel, slots),
        [VMEM, VMEM],
        [near_shape, far_shape, shape((SUM_ROWS, TILE), F32)],
        box,
    )(own, mate)
    state = dict(near=near, far=far)

    def send_halos():
        state.update(near=routed(state["near"], 1), far=routed(state["far"], 2))

    def tell_mate():
        near, far = state["near"], state["far"]
        state.update(second=swapped(near, 1), second_far=swapped(far, 1))

    def half_backward(part):
        last = [state["grad"]] if part else []
        (state["grad"],) = call(
            functools.partial(backward_kernel, part),
            [HBM, HBM] + [VMEM] * (11 + part),
            [field],
            work,
            flops=10**9,
        )(
            slot_to_brick, neighbors, dpre, own, mate, state["near"], state["second"],
            state["far"], state["second_far"], backward, spread, ends, shifts, *last,
        )

    beside = [send_halos, tell_mate, lambda: half_backward(0), lambda: half_backward(1)]
    masks = [2**p for p in range(1, devices.bit_length() - 1)]
    for mask in masks:
        other = swapped(total, mask)
        if beside:
            beside.pop(0)()
        if mask != masks[-1]:
            total, other, state = lax.optimization_barrier((total, other, state))
            total = total + other
    for task in beside:
        task()
    input_grad = state["grad"]
    kernel_sum, bias_sum = call(
        finish_kernel, [VMEM, VMEM], [shape((27 * GC, CH), F32), shape((1, CH), F32)]
    )(total, other)
    kernel_grad = jnp.transpose(kernel_sum.reshape(3, 3, 3, GC, CH), (4, 3, 0, 1, 2))
    return (activated, input_grad, kernel_grad, bias_sum.reshape(CH))


def solution(mesh):
    devices = mesh.shape["bricks"]
    assert devices & (devices - 1) == 0
    return jax.shard_map(
        shards,
        mesh=mesh,
        in_specs=(
            P("bricks", None, None),
            P(),
            P(),
            P("bricks", None),
            P("bricks"),
            P("bricks", None),
            P("bricks", None, None),
        ),
        out_specs=(P("bricks", None, None), P("bricks", None, None), P(), P()),
        check_vma=False,
    )
```

```python
import functools

import jax
import jax.numpy as jnp
import numpy as np
from jax import lax
from jax.experimental import pallas as pl
from jax.experimental.pallas import tpu as pltpu
from jax.sharding import PartitionSpec as P

CH = 64
GC = 8
PART = 16
PARTS = CH // PART
SIDES = (0, 1, 2, 3, 5, 6, 7, 8)
TILE = 128
NEAR = 7
EDGE = 3
BUSY = 10**10
HEAD = 16
SUM_ROWS = 128
BF = jnp.bfloat16
F32 = jnp.float32


@functools.cache
def tables():
    strips = np.zeros((4, 512, TILE), np.float32)
    spread = np.zeros((256, 4 * TILE), np.float32)
    ends = np.zeros((4, 384, TILE), np.float32)
    shifts = np.zeros((4, 256, 8 * TILE), np.float32)
    fold = np.zeros((10 * PART, 10 * GC), np.float32)
    for bc in range(9):
        for i in range(PART):
            fold[bc * PART + i, bc * GC + i % GC] = 1
    fold[9 * PART, 9 * GC] = 1
    for half in range(2):
        for xx in range(4):
            for w in range(8):
                i, xp = 2 * half + xx // 2, xx % 2
                spread[half * 64 + xx * 8 + w, i * TILE + xp * 8 + w] = 1
                spread[half * 64 + 32 + xx * 8 + w, i * TILE + 32 + xp * 8 + w] = 1
                spread[128 + half * 64 + xx * 8 + w, i * TILE + 64 + xp * 8 + w] = 1
    for t in range(4):
        q, r = t // 2, t % 2
        own_y, own_z = (0 if q else 7), (0 if r else 7)
        far_y, far_z = 7 - own_y, 7 - own_z
        for half in range(2):
            for xx in range(4):
                for w in range(8):
                    plane = (4 * half + xx) * 64
                    strips[t, plane + own_y * 8 + w, half * 64 + xx * 8 + w] = 1
                    strips[t, plane + w * 8 + own_z, half * 64 + 32 + xx * 8 + w] = 1
        for xp in range(2):
            for w in range(8):
                ends[t, xp * 64 + far_y * 8 + w, xp * 8 + w] = 1
                ends[t, 128 + xp * 64 + w * 8 + far_z, 32 + xp * 8 + w] = 1
                ends[t, 256 + xp * 64 + far_y * 8 + w, 64 + xp * 8 + w] = 1
        out_y, out_z = (-1 if q else 8), (-1 if r else 8)
        for b in range(3):
            for c in range(3):
                if b == 1 and c == 1:
                    continue
                column = SIDES.index(b * 3 + c)
                for xp in range(2):
                    for y in range(8):
                        for z in range(8):
                            yy, zz = y + b - 1, z + c - 1
                            in_y, in_z = 0 <= yy < 8, 0 <= zz < 8
                            if in_y and in_z:
                                k = xp * 64 + yy * 8 + zz
                            elif in_z and yy == out_y:
                                k = 128 + xp * 8 + zz
                            elif in_y and zz == out_z:
                                k = 160 + xp * 8 + yy
                            elif yy == out_y and zz == out_z:
                                k = 192 + xp * 8 + far_z
                            else:
                                continue
                            shifts[t, k, column * TILE + xp * 64 + y * 8 + z] = 1
    return strips, spread, ends, shifts, fold


def left_half(shape):
    return lax.broadcasted_iota(jnp.int32, shape, len(shape) - 1) % TILE < 64


def join_halves(left, right):
    mixed = jnp.where(left_half(left.shape), left.astype(F32), right.astype(F32))
    return mixed.astype(left.dtype)


def dot(a, b):
    return jnp.dot(a, b, preferred_element_type=F32)


def count_own(slot_ref):
    total = jnp.int32(0)
    for s in range(slot_ref.shape[0]):
        total = total + (slot_ref[s] >= 0).astype(jnp.int32)
    return total


def count_sent(head):
    return jnp.max(head.astype(F32)).astype(jnp.int32)


def kind_of(brick):
    return jnp.maximum(brick, 0) & 3


def pack_bricks(slot_ref, field_ref, strips_ref, msg_ref):
    slots = field_ref.shape[0]
    for s in range(slots):
        table = strips_ref[kind_of(slot_ref[s])]
        row = s * 2 * CH
        msg_ref[row : row + CH, :] = dot(field_ref[s], table).astype(BF)
        msg_ref[row + CH : row + 2 * CH, :] = join_halves(
            field_ref[s, :, 0:TILE], field_ref[s, :, 3 * TILE : 4 * TILE]
        )
    row = slots * 2 * CH
    count = count_own(slot_ref).astype(F32)
    msg_ref[row : row + HEAD, :] = jnp.full((HEAD, TILE), count, F32).astype(BF)


def bring(pairs, sems):
    copies = [pltpu.make_async_copy(a, b, sems.at[i]) for i, (a, b) in enumerate(pairs)]
    for copy in copies:
        copy.start()
    return copies


def pack_kernel(slot_hbm, field_hbm, strips_hbm, msg_ref, field_ref, strips_ref, slot_ref, sems):
    pairs = ((slot_hbm, slot_ref), (field_hbm, field_ref), (strips_hbm, strips_ref))
    for copy in bring(pairs, sems):
        copy.wait()
    pack_bricks(slot_ref, field_ref, strips_ref, msg_ref)


def route_body(slots, own_ref, mate_ref, near_ref, far_ref, box):
    odd = (lax.axis_index("bricks") & 1) == 1
    head = slots * 2 * CH
    mine = count_sent(own_ref[head : head + HEAD, :])
    other = count_sent(mate_ref[head : head + HEAD, :])
    for s in range(2 * slots):
        box[s] = own_ref[s * CH : (s + 1) * CH, :]
        box[2 * slots + s] = mate_ref[s * CH : (s + 1) * CH, :]
    for j in range(NEAR):
        up = jnp.where(j < mine, mine - 1 - j, slots + other - 1 - (j - mine))
        down = jnp.where(j < mine, j, slots + j - mine)
        at = jnp.clip(jnp.where(odd, up, down), 0, 2 * slots - 1)
        near_ref[j * CH : (j + 1) * CH, :] = box[2 * at + 1]
        if j < EDGE:
            near_ref[(NEAR + j) * CH : (NEAR + j + 1) * CH, :] = box[2 * at]
            far_ref[j * CH : (j + 1) * CH, :] = box[2 * at + 1]
    row = (NEAR + EDGE) * CH
    both = (mine + other).astype(F32)
    near_ref[row : row + HEAD, :] = jnp.full((HEAD, TILE), both, F32).astype(BF)


def route_kernel(slots, own_ref, mate_ref, near_ref, far_ref, box):
    route_body(slots, own_ref, mate_ref, near_ref, far_ref, box)


def route_sum_kernel(slots, own_ref, mate_ref, near_ref, far_ref, sum_ref, box):
    route_body(slots, own_ref, mate_ref, near_ref, far_ref, box)
    high = slots * 2 * CH + HEAD
    low = high + SUM_ROWS
    parts = []
    for ref in (own_ref, mate_ref):
        parts.append(
            ref[high : high + SUM_ROWS, :].astype(F32) + ref[low : low + SUM_ROWS, :].astype(F32)
        )
    sum_ref[...] = parts[0] + parts[1]


def weight_kernel(taps_ref, forward_ref, backward_ref, work):
    values = taps_ref[...].astype(F32)
    lanes = lax.broadcasted_iota(jnp.int32, (GC, CH), 1) // GC

    def block(tap, part):
        tile = values[tap * GC : (tap + 1) * GC, :]
        groups = (2 * part, 2 * part + 1)
        return jnp.concatenate([jnp.where(lanes == g, tile, 0.0) for g in groups], axis=0)

    work[...] = jnp.zeros_like(work)
    for part in range(PARTS):
        out = slice(part * PART, (part + 1) * PART)
        for bc in range(9):
            for a in range(3):
                work[bc * PART : (bc + 1) * PART, a * TILE : a * TILE + CH] = block(a * 9 + bc, part)
        for a in range(3):
            turned = work[:, a * TILE : (a + 1) * TILE].T
            forward_ref[part, a * PART : (a + 1) * PART, :] = turned[out, 0 : 9 * PART].astype(BF)
    for part in range(PARTS):
        out = slice(part * PART, (part + 1) * PART)
        for a in range(3):
            blocks = [block((2 - a) * 9 + 8 - bc, part)[:, out] for bc in range(9)]
            backward_ref[part, a * PART : (a + 1) * PART, :] = jnp.concatenate(blocks, axis=1).astype(BF)


def make_finder(
    slot_hbm, link_hbm, own_ref, mate_ref, first_ref, second_ref, first_far_ref, second_far_ref,
    planes, strips, slot_ref, link_ref, sems,
):
    copies = bring(((slot_hbm, slot_ref), (link_hbm, link_ref)), sems)
    slots = slot_ref.shape[0]
    odd = (lax.axis_index("bricks") & 1) == 1
    head = slots * 2 * CH
    mine = count_sent(own_ref[head : head + HEAD, :])
    other = count_sent(mate_ref[head : head + HEAD, :])
    row = (NEAR + EDGE) * CH
    counts = [count_sent(ref[row : row + HEAD, :]) for ref in (first_ref, second_ref)]
    for k, ref in enumerate((own_ref, mate_ref)):
        for s in range(slots):
            strips[k * slots + s] = ref[s * 2 * CH : s * 2 * CH + CH, :]
            planes[k * slots + s] = ref[s * 2 * CH + CH : (s + 1) * 2 * CH, :]
    for side, (near, far) in enumerate(((first_ref, first_far_ref), (second_ref, second_far_ref))):
        for j in range(NEAR):
            planes[2 * slots + side * NEAR + j] = near[j * CH : (j + 1) * CH, :]
        for j in range(EDGE):
            strips[2 * slots + side * EDGE + j] = near[(NEAR + j) * CH : (NEAR + j + 1) * CH, :]
            planes[2 * slots + 2 * NEAR + side * EDGE + j] = far[j * CH : (j + 1) * CH, :]
    nothing = 2 * slots + 2 * NEAR + 2 * EDGE
    planes[nothing] = jnp.zeros((CH, TILE), BF)
    for copy in copies:
        copy.wait()
    base = slot_ref[0]
    low_side = odd.astype(jnp.int32)
    high_side = 1 - low_side
    low_count = jnp.where(odd, counts[1], counts[0])
    high_count = jnp.where(odd, counts[0], counts[1])
    mate_first = jnp.where(odd, base - other, base + mine)
    chip_low = jnp.where(odd, base - other, base)
    chip_high = jnp.where(odd, base + mine, base + mine + other)

    def on_chip(brick):
        own = (brick >= base) & (brick < base + mine)
        return jnp.where(own, brick - base, slots + brick - mate_first)

    def find_strip(brick):
        low = 2 * slots + low_side * EDGE + (chip_low - 1 - brick)
        high = 2 * slots + high_side * EDGE + (brick - chip_high)
        at = jnp.where(brick < chip_low, low, jnp.where(brick >= chip_high, high, on_chip(brick)))
        return jnp.clip(at, 0, 2 * slots + 2 * EDGE - 1)

    def outside(distance, count, side):
        near = 2 * slots + side * NEAR + distance
        far = 2 * slots + 2 * NEAR + side * EDGE + distance - count
        return jnp.where(distance < count, near, far)

    def find_plane(brick, exists):
        low = outside(chip_low - 1 - brick, low_count, low_side)
        high = outside(brick - chip_high, high_count, high_side)
        at = jnp.where(brick < chip_low, low, jnp.where(brick >= chip_high, high, on_chip(brick)))
        return jnp.clip(jnp.where(exists, at, nothing), 0, nothing)

    return base, mine, find_strip, find_plane


def put_taps(taps, bc, values):
    for i in range(5):
        for p in range(PARTS):
            taps[p, bc * PART : (bc + 1) * PART, i * TILE : (i + 1) * TILE] = values[
                i * CH + p * PART : i * CH + (p + 1) * PART, :
            ]


def convolve_brick(
    s, base, find_strip, find_plane, link_ref, field_ref, planes, strips,
    spread_ref, ends_ref, shifts_ref, weight_ref, mixed, taps, sums,
):
    brick = base + s
    kind = brick & 3
    step_y = 2 - 2 * (kind & 2)
    step_z = 1 - 2 * (kind & 1)
    sides = (brick + step_y, brick + step_z, brick + step_y + step_z)
    has_low = link_ref[s, 0] >= 0
    has_high = link_ref[s, 1] >= 0

    def outer(near):
        high = planes[find_plane(near + 4, has_high)]
        low = planes[find_plane(near - 4, has_low)]
        return join_halves(high, low)

    beside_y, beside_z, beside_yz = [strips[find_strip(m)] for m in sides]
    of_y = lax.broadcasted_iota(jnp.int32, (CH, TILE), 1) % 64 < 32
    beside = jnp.where(of_y, beside_y.astype(F32), beside_z.astype(F32)).astype(BF)
    beside = jnp.concatenate([beside, beside_yz], axis=1)
    halo = dot(beside, spread_ref[...]).astype(BF)
    outer_beside = jnp.concatenate([outer(m) for m in sides], axis=1)
    for i in range(4):
        rows = slice(i * CH, (i + 1) * CH)
        mixed[rows, 0:TILE] = field_ref[s, :, i * TILE : (i + 1) * TILE]
        mixed[rows, TILE:] = halo[:, i * TILE : (i + 1) * TILE]
    mixed[4 * CH :, 0:TILE] = outer(brick)
    mixed[4 * CH :, TILE:] = dot(outer_beside, ends_ref[kind]).astype(BF)
    for k in range(0, 8, 2):
        part = dot(mixed[...], shifts_ref[kind, :, k * TILE : (k + 2) * TILE]).astype(BF)
        for e in range(2):
            put_taps(taps, SIDES[k + e], part[:, e * TILE : (e + 1) * TILE])
    put_taps(taps, 4, mixed[:, 0:TILE])
    for p in range(PARTS):
        part = dot(weight_ref[p], taps[p, 0 : 9 * PART, :])
        for a in range(3):
            at = a * CH + p * PART
            sums[at : at + PART, :] = part[a * PART : (a + 1) * PART, :]
    turned = []
    for a in (0, 2):
        rows = slice(a * CH, (a + 1) * CH)
        turned.append(
            [pltpu.roll(sums[rows, i * TILE : (i + 1) * TILE], 64, 1) for i in range(5)]
        )
    left = left_half((CH, TILE))
    tiles = []
    for i in range(4):
        lower = jnp.where(left, turned[0][(i - 1) % 5], turned[0][i])
        upper = jnp.where(left, turned[1][i], turned[1][i + 1])
        tiles.append(sums[CH : 2 * CH, i * TILE : (i + 1) * TILE] + lower + upper)
    return tiles


def forward_kernel(
    slot_hbm, link_hbm, field_ref, own_ref, mate_ref, first_ref, second_ref, first_far_ref,
    second_far_ref, weight_ref, bias_ref, cortex_ref, upstream_ref, strips_ref, spread_ref,
    ends_ref, shifts_ref, fold_ref, out_ref, dpre_ref, msg_ref,
    planes, strips, mixed, taps, sums, slot_ref, link_ref, sems, spots, grads, keeps,
):
    slots = field_ref.shape[0]
    base, mine, find_strip, find_plane = make_finder(
        slot_hbm, link_hbm, own_ref, mate_ref, first_ref, second_ref, first_far_ref, second_far_ref,
        planes, strips, slot_ref, link_ref, sems,
    )
    for s in range(slots):
        keeps[s] = jnp.broadcast_to(cortex_ref[s : s + 1, :].astype(F32), (8, 512))
    taps[:, 9 * PART :, :] = jnp.ones((PARTS, PART, 5 * TILE), BF)
    grads[...] = jnp.zeros_like(grads)
    for s in range(slots):

        @pl.when(s >= mine)
        def _():
            out_ref[s] = jnp.zeros((CH, 512), BF)
            dpre_ref[s] = jnp.zeros((CH, 512), BF)

    square = (CH, CH)
    diagonal = lax.broadcasted_iota(jnp.int32, square, 0) == lax.broadcasted_iota(jnp.int32, square, 1)
    bias = jnp.sum(jnp.where(diagonal, bias_ref[...], 0.0), axis=1, keepdims=True)
    left = left_half((CH, TILE))
    zero = jnp.zeros((CH, TILE), F32)

    def put_spots(a, i, values):
        for p in range(PARTS):
            spots[p, a * PART : (a + 1) * PART, i * TILE : (i + 1) * TILE] = values[
                p * PART : (p + 1) * PART, :
            ]

    def one_brick(s, carry):
        tiles = convolve_brick(
            s, base, find_strip, find_plane, link_ref, field_ref, planes, strips,
            spread_ref, ends_ref, shifts_ref, weight_ref, mixed, taps, sums,
        )
        turned = []
        for i in range(4):
            lanes = slice(i * TILE, (i + 1) * TILE)
            pre = tiles[i] + bias
            keep = keeps[s, 0:1, lanes]
            sigma = 1.0 / (1.0 + jnp.exp(-pre))
            out_ref[s, :, lanes] = (pre * sigma * keep).astype(BF)
            slope = sigma * (1.0 + pre * (1.0 - sigma))
            dpre = (upstream_ref[s, :, lanes].astype(F32) * keep * slope).astype(BF)
            dpre_ref[s, :, lanes] = dpre
            put_spots(1, i, dpre)
            turned.append(pltpu.roll(dpre.astype(F32), 64, 1))
        put_spots(1, 4, zero.astype(BF))
        turned.append(zero)
        for i in range(4):
            put_spots(0, i, jnp.where(left, turned[i], turned[i + 1]).astype(BF))
            before = turned[i - 1] if i else zero
            put_spots(2, i, jnp.where(left, before, turned[i]).astype(BF))
        put_spots(0, 4, jnp.where(left, 0.0, turned[0]).astype(BF))
        put_spots(2, 4, jnp.where(left, turned[3], 0.0).astype(BF))
        for p in range(PARTS):
            grads[p] += lax.dot_general(
                spots[p], taps[p], (((1,), (1,)), ((), ())), preferred_element_type=F32
            )
        return carry

    lax.fori_loop(0, mine, one_brick, 0)

    pack_bricks(slot_ref, dpre_ref, strips_ref, msg_ref)
    high = slots * 2 * CH + HEAD
    low = high + SUM_ROWS
    rows = jnp.concatenate(
        [grads[p, a * PART : (a + 1) * PART, :] for a in range(3) for p in range(PARTS)], axis=0
    )
    group = lax.broadcasted_iota(jnp.int32, rows.shape, 0) // GC % 2
    column = lax.broadcasted_iota(jnp.int32, rows.shape, 1)
    same = (column // GC % 2 == group) | (column >= 9 * PART)
    full = jnp.dot(
        jnp.where(same, rows, 0.0), fold_ref[...],
        precision=lax.Precision.HIGHEST, preferred_element_type=F32,
    ).T
    last = jnp.concatenate([full[:, TILE:], jnp.zeros((2 * GC, CH), F32)], axis=0)
    half = SUM_ROWS - 10 * GC
    last = jnp.concatenate([last[0:half], last[half:]], axis=1)
    for at, values in ((0, full[:, 0:TILE]), (10 * GC, last)):
        rounded = values.astype(BF)
        size = values.shape[0]
        msg_ref[high + at : high + at + size, :] = rounded
        msg_ref[low + at : low + at + size, :] = (values - rounded.astype(F32)).astype(BF)


def backward_kernel(part, *refs):
    if part:
        refs, last_ref = refs[:13] + refs[14:], refs[13]
        field_ref, own_ref, out_ref = refs[2], refs[3], refs[13]
        slots = field_ref.shape[0]
        head = slots * 2 * CH
        half = count_sent(own_ref[head : head + HEAD, :]) // 2
        for s in range(slots):

            @pl.when(s < half)
            def _():
                out_ref[s] = last_ref[s]

    backward_body(part, *refs)


def backward_body(
    part, slot_hbm, link_hbm, field_ref, own_ref, mate_ref, first_ref, second_ref, first_far_ref,
    second_far_ref, weight_ref, spread_ref, ends_ref, shifts_ref, out_ref,
    planes, strips, mixed, taps, sums, slot_ref, link_ref, sems,
):
    slots = field_ref.shape[0]
    base, mine, find_strip, find_plane = make_finder(
        slot_hbm, link_hbm, own_ref, mate_ref, first_ref, second_ref, first_far_ref, second_far_ref,
        planes, strips, slot_ref, link_ref, sems,
    )
    if part == 1:
        for s in range(slots):

            @pl.when(s >= mine)
            def _():
                out_ref[s] = jnp.zeros((CH, 512), BF)

    def one_brick(s, carry):
        tiles = convolve_brick(
            s, base, find_strip, find_plane, link_ref, field_ref, planes, strips,
            spread_ref, ends_ref, shifts_ref, weight_ref, mixed, taps, sums,
        )
        for i in range(4):
            out_ref[s, :, i * TILE : (i + 1) * TILE] = tiles[i].astype(BF)
        return carry

    half = mine // 2
    lax.fori_loop(half * part, mine if part else half, one_brick, 0)


def finish_kernel(a_ref, b_ref, kernel_ref, bias_ref):
    total = a_ref[...] + b_ref[...]
    first, last = total[0 : 10 * GC, :], total[10 * GC :, :]
    turned = pltpu.roll(first, 64, 1)
    parts = (first, turned, jnp.concatenate([last, pltpu.roll(last, 64, 1)], axis=0))
    for a, part in enumerate(parts):
        kernel_ref[a * 9 * GC : (a + 1) * 9 * GC, :] = part[0 : 9 * GC, 0:CH]
    bias_ref[...] = turned[9 * GC : 9 * GC + 1, 0:CH]


VMEM = pl.BlockSpec(memory_space=pltpu.VMEM)
HBM = pl.BlockSpec(memory_space=pltpu.HBM)


def call(kernel, ins, outs, scratch=(), flops=0, size=400000, limit=24):
    return pl.pallas_call(
        kernel,
        in_specs=ins,
        out_specs=tuple(VMEM for _ in outs),
        out_shape=tuple(outs),
        scratch_shapes=list(scratch),
        compiler_params=pltpu.CompilerParams(vmem_limit_bytes=limit * 2**20),
        cost_estimate=pl.CostEstimate(flops=flops, bytes_accessed=size, transcendentals=0),
    )


def sent(block, route):
    return lax.ppermute(block, "bricks", route)


def shards(voxels, kernel, bias, cortex, slot_to_brick, neighbors, cotangent):
    slots = voxels.shape[0]
    devices = lax.axis_size("bricks")
    strips, spread, ends, shifts, fold = (jnp.asarray(t, BF) for t in tables())
    fold = fold.astype(F32)
    shape = jax.ShapeDtypeStruct
    pack_rows = slots * 2 * CH + HEAD
    near_shape = shape(((NEAR + EDGE) * CH + HEAD, TILE), BF)
    far_shape = shape((EDGE * CH, TILE), BF)

    def routed(block, chips):
        pairs = []
        for d in range(devices):
            to = d + 2 * chips - 1 if d % 2 else d - 2 * chips + 1
            if 0 <= to < devices:
                pairs.append((d, to))
        return sent(block, pairs)

    def swapped(block, mask):
        return sent(block, [(d, d ^ mask) for d in range(devices)])

    box = [pltpu.VMEM((4 * slots, CH, TILE), BF)]
    work = [
        pltpu.VMEM((2 * slots + 2 * NEAR + 2 * EDGE + 1, CH, TILE), BF),
        pltpu.VMEM((2 * slots + 2 * EDGE, CH, TILE), BF),
        pltpu.VMEM((5 * CH, 2 * TILE), BF),
        pltpu.VMEM((PARTS, 10 * PART, 5 * TILE), BF),
        pltpu.VMEM((3 * CH, 5 * TILE), F32),
        pltpu.SMEM(slot_to_brick.shape, jnp.int32),
        pltpu.SMEM(neighbors.shape, jnp.int32),
        pltpu.SemaphoreType.DMA((2,)),
    ]
    field = shape(voxels.shape, BF)

    (own,) = call(
        pack_kernel,
        [HBM] * 3,
        [shape((pack_rows, TILE), BF)],
        [pltpu.VMEM(voxels.shape, BF), pltpu.VMEM(strips.shape, BF), pltpu.SMEM(slot_to_brick.shape, jnp.int32), pltpu.SemaphoreType.DMA((3,))],
        limit=60,
    )(slot_to_brick, voxels, strips)
    mate = swapped(own, 1)
    weight_shape = shape((PARTS, 3 * PART, 9 * PART), BF)
    taps = jnp.transpose(kernel, (2, 3, 4, 1, 0)).reshape(27 * GC, CH)
    staged = call(
        weight_kernel, [VMEM], [weight_shape] * 2, [pltpu.VMEM((2 * TILE, 3 * TILE), F32)], flops=BUSY
    )(taps)
    near, far = call(
        functools.partial(route_kernel, slots), [VMEM, VMEM], [near_shape, far_shape], box,
        flops=BUSY,
    )(own, mate)
    near, far = routed(near, 1), routed(far, 2)
    near, far, staged = lax.optimization_barrier((near, far, staged))
    forward, backward = staged
    received = (near, swapped(near, 1), far, swapped(far, 1))
    activated, dpre, own = call(
        forward_kernel,
        [HBM, HBM] + [VMEM] * 16,
        [field, field, shape((pack_rows + 2 * SUM_ROWS, TILE), BF)],
        work
        + [
            pltpu.VMEM((PARTS, 3 * PART, 5 * TILE), BF),
            pltpu.VMEM((PARTS, 3 * PART, 10 * PART), F32),
            pltpu.VMEM((slots, 8, 512), F32),
        ],
        flops=4 * 10**9,
    )(
        slot_to_brick, neighbors, voxels, own, mate, *received, forward, bias.reshape(1, CH),
        cortex, cotangent, strips, spread, ends, shifts, fold,
    )
    mate = swapped(own, 1)
    near, far, total = call(
        functools.partial(route_sum_kernel, slots),
        [VMEM, VMEM],
        [near_shape, far_shape, shape((SUM_ROWS, TILE), F32)],
        box,
    )(own, mate)
    state = dict(near=near, far=far)

    def send_halos():
        state.update(near=routed(state["near"], 1), far=routed(state["far"], 2))

    def tell_mate():
        near, far = state["near"], state["far"]
        state.update(second=swapped(near, 1), second_far=swapped(far, 1))

    def half_backward(part):
        last = [state["grad"]] if part else []
        (state["grad"],) = call(
            functools.partial(backward_kernel, part),
            [HBM, HBM] + [VMEM] * (11 + part),
            [field],
            work,
            flops=10**9,
        )(
            slot_to_brick, neighbors, dpre, own, mate, state["near"], state["second"],
            state["far"], state["second_far"], backward, spread, ends, shifts, *last,
        )

    beside = [send_halos, tell_mate, lambda: half_backward(0), lambda: half_backward(1)]
    masks = [2**p for p in range(1, devices.bit_length() - 1)]
    for mask in masks:
        other = swapped(total, mask)
        if beside:
            beside.pop(0)()
        if mask != masks[-1]:
            total, other, state = lax.optimization_barrier((total, other, state))
            total = total + other
    for task in beside:
        task()
    input_grad = state["grad"]
    kernel_sum, bias_sum = call(
        finish_kernel, [VMEM, VMEM], [shape((27 * GC, CH), F32), shape((1, CH), F32)]
    )(total, other)
    kernel_grad = jnp.transpose(kernel_sum.reshape(3, 3, 3, GC, CH), (4, 3, 0, 1, 2))
    return (activated, input_grad, kernel_grad, bias_sum.reshape(CH))


def solution(mesh):
    devices = mesh.shape["bricks"]
    assert devices & (devices - 1) == 0
    return jax.shard_map(
        shards,
        mesh=mesh,
        in_specs=(
            P("bricks", None, None),
            P(),
            P(),
            P("bricks", None),
            P("bricks"),
            P("bricks", None),
            P("bricks", None, None),
        ),
        out_specs=(P("bricks", None, None), P("bricks", None, None), P(), P()),
        check_vma=False,
    )
```

```python
import functools

import jax
import jax.numpy as jnp
import numpy as np
from jax import lax
from jax.experimental import pallas as pl
from jax.experimental.pallas import tpu as pltpu
from jax.sharding import PartitionSpec as P

CH = 64
GC = 8
PART = 16
PARTS = CH // PART
SIDES = (0, 1, 2, 3, 5, 6, 7, 8)
TILE = 128
NEAR = 7
EDGE = 3
BUSY = 10**10
HEAD = 16
SUM_ROWS = 128
BF = jnp.bfloat16
F32 = jnp.float32


@functools.cache
def tables():
    strips = np.zeros((4, 512, TILE), np.float32)
    spread = np.zeros((256, 4 * TILE), np.float32)
    ends = np.zeros((4, 384, TILE), np.float32)
    shifts = np.zeros((4, 256, 8 * TILE), np.float32)
    fold = np.zeros((10 * PART, 10 * GC), np.float32)
    for bc in range(9):
        for i in range(PART):
            fold[bc * PART + i, bc * GC + i % GC] = 1
    fold[9 * PART, 9 * GC] = 1
    for half in range(2):
        for xx in range(4):
            for w in range(8):
                i, xp = 2 * half + xx // 2, xx % 2
                spread[half * 64 + xx * 8 + w, i * TILE + xp * 8 + w] = 1
                spread[half * 64 + 32 + xx * 8 + w, i * TILE + 32 + xp * 8 + w] = 1
                spread[128 + half * 64 + xx * 8 + w, i * TILE + 64 + xp * 8 + w] = 1
    for t in range(4):
        q, r = t // 2, t % 2
        own_y, own_z = (0 if q else 7), (0 if r else 7)
        far_y, far_z = 7 - own_y, 7 - own_z
        for half in range(2):
            for xx in range(4):
                for w in range(8):
                    plane = (4 * half + xx) * 64
                    strips[t, plane + own_y * 8 + w, half * 64 + xx * 8 + w] = 1
                    strips[t, plane + w * 8 + own_z, half * 64 + 32 + xx * 8 + w] = 1
        for xp in range(2):
            for w in range(8):
                ends[t, xp * 64 + far_y * 8 + w, xp * 8 + w] = 1
                ends[t, 128 + xp * 64 + w * 8 + far_z, 32 + xp * 8 + w] = 1
                ends[t, 256 + xp * 64 + far_y * 8 + w, 64 + xp * 8 + w] = 1
        out_y, out_z = (-1 if q else 8), (-1 if r else 8)
        for b in range(3):
            for c in range(3):
                if b == 1 and c == 1:
                    continue
                column = SIDES.index(b * 3 + c)
                for xp in range(2):
                    for y in range(8):
                        for z in range(8):
                            yy, zz = y + b - 1, z + c - 1
                            in_y, in_z = 0 <= yy < 8, 0 <= zz < 8
                            if in_y and in_z:
                                k = xp * 64 + yy * 8 + zz
                            elif in_z and yy == out_y:
                                k = 128 + xp * 8 + zz
                            elif in_y and zz == out_z:
                                k = 160 + xp * 8 + yy
                            elif yy == out_y and zz == out_z:
                                k = 192 + xp * 8 + far_z
                            else:
                                continue
                            shifts[t, k, column * TILE + xp * 64 + y * 8 + z] = 1
    return strips, spread, ends, shifts, fold


def left_half(shape):
    return lax.broadcasted_iota(jnp.int32, shape, len(shape) - 1) % TILE < 64


def join_halves(left, right):
    mixed = jnp.where(left_half(left.shape), left.astype(F32), right.astype(F32))
    return mixed.astype(left.dtype)


def dot(a, b):
    return jnp.dot(a, b, preferred_element_type=F32)


def count_own(slot_ref):
    total = jnp.int32(0)
    for s in range(slot_ref.shape[0]):
        total = total + (slot_ref[s] >= 0).astype(jnp.int32)
    return total


def count_sent(head):
    return jnp.max(head.astype(F32)).astype(jnp.int32)


def kind_of(brick):
    return jnp.maximum(brick, 0) & 3


def pack_bricks(slot_ref, field_ref, strips_ref, msg_ref):
    slots = field_ref.shape[0]
    for s in range(slots):
        table = strips_ref[kind_of(slot_ref[s])]
        row = s * 2 * CH
        msg_ref[row : row + CH, :] = dot(field_ref[s], table).astype(BF)
        msg_ref[row + CH : row + 2 * CH, :] = join_halves(
            field_ref[s, :, 0:TILE], field_ref[s, :, 3 * TILE : 4 * TILE]
        )
    row = slots * 2 * CH
    count = count_own(slot_ref).astype(F32)
    msg_ref[row : row + HEAD, :] = jnp.full((HEAD, TILE), count, F32).astype(BF)


def bring(pairs, sems):
    copies = [pltpu.make_async_copy(a, b, sems.at[i]) for i, (a, b) in enumerate(pairs)]
    for copy in copies:
        copy.start()
    return copies


def pack_kernel(slot_hbm, field_hbm, strips_hbm, msg_ref, field_ref, strips_ref, slot_ref, sems):
    pairs = ((slot_hbm, slot_ref), (field_hbm, field_ref), (strips_hbm, strips_ref))
    for copy in bring(pairs, sems):
        copy.wait()
    pack_bricks(slot_ref, field_ref, strips_ref, msg_ref)


def route_body(slots, own_ref, mate_ref, near_ref, far_ref, box):
    odd = (lax.axis_index("bricks") & 1) == 1
    head = slots * 2 * CH
    mine = count_sent(own_ref[head : head + HEAD, :])
    other = count_sent(mate_ref[head : head + HEAD, :])
    for s in range(2 * slots):
        box[s] = own_ref[s * CH : (s + 1) * CH, :]
        box[2 * slots + s] = mate_ref[s * CH : (s + 1) * CH, :]
    for j in range(NEAR):
        up = jnp.where(j < mine, mine - 1 - j, slots + other - 1 - (j - mine))
        down = jnp.where(j < mine, j, slots + j - mine)
        at = jnp.clip(jnp.where(odd, up, down), 0, 2 * slots - 1)
        near_ref[j * CH : (j + 1) * CH, :] = box[2 * at + 1]
        if j < EDGE:
            near_ref[(NEAR + j) * CH : (NEAR + j + 1) * CH, :] = box[2 * at]
            far_ref[j * CH : (j + 1) * CH, :] = box[2 * at + 1]
    row = (NEAR + EDGE) * CH
    both = (mine + other).astype(F32)
    near_ref[row : row + HEAD, :] = jnp.full((HEAD, TILE), both, F32).astype(BF)


def route_kernel(slots, own_ref, mate_ref, near_ref, far_ref, box):
    route_body(slots, own_ref, mate_ref, near_ref, far_ref, box)


def route_sum_kernel(slots, own_ref, mate_ref, near_ref, far_ref, sum_ref, box):
    route_body(slots, own_ref, mate_ref, near_ref, far_ref, box)
    high = slots * 2 * CH + HEAD
    low = high + SUM_ROWS
    parts = []
    for ref in (own_ref, mate_ref):
        parts.append(
            ref[high : high + SUM_ROWS, :].astype(F32) + ref[low : low + SUM_ROWS, :].astype(F32)
        )
    sum_ref[...] = parts[0] + parts[1]


def weight_kernel(taps_ref, forward_ref, backward_ref, work):
    values = taps_ref[...].astype(F32)
    lanes = lax.broadcasted_iota(jnp.int32, (GC, CH), 1) // GC

    def block(tap, part):
        tile = values[tap * GC : (tap + 1) * GC, :]
        groups = (2 * part, 2 * part + 1)
        return jnp.concatenate([jnp.where(lanes == g, tile, 0.0) for g in groups], axis=0)

    work[...] = jnp.zeros_like(work)
    for part in range(PARTS):
        out = slice(part * PART, (part + 1) * PART)
        for bc in range(9):
            for a in range(3):
                work[bc * PART : (bc + 1) * PART, a * TILE : a * TILE + CH] = block(a * 9 + bc, part)
        for a in range(3):
            turned = work[:, a * TILE : (a + 1) * TILE].T
            forward_ref[part, a * PART : (a + 1) * PART, :] = turned[out, 0 : 9 * PART].astype(BF)
    for part in range(PARTS):
        out = slice(part * PART, (part + 1) * PART)
        for a in range(3):
            blocks = [block((2 - a) * 9 + 8 - bc, part)[:, out] for bc in range(9)]
            backward_ref[part, a * PART : (a + 1) * PART, :] = jnp.concatenate(blocks, axis=1).astype(BF)


def make_finder(
    slot_hbm, link_hbm, own_ref, mate_ref, first_ref, second_ref, first_far_ref, second_far_ref,
    planes, strips, slot_ref, link_ref, sems,
):
    copies = bring(((slot_hbm, slot_ref), (link_hbm, link_ref)), sems)
    slots = slot_ref.shape[0]
    odd = (lax.axis_index("bricks") & 1) == 1
    head = slots * 2 * CH
    mine = count_sent(own_ref[head : head + HEAD, :])
    other = count_sent(mate_ref[head : head + HEAD, :])
    row = (NEAR + EDGE) * CH
    counts = [count_sent(ref[row : row + HEAD, :]) for ref in (first_ref, second_ref)]
    for k, ref in enumerate((own_ref, mate_ref)):
        for s in range(slots):
            strips[k * slots + s] = ref[s * 2 * CH : s * 2 * CH + CH, :]
            planes[k * slots + s] = ref[s * 2 * CH + CH : (s + 1) * 2 * CH, :]
    for side, (near, far) in enumerate(((first_ref, first_far_ref), (second_ref, second_far_ref))):
        for j in range(NEAR):
            planes[2 * slots + side * NEAR + j] = near[j * CH : (j + 1) * CH, :]
        for j in range(EDGE):
            strips[2 * slots + side * EDGE + j] = near[(NEAR + j) * CH : (NEAR + j + 1) * CH, :]
            planes[2 * slots + 2 * NEAR + side * EDGE + j] = far[j * CH : (j + 1) * CH, :]
    nothing = 2 * slots + 2 * NEAR + 2 * EDGE
    planes[nothing] = jnp.zeros((CH, TILE), BF)
    for copy in copies:
        copy.wait()
    base = slot_ref[0]
    low_side = odd.astype(jnp.int32)
    high_side = 1 - low_side
    low_count = jnp.where(odd, counts[1], counts[0])
    high_count = jnp.where(odd, counts[0], counts[1])
    mate_first = jnp.where(odd, base - other, base + mine)
    chip_low = jnp.where(odd, base - other, base)
    chip_high = jnp.where(odd, base + mine, base + mine + other)

    def on_chip(brick):
        own = (brick >= base) & (brick < base + mine)
        return jnp.where(own, brick - base, slots + brick - mate_first)

    def find_strip(brick):
        low = 2 * slots + low_side * EDGE + (chip_low - 1 - brick)
        high = 2 * slots + high_side * EDGE + (brick - chip_high)
        at = jnp.where(brick < chip_low, low, jnp.where(brick >= chip_high, high, on_chip(brick)))
        return jnp.clip(at, 0, 2 * slots + 2 * EDGE - 1)

    def outside(distance, count, side):
        near = 2 * slots + side * NEAR + distance
        far = 2 * slots + 2 * NEAR + side * EDGE + distance - count
        return jnp.where(distance < count, near, far)

    def find_plane(brick, exists):
        low = outside(chip_low - 1 - brick, low_count, low_side)
        high = outside(brick - chip_high, high_count, high_side)
        at = jnp.where(brick < chip_low, low, jnp.where(brick >= chip_high, high, on_chip(brick)))
        return jnp.clip(jnp.where(exists, at, nothing), 0, nothing)

    return base, mine, find_strip, find_plane


def convolve_pair(
    pair, base, find_strip, find_plane, link_ref, field_ref, planes, strips,
    spread_ref, ends_ref, shifts_ref, weight_ref, mixed, taps, sums,
):
    slots = (2 * pair, 2 * pair + 1)
    kinds, outers, besides = [], [], []
    of_y = lax.broadcasted_iota(jnp.int32, (CH, TILE), 1) % 64 < 32
    for s in slots:
        brick = base + s
        kind = brick & 3
        step_y = 2 - 2 * (kind & 2)
        step_z = 1 - 2 * (kind & 1)
        sides = (brick + step_y, brick + step_z, brick + step_y + step_z)
        has_low = link_ref[s, 0] >= 0
        has_high = link_ref[s, 1] >= 0

        def outer(near):
            high = planes[find_plane(near + 4, has_high)]
            low = planes[find_plane(near - 4, has_low)]
            return join_halves(high, low)

        beside_y, beside_z, beside_yz = [strips[find_strip(m)] for m in sides]
        beside = jnp.where(of_y, beside_y.astype(F32), beside_z.astype(F32)).astype(BF)
        besides.append(jnp.concatenate([beside, beside_yz], axis=1))
        kinds.append(kind)
        outers.append((outer(brick), jnp.concatenate([outer(m) for m in sides], axis=1)))
    halos = dot(jnp.concatenate(besides, axis=0), spread_ref[...]).astype(BF)
    for e, s in enumerate(slots):
        for i in range(4):
            rows = slice(i * CH, (i + 1) * CH)
            mixed[e, rows, 0:TILE] = field_ref[s, :, i * TILE : (i + 1) * TILE]
            mixed[e, rows, TILE:] = halos[e * CH : (e + 1) * CH, i * TILE : (i + 1) * TILE]
        mixed[e, 4 * CH :, 0:TILE] = outers[e][0]
        mixed[e, 4 * CH :, TILE:] = dot(outers[e][1], ends_ref[kinds[e]]).astype(BF)

    def put_taps(e, bc, values):
        for i in range(5):
            lanes = slice((5 * e + i) * TILE, (5 * e + i + 1) * TILE)
            for p in range(PARTS):
                taps[p, bc * PART : (bc + 1) * PART, lanes] = values[
                    i * CH + p * PART : i * CH + (p + 1) * PART, :
                ]

    for e in range(2):
        for k in range(0, 8, 2):
            part = dot(mixed[e], shifts_ref[kinds[e], :, k * TILE : (k + 2) * TILE]).astype(BF)
            put_taps(e, SIDES[k], part[:, 0:TILE])
            put_taps(e, SIDES[k + 1], part[:, TILE:])
        put_taps(e, 4, mixed[e, :, 0:TILE])
    for p in range(PARTS):
        part = dot(weight_ref[p], taps[p, 0 : 9 * PART, :])
        for a in range(3):
            at = a * CH + p * PART
            sums[at : at + PART, :] = part[a * PART : (a + 1) * PART, :]
    left = left_half((CH, TILE))
    results = []
    for e in range(2):
        first = 5 * e
        turned = []
        for a in (0, 2):
            rows = slice(a * CH, (a + 1) * CH)
            turned.append(
                [
                    pltpu.roll(sums[rows, (first + i) * TILE : (first + i + 1) * TILE], 64, 1)
                    for i in range(5)
                ]
            )
        tiles = []
        for i in range(4):
            lower = jnp.where(left, turned[0][(i - 1) % 5], turned[0][i])
            upper = jnp.where(left, turned[1][i], turned[1][i + 1])
            lanes = slice((first + i) * TILE, (first + i + 1) * TILE)
            tiles.append(sums[CH : 2 * CH, lanes] + lower + upper)
        results.append(tiles)
    return results


def forward_kernel(
    slot_hbm, link_hbm, field_ref, own_ref, mate_ref, first_ref, second_ref, first_far_ref,
    second_far_ref, weight_ref, bias_ref, cortex_ref, upstream_ref, strips_ref, spread_ref,
    ends_ref, shifts_ref, fold_ref, out_ref, dpre_ref, msg_ref,
    planes, strips, mixed, taps, sums, slot_ref, link_ref, sems, spots, grads,
):
    slots = field_ref.shape[0]
    base, mine, find_strip, find_plane = make_finder(
        slot_hbm, link_hbm, own_ref, mate_ref, first_ref, second_ref, first_far_ref, second_far_ref,
        planes, strips, slot_ref, link_ref, sems,
    )
    for pair in range(slots // 2):
        taps[pair, :, 9 * PART :, :] = jnp.ones((PARTS, PART, 10 * TILE), BF)

    square = (CH, CH)
    diagonal = lax.broadcasted_iota(jnp.int32, square, 0) == lax.broadcasted_iota(jnp.int32, square, 1)
    bias = jnp.sum(jnp.where(diagonal, bias_ref[...], 0.0), axis=1, keepdims=True)
    left = left_half((CH, TILE))
    zero = jnp.zeros((CH, TILE), F32)

    def put_spots(pair, a, i, values):
        for p in range(PARTS):
            spots[pair, p, a * PART : (a + 1) * PART, i * TILE : (i + 1) * TILE] = values[
                p * PART : (p + 1) * PART, :
            ]

    for pair in range(slots // 2):
        results = convolve_pair(
            pair, base, find_strip, find_plane, link_ref, field_ref, planes, strips,
            spread_ref, ends_ref, shifts_ref, weight_ref, mixed.at[pair], taps.at[pair], sums.at[pair],
        )
        for e, tiles in enumerate(results):
            s = 2 * pair + e
            present = jnp.where(s < mine, 1.0, 0.0)
            turned = []
            for i in range(4):
                lanes = slice(i * TILE, (i + 1) * TILE)
                pre = tiles[i] + bias
                keep = cortex_ref[s : s + 1, lanes].astype(F32) * present
                sigma = 1.0 / (1.0 + jnp.exp(-pre))
                out_ref[s, :, lanes] = (pre * sigma * keep).astype(BF)
                slope = sigma * (1.0 + pre * (1.0 - sigma))
                dpre = (upstream_ref[s, :, lanes].astype(F32) * keep * slope).astype(BF)
                dpre_ref[s, :, lanes] = dpre
                put_spots(pair, 1, 5 * e + i, dpre)
                turned.append(pltpu.roll(dpre.astype(F32), 64, 1))
            put_spots(pair, 1, 5 * e + 4, zero.astype(BF))
            turned.append(zero)
            for i in range(4):
                here = jnp.where(left, turned[i], turned[i + 1])
                put_spots(pair, 0, 5 * e + i, here.astype(BF))
                here = jnp.where(left, turned[i - 1] if i else zero, turned[i])
                put_spots(pair, 2, 5 * e + i, here.astype(BF))
            put_spots(pair, 0, 5 * e + 4, jnp.where(left, 0.0, turned[0]).astype(BF))
            put_spots(pair, 2, 5 * e + 4, jnp.where(left, turned[3], 0.0).astype(BF))
        for p in range(PARTS):
            term = lax.dot_general(
                spots[pair, p], taps[pair, p], (((1,), (1,)), ((), ())), preferred_element_type=F32
            )
            grads[p] = grads[p] + term if pair else term

    pack_bricks(slot_ref, dpre_ref, strips_ref, msg_ref)
    high = slots * 2 * CH + HEAD
    low = high + SUM_ROWS
    rows = jnp.concatenate(
        [grads[p, a * PART : (a + 1) * PART, :] for a in range(3) for p in range(PARTS)], axis=0
    )
    group = lax.broadcasted_iota(jnp.int32, rows.shape, 0) // GC % 2
    column = lax.broadcasted_iota(jnp.int32, rows.shape, 1)
    same = (column // GC % 2 == group) | (column >= 9 * PART)
    full = jnp.dot(
        jnp.where(same, rows, 0.0), fold_ref[...],
        precision=lax.Precision.HIGHEST, preferred_element_type=F32,
    ).T
    last = jnp.concatenate([full[:, TILE:], jnp.zeros((2 * GC, CH), F32)], axis=0)
    half = SUM_ROWS - 10 * GC
    last = jnp.concatenate([last[0:half], last[half:]], axis=1)
    for at, values in ((0, full[:, 0:TILE]), (10 * GC, last)):
        rounded = values.astype(BF)
        size = values.shape[0]
        msg_ref[high + at : high + at + size, :] = rounded
        msg_ref[low + at : low + at + size, :] = (values - rounded.astype(F32)).astype(BF)


def backward_kernel(pairs, *refs):
    if pairs[0] == 0:
        backward_body(pairs, *refs)
        return
    last_ref, out_ref = refs[13], refs[14]
    for s in range(2 * pairs[0]):
        out_ref[s] = last_ref[s]
    backward_body(pairs, *refs[:13], *refs[14:])


def backward_body(
    pairs, slot_hbm, link_hbm, field_ref, own_ref, mate_ref, first_ref, second_ref, first_far_ref,
    second_far_ref, weight_ref, spread_ref, ends_ref, shifts_ref, out_ref,
    planes, strips, mixed, taps, sums, slot_ref, link_ref, sems,
):
    base, mine, find_strip, find_plane = make_finder(
        slot_hbm, link_hbm, own_ref, mate_ref, first_ref, second_ref, first_far_ref, second_far_ref,
        planes, strips, slot_ref, link_ref, sems,
    )
    for pair in pairs:
        results = convolve_pair(
            pair, base, find_strip, find_plane, link_ref, field_ref, planes, strips,
            spread_ref, ends_ref, shifts_ref, weight_ref, mixed.at[pair], taps.at[pair], sums.at[pair],
        )
        for e, tiles in enumerate(results):
            s = 2 * pair + e
            present = jnp.where(s < mine, 1.0, 0.0)
            for i in range(4):
                out_ref[s, :, i * TILE : (i + 1) * TILE] = (tiles[i] * present).astype(BF)


def finish_kernel(a_ref, b_ref, kernel_ref, bias_ref):
    total = a_ref[...] + b_ref[...]
    first, last = total[0 : 10 * GC, :], total[10 * GC :, :]
    turned = pltpu.roll(first, 64, 1)
    parts = (first, turned, jnp.concatenate([last, pltpu.roll(last, 64, 1)], axis=0))
    for a, part in enumerate(parts):
        kernel_ref[a * 9 * GC : (a + 1) * 9 * GC, :] = part[0 : 9 * GC, 0:CH]
    bias_ref[...] = turned[9 * GC : 9 * GC + 1, 0:CH]


VMEM = pl.BlockSpec(memory_space=pltpu.VMEM)
HBM = pl.BlockSpec(memory_space=pltpu.HBM)


def call(kernel, ins, outs, scratch=(), flops=0, size=400000, limit=24):
    return pl.pallas_call(
        kernel,
        in_specs=ins,
        out_specs=tuple(VMEM for _ in outs),
        out_shape=tuple(outs),
        scratch_shapes=list(scratch),
        compiler_params=pltpu.CompilerParams(vmem_limit_bytes=limit * 2**20),
        cost_estimate=pl.CostEstimate(flops=flops, bytes_accessed=size, transcendentals=0),
    )


def sent(block, route):
    return lax.ppermute(block, "bricks", route)


def shards(voxels, kernel, bias, cortex, slot_to_brick, neighbors, cotangent):
    slots = voxels.shape[0]
    devices = lax.axis_size("bricks")
    strips, spread, ends, shifts, fold = (jnp.asarray(t, BF) for t in tables())
    fold = fold.astype(F32)
    shape = jax.ShapeDtypeStruct
    pack_rows = slots * 2 * CH + HEAD
    near_shape = shape(((NEAR + EDGE) * CH + HEAD, TILE), BF)
    far_shape = shape((EDGE * CH, TILE), BF)

    def routed(block, chips):
        pairs = []
        for d in range(devices):
            to = d + 2 * chips - 1 if d % 2 else d - 2 * chips + 1
            if 0 <= to < devices:
                pairs.append((d, to))
        return sent(block, pairs)

    def swapped(block, mask):
        return sent(block, [(d, d ^ mask) for d in range(devices)])

    box = [pltpu.VMEM((4 * slots, CH, TILE), BF)]
    work = [
        pltpu.VMEM((2 * slots + 2 * NEAR + 2 * EDGE + 1, CH, TILE), BF),
        pltpu.VMEM((2 * slots + 2 * EDGE, CH, TILE), BF),
        pltpu.VMEM((slots // 2, 2, 5 * CH, 2 * TILE), BF),
        pltpu.VMEM((slots // 2, PARTS, 10 * PART, 10 * TILE), BF),
        pltpu.VMEM((slots // 2, 3 * CH, 10 * TILE), F32),
        pltpu.SMEM(slot_to_brick.shape, jnp.int32),
        pltpu.SMEM(neighbors.shape, jnp.int32),
        pltpu.SemaphoreType.DMA((2,)),
    ]
    field = shape(voxels.shape, BF)

    (own,) = call(
        pack_kernel,
        [HBM] * 3,
        [shape((pack_rows, TILE), BF)],
        [pltpu.VMEM(voxels.shape, BF), pltpu.VMEM(strips.shape, BF), pltpu.SMEM(slot_to_brick.shape, jnp.int32), pltpu.SemaphoreType.DMA((3,))],
        limit=60,
    )(slot_to_brick, voxels, strips)
    mate = swapped(own, 1)
    weight_shape = shape((PARTS, 3 * PART, 9 * PART), BF)
    taps = jnp.transpose(kernel, (2, 3, 4, 1, 0)).reshape(27 * GC, CH)
    staged = call(
        weight_kernel, [VMEM], [weight_shape] * 2, [pltpu.VMEM((2 * TILE, 3 * TILE), F32)], flops=BUSY
    )(taps)
    near, far = call(
        functools.partial(route_kernel, slots), [VMEM, VMEM], [near_shape, far_shape], box,
        flops=BUSY,
    )(own, mate)
    near, far = routed(near, 1), routed(far, 2)
    near, far, staged = lax.optimization_barrier((near, far, staged))
    forward, backward = staged
    received = (near, swapped(near, 1), far, swapped(far, 1))
    activated, dpre, own = call(
        forward_kernel,
        [HBM, HBM] + [VMEM] * 16,
        [field, field, shape((pack_rows + 2 * SUM_ROWS, TILE), BF)],
        work
        + [
            pltpu.VMEM((slots // 2, PARTS, 3 * PART, 10 * TILE), BF),
            pltpu.VMEM((PARTS, 3 * PART, 10 * PART), F32),
        ],
        flops=4 * 10**9,
    )(
        slot_to_brick, neighbors, voxels, own, mate, *received, forward, bias.reshape(1, CH),
        cortex, cotangent, strips, spread, ends, shifts, fold,
    )
    mate = swapped(own, 1)
    near, far, total = call(
        functools.partial(route_sum_kernel, slots),
        [VMEM, VMEM],
        [near_shape, far_shape, shape((SUM_ROWS, TILE), F32)],
        box,
    )(own, mate)
    state = dict(near=near, far=far)

    def send_halos():
        state.update(near=routed(state["near"], 1), far=routed(state["far"], 2))

    def tell_mate():
        near, far = state["near"], state["far"]
        state.update(second=swapped(near, 1), second_far=swapped(far, 1))

    def part_backward(pairs):
        last = [state["grad"]] if pairs[0] else []
        (state["grad"],) = call(
            functools.partial(backward_kernel, pairs),
            [HBM, HBM] + [VMEM] * (11 + len(last)),
            [field],
            work,
            flops=10**9,
        )(
            slot_to_brick, neighbors, dpre, own, mate, state["near"], state["second"],
            state["far"], state["second_far"], backward, spread, ends, shifts, *last,
        )

    pairs = range(slots // 2)
    beside = [
        send_halos,
        tell_mate,
        lambda: part_backward(pairs[:1]),
        lambda: part_backward(pairs[1:]),
    ]
    masks = [2**p for p in range(1, devices.bit_length() - 1)]
    for mask in masks:
        other = swapped(total, mask)
        if beside:
            beside.pop(0)()
        if mask != masks[-1]:
            total, other, state = lax.optimization_barrier((total, other, state))
            total = total + other
    for task in beside:
        task()
    input_grad = state["grad"]
    kernel_sum, bias_sum = call(
        finish_kernel, [VMEM, VMEM], [shape((27 * GC, CH), F32), shape((1, CH), F32)]
    )(total, other)
    kernel_grad = jnp.transpose(kernel_sum.reshape(3, 3, 3, GC, CH), (4, 3, 0, 1, 2))
    return (activated, input_grad, kernel_grad, bias_sum.reshape(CH))


def solution(mesh):
    devices = mesh.shape["bricks"]
    assert devices & (devices - 1) == 0
    return jax.shard_map(
        shards,
        mesh=mesh,
        in_specs=(
            P("bricks", None, None),
            P(),
            P(),
            P("bricks", None),
            P("bricks"),
            P("bricks", None),
            P("bricks", None, None),
        ),
        out_specs=(P("bricks", None, None), P("bricks", None, None), P(), P()),
        check_vma=False,
    )
```

```python
import functools

import jax
import jax.numpy as jnp
import numpy as np
from jax import lax
from jax.experimental import pallas as pl
from jax.experimental.pallas import tpu as pltpu
from jax.sharding import PartitionSpec as P

CH = 64
GC = 8
PART = 16
PARTS = CH // PART
SIDES = (0, 1, 2, 3, 5, 6, 7, 8)
TILE = 128
NEAR = 8
FAR = 4
EDGE = 3
BUSY = 10**10
HEAD = 16
NEAR_ROWS = (NEAR // 2 + EDGE) * CH + HEAD
SUM_ROWS = 128
BF = jnp.bfloat16
F32 = jnp.float32


@functools.cache
def tables():
    strips = np.zeros((4, 512, TILE), np.float32)
    spread = np.zeros((256, 4 * TILE), np.float32)
    ends = np.zeros((4, 384, TILE), np.float32)
    shifts = np.zeros((4, 256, 8 * TILE), np.float32)
    fold = np.zeros((10 * PART, 10 * GC), np.float32)
    for bc in range(9):
        for i in range(PART):
            fold[bc * PART + i, bc * GC + i % GC] = 1
    fold[9 * PART, 9 * GC] = 1
    for half in range(2):
        for xx in range(4):
            for w in range(8):
                i, xp = 2 * half + xx // 2, xx % 2
                spread[half * 64 + xx * 8 + w, i * TILE + xp * 8 + w] = 1
                spread[half * 64 + 32 + xx * 8 + w, i * TILE + 32 + xp * 8 + w] = 1
                spread[128 + half * 64 + xx * 8 + w, i * TILE + 64 + xp * 8 + w] = 1
    for t in range(4):
        q, r = t // 2, t % 2
        own_y, own_z = (0 if q else 7), (0 if r else 7)
        far_y, far_z = 7 - own_y, 7 - own_z
        for half in range(2):
            for xx in range(4):
                for w in range(8):
                    plane = (4 * half + xx) * 64
                    strips[t, plane + own_y * 8 + w, half * 64 + xx * 8 + w] = 1
                    strips[t, plane + w * 8 + own_z, half * 64 + 32 + xx * 8 + w] = 1
        for xp in range(2):
            for w in range(8):
                ends[t, xp * 64 + far_y * 8 + w, xp * 8 + w] = 1
                ends[t, 128 + xp * 64 + w * 8 + far_z, 32 + xp * 8 + w] = 1
                ends[t, 256 + xp * 64 + far_y * 8 + w, 64 + xp * 8 + w] = 1
        out_y, out_z = (-1 if q else 8), (-1 if r else 8)
        for b in range(3):
            for c in range(3):
                if b == 1 and c == 1:
                    continue
                column = SIDES.index(b * 3 + c)
                for xp in range(2):
                    for y in range(8):
                        for z in range(8):
                            yy, zz = y + b - 1, z + c - 1
                            in_y, in_z = 0 <= yy < 8, 0 <= zz < 8
                            if in_y and in_z:
                                k = xp * 64 + yy * 8 + zz
                            elif in_z and yy == out_y:
                                k = 128 + xp * 8 + zz
                            elif in_y and zz == out_z:
                                k = 160 + xp * 8 + yy
                            elif yy == out_y and zz == out_z:
                                k = 192 + xp * 8 + far_z
                            else:
                                continue
                            shifts[t, k, column * TILE + xp * 64 + y * 8 + z] = 1
    return strips, spread, ends, shifts, fold


def left_half(shape):
    return lax.broadcasted_iota(jnp.int32, shape, len(shape) - 1) % TILE < 64


def join_halves(left, right):
    mixed = jnp.where(left_half(left.shape), left.astype(F32), right.astype(F32))
    return mixed.astype(left.dtype)


def dot(a, b):
    return jnp.dot(a, b, preferred_element_type=F32)


def count_own(slot_ref):
    total = jnp.int32(0)
    for s in range(slot_ref.shape[0]):
        total = total + (slot_ref[s] >= 0).astype(jnp.int32)
    return total


def count_sent(head):
    return jnp.max(head.astype(F32)).astype(jnp.int32)


def kind_of(brick):
    return jnp.maximum(brick, 0) & 3


def pack_bricks(slot_ref, field_ref, strips_ref, msg_ref):
    slots = field_ref.shape[0]
    for s in range(slots):
        table = strips_ref[kind_of(slot_ref[s])]
        row = s * 2 * CH
        msg_ref[row : row + CH, :] = dot(field_ref[s], table).astype(BF)
        msg_ref[row + CH : row + 2 * CH, :] = join_halves(
            field_ref[s, :, 0:TILE], field_ref[s, :, 3 * TILE : 4 * TILE]
        )
    row = slots * 2 * CH
    count = count_own(slot_ref).astype(F32)
    msg_ref[row : row + HEAD, :] = jnp.full((HEAD, TILE), count, F32).astype(BF)


def bring(pairs, sems):
    copies = [pltpu.make_async_copy(a, b, sems.at[i]) for i, (a, b) in enumerate(pairs)]
    for copy in copies:
        copy.start()
    return copies


def pack_kernel(slot_hbm, field_hbm, strips_hbm, msg_ref, field_ref, strips_ref, slot_ref, sems):
    pairs = ((slot_hbm, slot_ref), (field_hbm, field_ref), (strips_hbm, strips_ref))
    for copy in bring(pairs, sems):
        copy.wait()
    pack_bricks(slot_ref, field_ref, strips_ref, msg_ref)


def route_body(slots, own_ref, mate_ref, near_ref, far_ref, box):
    odd = (lax.axis_index("bricks") & 1) == 1
    head = slots * 2 * CH
    mine = count_sent(own_ref[head : head + HEAD, :])
    other = count_sent(mate_ref[head : head + HEAD, :])
    for s in range(2 * slots):
        box[s] = own_ref[s * CH : (s + 1) * CH, :]
        box[2 * slots + s] = mate_ref[s * CH : (s + 1) * CH, :]

    def place(j):
        up = jnp.where(j < mine, mine - 1 - j, slots + other - 1 - (j - mine))
        down = jnp.where(j < mine, j, slots + j - mine)
        return jnp.clip(jnp.where(odd, up, down), 0, 2 * slots - 1)

    half = lax.broadcasted_iota(jnp.int32, (CH, TILE), 1) // 64
    counts_here = half == odd.astype(jnp.int32)
    for j in range(0, NEAR, 2):
        first, second = [box[2 * place(j + e) + 1].astype(F32) for e in range(2)]
        both = jnp.where(counts_here, first, pltpu.roll(second, 64, 1)).astype(BF)
        near_ref[j // 2 * CH : (j // 2 + 1) * CH, :] = both
        if j < FAR:
            far_ref[j // 2 * CH : (j // 2 + 1) * CH, :] = both
    for j in range(EDGE):
        row = (NEAR // 2 + j) * CH
        near_ref[row : row + CH, :] = box[2 * place(j)]
    row = (NEAR // 2 + EDGE) * CH
    both = (mine + other).astype(F32)
    near_ref[row : row + HEAD, :] = jnp.full((HEAD, TILE), both, F32).astype(BF)


def route_kernel(slots, own_ref, mate_ref, near_ref, far_ref, box):
    route_body(slots, own_ref, mate_ref, near_ref, far_ref, box)


def route_sum_kernel(slots, own_ref, mate_ref, near_ref, far_ref, sum_ref, box):
    route_body(slots, own_ref, mate_ref, near_ref, far_ref, box)
    high = slots * 2 * CH + HEAD
    low = high + SUM_ROWS
    parts = []
    for ref in (own_ref, mate_ref):
        parts.append(
            ref[high : high + SUM_ROWS, :].astype(F32) + ref[low : low + SUM_ROWS, :].astype(F32)
        )
    total = parts[0] + parts[1]
    rounded = total.astype(BF)
    rest = (total - rounded.astype(F32)).astype(BF)
    near_ref[NEAR_ROWS : NEAR_ROWS + SUM_ROWS, :] = rounded
    near_ref[NEAR_ROWS + SUM_ROWS :, :] = rest
    sum_ref[...] = rounded.astype(F32) + rest.astype(F32)


def join_kernel(sum_ref, first_ref, second_ref, out_ref):
    device = lax.axis_index("bricks")
    itself = (device & 1) != ((device >> 1) & 1)
    high = slice(NEAR_ROWS, NEAR_ROWS + SUM_ROWS)
    low = slice(NEAR_ROWS + SUM_ROWS, NEAR_ROWS + 2 * SUM_ROWS)
    parts = [ref[high, :].astype(F32) + ref[low, :].astype(F32) for ref in (first_ref, second_ref)]
    out_ref[...] = sum_ref[...] + jnp.where(itself, parts[0], parts[1])


def weight_kernel(taps_ref, forward_ref, backward_ref, work):
    values = taps_ref[...].astype(F32)
    lanes = lax.broadcasted_iota(jnp.int32, (GC, CH), 1) // GC

    def block(tap, part):
        tile = values[tap * GC : (tap + 1) * GC, :]
        groups = (2 * part, 2 * part + 1)
        return jnp.concatenate([jnp.where(lanes == g, tile, 0.0) for g in groups], axis=0)

    work[...] = jnp.zeros_like(work)
    for part in range(PARTS):
        out = slice(part * PART, (part + 1) * PART)
        for bc in range(9):
            for a in range(3):
                work[bc * PART : (bc + 1) * PART, a * TILE : a * TILE + CH] = block(a * 9 + bc, part)
        for a in range(3):
            turned = work[:, a * TILE : (a + 1) * TILE].T
            forward_ref[part, a * PART : (a + 1) * PART, :] = turned[out, 0 : 9 * PART].astype(BF)
    for part in range(PARTS):
        out = slice(part * PART, (part + 1) * PART)
        for a in range(3):
            blocks = [block((2 - a) * 9 + 8 - bc, part)[:, out] for bc in range(9)]
            backward_ref[part, a * PART : (a + 1) * PART, :] = jnp.concatenate(blocks, axis=1).astype(BF)


def make_finder(
    slot_hbm, link_hbm, own_ref, mate_ref, first_ref, second_ref, first_far_ref, second_far_ref,
    planes, strips, slot_ref, link_ref, sems,
):
    copies = bring(((slot_hbm, slot_ref), (link_hbm, link_ref)), sems)
    slots = slot_ref.shape[0]
    odd = (lax.axis_index("bricks") & 1) == 1
    head = slots * 2 * CH
    mine = count_sent(own_ref[head : head + HEAD, :])
    other = count_sent(mate_ref[head : head + HEAD, :])
    row = (NEAR // 2 + EDGE) * CH
    counts = [count_sent(ref[row : row + HEAD, :]) for ref in (first_ref, second_ref)]
    for k, ref in enumerate((own_ref, mate_ref)):
        for s in range(slots):
            strips[k * slots + s] = ref[s * 2 * CH : s * 2 * CH + CH, :]
            planes[k * slots + s] = ref[s * 2 * CH + CH : (s + 1) * 2 * CH, :]
    for side, (near, far) in enumerate(((first_ref, first_far_ref), (second_ref, second_far_ref))):
        for start, ref, count in ((side * NEAR, near, NEAR), (2 * NEAR + side * FAR, far, FAR)):
            for j in range(0, count, 2):
                tile = ref[j // 2 * CH : (j // 2 + 1) * CH, :]
                planes[2 * slots + start + j] = tile
                planes[2 * slots + start + j + 1] = pltpu.roll(tile.astype(F32), 64, 1).astype(BF)
        for j in range(EDGE):
            row = (NEAR // 2 + j) * CH
            strips[2 * slots + side * EDGE + j] = near[row : row + CH, :]
    nothing = 2 * slots + 2 * NEAR + 2 * FAR
    planes[nothing] = jnp.zeros((CH, TILE), BF)
    for copy in copies:
        copy.wait()
    base = slot_ref[0]
    low_side = odd.astype(jnp.int32)
    high_side = 1 - low_side
    low_count = jnp.where(odd, counts[1], counts[0])
    high_count = jnp.where(odd, counts[0], counts[1])
    mate_first = jnp.where(odd, base - other, base + mine)
    chip_low = jnp.where(odd, base - other, base)
    chip_high = jnp.where(odd, base + mine, base + mine + other)

    def on_chip(brick):
        own = (brick >= base) & (brick < base + mine)
        return jnp.where(own, brick - base, slots + brick - mate_first)

    def find_strip(brick):
        low = 2 * slots + low_side * EDGE + (chip_low - 1 - brick)
        high = 2 * slots + high_side * EDGE + (brick - chip_high)
        at = jnp.where(brick < chip_low, low, jnp.where(brick >= chip_high, high, on_chip(brick)))
        return jnp.clip(at, 0, 2 * slots + 2 * EDGE - 1)

    def outside(distance, count, side):
        near = 2 * slots + side * NEAR + distance
        far = 2 * slots + 2 * NEAR + side * FAR + distance - count
        return jnp.where(distance < count, near, far)

    def find_plane(brick, exists):
        low = outside(chip_low - 1 - brick, low_count, low_side)
        high = outside(brick - chip_high, high_count, high_side)
        at = jnp.where(brick < chip_low, low, jnp.where(brick >= chip_high, high, on_chip(brick)))
        return jnp.clip(jnp.where(exists, at, nothing), 0, nothing)

    return base, mine, find_strip, find_plane


def convolve_pair(
    pair, base, find_strip, find_plane, link_ref, field_ref, planes, strips,
    spread_ref, ends_ref, shifts_ref, weight_ref, mixed, taps, sums,
):
    slots = (2 * pair, 2 * pair + 1)
    kinds, outers, besides = [], [], []
    of_y = lax.broadcasted_iota(jnp.int32, (CH, TILE), 1) % 64 < 32
    for s in slots:
        brick = base + s
        kind = brick & 3
        step_y = 2 - 2 * (kind & 2)
        step_z = 1 - 2 * (kind & 1)
        sides = (brick + step_y, brick + step_z, brick + step_y + step_z)
        has_low = link_ref[s, 0] >= 0
        has_high = link_ref[s, 1] >= 0

        def outer(near):
            high = planes[find_plane(near + 4, has_high)]
            low = planes[find_plane(near - 4, has_low)]
            return join_halves(high, low)

        beside_y, beside_z, beside_yz = [strips[find_strip(m)] for m in sides]
        beside = jnp.where(of_y, beside_y.astype(F32), beside_z.astype(F32)).astype(BF)
        besides.append(jnp.concatenate([beside, beside_yz], axis=1))
        kinds.append(kind)
        outers.append((outer(brick), jnp.concatenate([outer(m) for m in sides], axis=1)))
    halos = dot(jnp.concatenate(besides, axis=0), spread_ref[...]).astype(BF)
    for e, s in enumerate(slots):
        for i in range(4):
            rows = slice(i * CH, (i + 1) * CH)
            mixed[e, rows, 0:TILE] = field_ref[s, :, i * TILE : (i + 1) * TILE]
            mixed[e, rows, TILE:] = halos[e * CH : (e + 1) * CH, i * TILE : (i + 1) * TILE]
        mixed[e, 4 * CH :, 0:TILE] = outers[e][0]
        mixed[e, 4 * CH :, TILE:] = dot(outers[e][1], ends_ref[kinds[e]]).astype(BF)

    def put_taps(e, bc, values):
        for i in range(5):
            lanes = slice((5 * e + i) * TILE, (5 * e + i + 1) * TILE)
            for p in range(PARTS):
                taps[p, bc * PART : (bc + 1) * PART, lanes] = values[
                    i * CH + p * PART : i * CH + (p + 1) * PART, :
                ]

    for e in range(2):
        for k in range(0, 8, 2):
            part = dot(mixed[e], shifts_ref[kinds[e], :, k * TILE : (k + 2) * TILE]).astype(BF)
            put_taps(e, SIDES[k], part[:, 0:TILE])
            put_taps(e, SIDES[k + 1], part[:, TILE:])
        put_taps(e, 4, mixed[e, :, 0:TILE])
    for p in range(PARTS):
        part = dot(weight_ref[p], taps[p, 0 : 9 * PART, :])
        for a in range(3):
            at = a * CH + p * PART
            sums[at : at + PART, :] = part[a * PART : (a + 1) * PART, :]
    left = left_half((CH, TILE))
    results = []
    for e in range(2):
        first = 5 * e
        turned = []
        for a in (0, 2):
            rows = slice(a * CH, (a + 1) * CH)
            turned.append(
                [
                    pltpu.roll(sums[rows, (first + i) * TILE : (first + i + 1) * TILE], 64, 1)
                    for i in range(5)
                ]
            )
        tiles = []
        for i in range(4):
            lower = jnp.where(left, turned[0][(i - 1) % 5], turned[0][i])
            upper = jnp.where(left, turned[1][i], turned[1][i + 1])
            lanes = slice((first + i) * TILE, (first + i + 1) * TILE)
            tiles.append(sums[CH : 2 * CH, lanes] + lower + upper)
        results.append(tiles)
    return results


def forward_kernel(
    slot_hbm, link_hbm, field_ref, own_ref, mate_ref, first_ref, second_ref, first_far_ref,
    second_far_ref, weight_ref, bias_ref, cortex_ref, upstream_ref, strips_ref, spread_ref,
    ends_ref, shifts_ref, fold_ref, out_ref, dpre_ref, msg_ref,
    planes, strips, mixed, taps, sums, slot_ref, link_ref, sems, spots, grads,
):
    slots = field_ref.shape[0]
    base, mine, find_strip, find_plane = make_finder(
        slot_hbm, link_hbm, own_ref, mate_ref, first_ref, second_ref, first_far_ref, second_far_ref,
        planes, strips, slot_ref, link_ref, sems,
    )
    for pair in range(slots // 2):
        taps[pair, :, 9 * PART :, :] = jnp.ones((PARTS, PART, 10 * TILE), BF)

    square = (CH, CH)
    diagonal = lax.broadcasted_iota(jnp.int32, square, 0) == lax.broadcasted_iota(jnp.int32, square, 1)
    bias = jnp.sum(jnp.where(diagonal, bias_ref[...], 0.0), axis=1, keepdims=True)
    left = left_half((CH, TILE))
    zero = jnp.zeros((CH, TILE), F32)

    def put_spots(pair, a, i, values):
        for p in range(PARTS):
            spots[pair, p, a * PART : (a + 1) * PART, i * TILE : (i + 1) * TILE] = values[
                p * PART : (p + 1) * PART, :
            ]

    for pair in range(slots // 2):
        results = convolve_pair(
            pair, base, find_strip, find_plane, link_ref, field_ref, planes, strips,
            spread_ref, ends_ref, shifts_ref, weight_ref, mixed.at[pair], taps.at[pair], sums.at[pair],
        )
        for e, tiles in enumerate(results):
            s = 2 * pair + e
            present = jnp.where(s < mine, 1.0, 0.0)
            turned = []
            for i in range(4):
                lanes = slice(i * TILE, (i + 1) * TILE)
                pre = tiles[i] + bias
                keep = cortex_ref[s : s + 1, lanes].astype(F32) * present
                sigma = 1.0 / (1.0 + jnp.exp(-pre))
                out_ref[s, :, lanes] = (pre * sigma * keep).astype(BF)
                slope = sigma * (1.0 + pre * (1.0 - sigma))
                dpre = (upstream_ref[s, :, lanes].astype(F32) * keep * slope).astype(BF)
                dpre_ref[s, :, lanes] = dpre
                put_spots(pair, 1, 5 * e + i, dpre)
                turned.append(pltpu.roll(dpre.astype(F32), 64, 1))
            put_spots(pair, 1, 5 * e + 4, zero.astype(BF))
            turned.append(zero)
            for i in range(4):
                here = jnp.where(left, turned[i], turned[i + 1])
                put_spots(pair, 0, 5 * e + i, here.astype(BF))
                here = jnp.where(left, turned[i - 1] if i else zero, turned[i])
                put_spots(pair, 2, 5 * e + i, here.astype(BF))
            put_spots(pair, 0, 5 * e + 4, jnp.where(left, 0.0, turned[0]).astype(BF))
            put_spots(pair, 2, 5 * e + 4, jnp.where(left, turned[3], 0.0).astype(BF))
        for p in range(PARTS):
            term = lax.dot_general(
                spots[pair, p], taps[pair, p], (((1,), (1,)), ((), ())), preferred_element_type=F32
            )
            grads[p] = grads[p] + term if pair else term

    pack_bricks(slot_ref, dpre_ref, strips_ref, msg_ref)
    high = slots * 2 * CH + HEAD
    low = high + SUM_ROWS
    rows = jnp.concatenate(
        [grads[p, a * PART : (a + 1) * PART, :] for a in range(3) for p in range(PARTS)], axis=0
    )
    group = lax.broadcasted_iota(jnp.int32, rows.shape, 0) // GC % 2
    column = lax.broadcasted_iota(jnp.int32, rows.shape, 1)
    same = (column // GC % 2 == group) | (column >= 9 * PART)
    full = jnp.dot(
        jnp.where(same, rows, 0.0), fold_ref[...],
        precision=lax.Precision.HIGHEST, preferred_element_type=F32,
    ).T
    last = jnp.concatenate([full[:, TILE:], jnp.zeros((2 * GC, CH), F32)], axis=0)
    half = SUM_ROWS - 10 * GC
    last = jnp.concatenate([last[0:half], last[half:]], axis=1)
    for at, values in ((0, full[:, 0:TILE]), (10 * GC, last)):
        rounded = values.astype(BF)
        size = values.shape[0]
        msg_ref[high + at : high + at + size, :] = rounded
        msg_ref[low + at : low + at + size, :] = (values - rounded.astype(F32)).astype(BF)


def backward_kernel(pairs, *refs):
    if pairs[0] == 0:
        backward_body(pairs, *refs)
        return
    last_ref, out_ref = refs[13], refs[14]
    for s in range(2 * pairs[0]):
        out_ref[s] = last_ref[s]
    backward_body(pairs, *refs[:13], *refs[14:])


def backward_body(
    pairs, slot_hbm, link_hbm, field_ref, own_ref, mate_ref, first_ref, second_ref, first_far_ref,
    second_far_ref, weight_ref, spread_ref, ends_ref, shifts_ref, out_ref,
    planes, strips, mixed, taps, sums, slot_ref, link_ref, sems,
):
    base, mine, find_strip, find_plane = make_finder(
        slot_hbm, link_hbm, own_ref, mate_ref, first_ref, second_ref, first_far_ref, second_far_ref,
        planes, strips, slot_ref, link_ref, sems,
    )
    for pair in pairs:
        results = convolve_pair(
            pair, base, find_strip, find_plane, link_ref, field_ref, planes, strips,
            spread_ref, ends_ref, shifts_ref, weight_ref, mixed.at[pair], taps.at[pair], sums.at[pair],
        )
        for e, tiles in enumerate(results):
            s = 2 * pair + e
            present = jnp.where(s < mine, 1.0, 0.0)
            for i in range(4):
                out_ref[s, :, i * TILE : (i + 1) * TILE] = (tiles[i] * present).astype(BF)


def finish_kernel(a_ref, b_ref, kernel_ref, bias_ref):
    total = a_ref[...] + b_ref[...]
    first, last = total[0 : 10 * GC, :], total[10 * GC :, :]
    turned = pltpu.roll(first, 64, 1)
    parts = (first, turned, jnp.concatenate([last, pltpu.roll(last, 64, 1)], axis=0))
    for a, part in enumerate(parts):
        kernel_ref[a * 9 * GC : (a + 1) * 9 * GC, :] = part[0 : 9 * GC, 0:CH]
    bias_ref[...] = turned[9 * GC : 9 * GC + 1, 0:CH]


VMEM = pl.BlockSpec(memory_space=pltpu.VMEM)
HBM = pl.BlockSpec(memory_space=pltpu.HBM)


def call(kernel, ins, outs, scratch=(), flops=0, size=400000, limit=24):
    return pl.pallas_call(
        kernel,
        in_specs=ins,
        out_specs=tuple(VMEM for _ in outs),
        out_shape=tuple(outs),
        scratch_shapes=list(scratch),
        compiler_params=pltpu.CompilerParams(vmem_limit_bytes=limit * 2**20),
        cost_estimate=pl.CostEstimate(flops=flops, bytes_accessed=size, transcendentals=0),
    )


def sent(block, route):
    return lax.ppermute(block, "bricks", route)


def shards(voxels, kernel, bias, cortex, slot_to_brick, neighbors, cotangent):
    slots = voxels.shape[0]
    devices = lax.axis_size("bricks")
    strips, spread, ends, shifts, fold = (jnp.asarray(t, BF) for t in tables())
    fold = fold.astype(F32)
    shape = jax.ShapeDtypeStruct
    pack_rows = slots * 2 * CH + HEAD
    near_shape = shape((NEAR_ROWS, TILE), BF)
    near_sum_shape = shape((NEAR_ROWS + 2 * SUM_ROWS, TILE), BF)
    far_shape = shape((FAR // 2 * CH, TILE), BF)

    def routed(block, chips):
        pairs = []
        for d in range(devices):
            to = d + 2 * chips - 1 if d % 2 else d - 2 * chips + 1
            if 0 <= to < devices:
                pairs.append((d, to))
        return sent(block, pairs)

    def swapped(block, mask):
        return sent(block, [(d, d ^ mask) for d in range(devices)])

    box = [pltpu.VMEM((4 * slots, CH, TILE), BF)]
    work = [
        pltpu.VMEM((2 * slots + 2 * NEAR + 2 * FAR + 1, CH, TILE), BF),
        pltpu.VMEM((2 * slots + 2 * EDGE, CH, TILE), BF),
        pltpu.VMEM((slots // 2, 2, 5 * CH, 2 * TILE), BF),
        pltpu.VMEM((slots // 2, PARTS, 10 * PART, 10 * TILE), BF),
        pltpu.VMEM((slots // 2, 3 * CH, 10 * TILE), F32),
        pltpu.SMEM(slot_to_brick.shape, jnp.int32),
        pltpu.SMEM(neighbors.shape, jnp.int32),
        pltpu.SemaphoreType.DMA((2,)),
    ]
    field = shape(voxels.shape, BF)

    (own,) = call(
        pack_kernel,
        [HBM] * 3,
        [shape((pack_rows, TILE), BF)],
        [pltpu.VMEM(voxels.shape, BF), pltpu.VMEM(strips.shape, BF), pltpu.SMEM(slot_to_brick.shape, jnp.int32), pltpu.SemaphoreType.DMA((3,))],
        limit=60,
    )(slot_to_brick, voxels, strips)
    mate = swapped(own, 1)
    weight_shape = shape((PARTS, 3 * PART, 9 * PART), BF)
    taps = jnp.transpose(kernel, (2, 3, 4, 1, 0)).reshape(27 * GC, CH)
    staged = call(
        weight_kernel, [VMEM], [weight_shape] * 2, [pltpu.VMEM((2 * TILE, 3 * TILE), F32)], flops=BUSY
    )(taps)
    near, far = call(
        functools.partial(route_kernel, slots), [VMEM, VMEM], [near_shape, far_shape], box,
        flops=BUSY,
    )(own, mate)
    far, near = routed(far, 2), routed(near, 1)
    near, far, staged = lax.optimization_barrier((near, far, staged))
    forward, backward = staged
    received = (near, swapped(near, 1), far, swapped(far, 1))
    activated, dpre, own = call(
        forward_kernel,
        [HBM, HBM] + [VMEM] * 16,
        [field, field, shape((pack_rows + 2 * SUM_ROWS, TILE), BF)],
        work
        + [
            pltpu.VMEM((slots // 2, PARTS, 3 * PART, 10 * TILE), BF),
            pltpu.VMEM((PARTS, 3 * PART, 10 * PART), F32),
        ],
        flops=4 * 10**9,
    )(
        slot_to_brick, neighbors, voxels, own, mate, *received, forward, bias.reshape(1, CH),
        cortex, cotangent, strips, spread, ends, shifts, fold,
    )
    mate = swapped(own, 1)
    near, far, total = call(
        functools.partial(route_sum_kernel, slots),
        [VMEM, VMEM],
        [near_sum_shape, far_shape, shape((SUM_ROWS, TILE), F32)],
        box,
    )(own, mate)
    near = routed(near, 1)
    second = swapped(near, 1)
    (total,) = call(join_kernel, [VMEM] * 3, [shape((SUM_ROWS, TILE), F32)])(total, near, second)
    state = {}

    def part_backward(pair):
        last = [state["grad"]] if pair else []
        (state["grad"],) = call(
            functools.partial(backward_kernel, (pair,)),
            [HBM, HBM] + [VMEM] * (11 + len(last)),
            [field],
            work,
            flops=10**9,
        )(
            slot_to_brick, neighbors, dpre, own, mate, near, second, far, second_far,
            backward, spread, ends, shifts, *last,
        )

    pairs = list(range(slots // 2))
    masks = [2**p for p in range(2, devices.bit_length() - 1)]
    for at, mask in enumerate(masks):
        other = swapped(total, mask)
        if at == 0:
            far, total = lax.optimization_barrier((far, total))
            far = routed(far, 2)
        elif pairs:
            if at == 1:
                second_far = swapped(far, 1)
            part_backward(pairs.pop(0))
        if mask != masks[-1]:
            total, other, state = lax.optimization_barrier((total, other, state))
            total = total + other
            if at == 0:
                far, total = lax.optimization_barrier((far, total))
    for pair in pairs:
        part_backward(pair)
    input_grad = state["grad"]
    kernel_sum, bias_sum = call(
        finish_kernel, [VMEM, VMEM], [shape((27 * GC, CH), F32), shape((1, CH), F32)]
    )(total, other)
    kernel_grad = jnp.transpose(kernel_sum.reshape(3, 3, 3, GC, CH), (4, 3, 0, 1, 2))
    return (activated, input_grad, kernel_grad, bias_sum.reshape(CH))


def solution(mesh):
    devices = mesh.shape["bricks"]
    assert devices & (devices - 1) == 0
    return jax.shard_map(
        shards,
        mesh=mesh,
        in_specs=(
            P("bricks", None, None),
            P(),
            P(),
            P("bricks", None),
            P("bricks"),
            P("bricks", None),
            P("bricks", None, None),
        ),
        out_specs=(P("bricks", None, None), P("bricks", None, None), P(), P()),
        check_vma=False,
    )
```

```python
import functools

import jax
import jax.numpy as jnp
import numpy as np
from jax import lax
from jax.experimental import pallas as pl
from jax.experimental.pallas import tpu as pltpu
from jax.sharding import PartitionSpec as P

CH = 64
GC = 8
PART = 16
PARTS = CH // PART
SIDES = (0, 1, 2, 3, 5, 6, 7, 8)
TILE = 128
NEAR = 8
FAR = 4
EDGE = 3
BUSY = 10**10
HEAD = 16
NEAR_ROWS = (NEAR // 2 + 2) * CH + HEAD
SUM_ROWS = 128
BF = jnp.bfloat16
F32 = jnp.float32


@functools.cache
def tables():
    strips = np.zeros((4, 512, TILE), np.float32)
    spread = np.zeros((256, 4 * TILE), np.float32)
    ends = np.zeros((4, 384, TILE), np.float32)
    shifts = np.zeros((4, 256, 8 * TILE), np.float32)
    fold = np.zeros((10 * PART, 10 * GC), np.float32)
    for bc in range(9):
        for i in range(PART):
            fold[bc * PART + i, bc * GC + i % GC] = 1
    fold[9 * PART, 9 * GC] = 1
    for half in range(2):
        for xx in range(4):
            for w in range(8):
                i, xp = 2 * half + xx // 2, xx % 2
                spread[half * 64 + xx * 8 + w, i * TILE + xp * 8 + w] = 1
                spread[half * 64 + 32 + xx * 8 + w, i * TILE + 32 + xp * 8 + w] = 1
                spread[128 + half * 64 + xx * 8 + w, i * TILE + 64 + xp * 8 + w] = 1
    for t in range(4):
        q, r = t // 2, t % 2
        own_y, own_z = (0 if q else 7), (0 if r else 7)
        far_y, far_z = 7 - own_y, 7 - own_z
        for half in range(2):
            for xx in range(4):
                for w in range(8):
                    plane = (4 * half + xx) * 64
                    strips[t, plane + own_y * 8 + w, half * 64 + xx * 8 + w] = 1
                    strips[t, plane + w * 8 + own_z, half * 64 + 32 + xx * 8 + w] = 1
        for xp in range(2):
            for w in range(8):
                ends[t, xp * 64 + far_y * 8 + w, xp * 8 + w] = 1
                ends[t, 128 + xp * 64 + w * 8 + far_z, 32 + xp * 8 + w] = 1
                ends[t, 256 + xp * 64 + far_y * 8 + w, 64 + xp * 8 + w] = 1
        out_y, out_z = (-1 if q else 8), (-1 if r else 8)
        for b in range(3):
            for c in range(3):
                if b == 1 and c == 1:
                    continue
                column = SIDES.index(b * 3 + c)
                for xp in range(2):
                    for y in range(8):
                        for z in range(8):
                            yy, zz = y + b - 1, z + c - 1
                            in_y, in_z = 0 <= yy < 8, 0 <= zz < 8
                            if in_y and in_z:
                                k = xp * 64 + yy * 8 + zz
                            elif in_z and yy == out_y:
                                k = 128 + xp * 8 + zz
                            elif in_y and zz == out_z:
                                k = 160 + xp * 8 + yy
                            elif yy == out_y and zz == out_z:
                                k = 192 + xp * 8 + far_z
                            else:
                                continue
                            shifts[t, k, column * TILE + xp * 64 + y * 8 + z] = 1
    return strips, spread, ends, shifts, fold


def left_half(shape):
    return lax.broadcasted_iota(jnp.int32, shape, len(shape) - 1) % TILE < 64


def join_halves(left, right):
    mixed = jnp.where(left_half(left.shape), left.astype(F32), right.astype(F32))
    return mixed.astype(left.dtype)


def dot(a, b):
    return jnp.dot(a, b, preferred_element_type=F32)


def count_own(slot_ref):
    total = jnp.int32(0)
    for s in range(slot_ref.shape[0]):
        total = total + (slot_ref[s] >= 0).astype(jnp.int32)
    return total


def count_sent(head):
    return jnp.max(head.astype(F32)).astype(jnp.int32)


def kind_of(brick):
    return jnp.maximum(brick, 0) & 3


def pack_bricks(slot_ref, field_ref, strips_ref, msg_ref):
    slots = field_ref.shape[0]
    for s in range(slots):
        table = strips_ref[kind_of(slot_ref[s])]
        row = s * 2 * CH
        msg_ref[row : row + CH, :] = dot(field_ref[s], table).astype(BF)
        msg_ref[row + CH : row + 2 * CH, :] = join_halves(
            field_ref[s, :, 0:TILE], field_ref[s, :, 3 * TILE : 4 * TILE]
        )
    row = slots * 2 * CH
    count = count_own(slot_ref).astype(F32)
    msg_ref[row : row + HEAD, :] = jnp.full((HEAD, TILE), count, F32).astype(BF)


def bring(pairs, sems):
    copies = [pltpu.make_async_copy(a, b, sems.at[i]) for i, (a, b) in enumerate(pairs)]
    for copy in copies:
        copy.start()
    return copies


def pack_kernel(slot_hbm, field_hbm, strips_hbm, msg_ref, field_ref, strips_ref, slot_ref, sems):
    pairs = ((slot_hbm, slot_ref), (field_hbm, field_ref), (strips_hbm, strips_ref))
    for copy in bring(pairs, sems):
        copy.wait()
    pack_bricks(slot_ref, field_ref, strips_ref, msg_ref)


def route_body(slots, own_ref, mate_ref, near_ref, far_ref, box):
    odd = (lax.axis_index("bricks") & 1) == 1
    head = slots * 2 * CH
    mine = count_sent(own_ref[head : head + HEAD, :])
    other = count_sent(mate_ref[head : head + HEAD, :])
    for s in range(2 * slots):
        box[s] = own_ref[s * CH : (s + 1) * CH, :]
        box[2 * slots + s] = mate_ref[s * CH : (s + 1) * CH, :]

    def place(j):
        up = jnp.where(j < mine, mine - 1 - j, slots + other - 1 - (j - mine))
        down = jnp.where(j < mine, j, slots + j - mine)
        return jnp.clip(jnp.where(odd, up, down), 0, 2 * slots - 1)

    half = lax.broadcasted_iota(jnp.int32, (CH, TILE), 1) // 64
    counts_here = half == odd.astype(jnp.int32)
    for j in range(0, NEAR, 2):
        first, second = [box[2 * place(j + e) + 1].astype(F32) for e in range(2)]
        both = jnp.where(counts_here, first, pltpu.roll(second, 64, 1)).astype(BF)
        near_ref[j // 2 * CH : (j // 2 + 1) * CH, :] = both
        if j < FAR:
            far_ref[j // 2 * CH : (j // 2 + 1) * CH, :] = both
    of_y = lax.broadcasted_iota(jnp.int32, (CH, TILE), 1) % 64 < 32
    row = NEAR // 2 * CH
    near_ref[row : row + CH, :] = box[2 * place(0)]
    first, second = [box[2 * place(j)].astype(F32) for j in (1, 2)]
    near_ref[row + CH : row + 2 * CH, :] = jnp.where(of_y, first, pltpu.roll(second, 32, 1)).astype(BF)
    row = (NEAR // 2 + 2) * CH
    both = (mine + other).astype(F32)
    near_ref[row : row + HEAD, :] = jnp.full((HEAD, TILE), both, F32).astype(BF)


def route_kernel(slots, own_ref, mate_ref, near_ref, far_ref, box):
    route_body(slots, own_ref, mate_ref, near_ref, far_ref, box)


def route_sum_kernel(slots, own_ref, mate_ref, near_ref, far_ref, sum_ref, box):
    route_body(slots, own_ref, mate_ref, near_ref, far_ref, box)
    high = slots * 2 * CH + HEAD
    low = high + SUM_ROWS
    parts = []
    for ref in (own_ref, mate_ref):
        parts.append(
            ref[high : high + SUM_ROWS, :].astype(F32) + ref[low : low + SUM_ROWS, :].astype(F32)
        )
    sum_ref[...] = parts[0] + parts[1]


def merge_kernel(near_ref, far_ref, out_ref):
    out_ref[0:NEAR_ROWS, :] = near_ref[...]
    out_ref[NEAR_ROWS:, :] = far_ref[...]


def weight_kernel(taps_ref, forward_ref, backward_ref, work):
    values = taps_ref[...].astype(F32)
    lanes = lax.broadcasted_iota(jnp.int32, (GC, CH), 1) // GC

    def block(tap, part):
        tile = values[tap * GC : (tap + 1) * GC, :]
        groups = (2 * part, 2 * part + 1)
        return jnp.concatenate([jnp.where(lanes == g, tile, 0.0) for g in groups], axis=0)

    work[...] = jnp.zeros_like(work)
    for part in range(PARTS):
        out = slice(part * PART, (part + 1) * PART)
        for bc in range(9):
            for a in range(3):
                work[bc * PART : (bc + 1) * PART, a * TILE : a * TILE + CH] = block(a * 9 + bc, part)
        for a in range(3):
            turned = work[:, a * TILE : (a + 1) * TILE].T
            forward_ref[part, a * PART : (a + 1) * PART, :] = turned[out, 0 : 9 * PART].astype(BF)
    for part in range(PARTS):
        out = slice(part * PART, (part + 1) * PART)
        for a in range(3):
            blocks = [block((2 - a) * 9 + 8 - bc, part)[:, out] for bc in range(9)]
            backward_ref[part, a * PART : (a + 1) * PART, :] = jnp.concatenate(blocks, axis=1).astype(BF)


def make_finder(
    slot_hbm, link_hbm, own_ref, mate_ref, first_ref, second_ref,
    planes, strips, slot_ref, link_ref, sems,
):
    copies = bring(((slot_hbm, slot_ref), (link_hbm, link_ref)), sems)
    slots = slot_ref.shape[0]
    odd = (lax.axis_index("bricks") & 1) == 1
    head = slots * 2 * CH
    mine = count_sent(own_ref[head : head + HEAD, :])
    other = count_sent(mate_ref[head : head + HEAD, :])
    row = (NEAR // 2 + 2) * CH
    counts = [count_sent(ref[row : row + HEAD, :]) for ref in (first_ref, second_ref)]
    for k, ref in enumerate((own_ref, mate_ref)):
        for s in range(slots):
            strips[k * slots + s] = ref[s * 2 * CH : s * 2 * CH + CH, :]
            planes[k * slots + s] = ref[s * 2 * CH + CH : (s + 1) * 2 * CH, :]
    for side, near in enumerate((first_ref, second_ref)):
        for start, begin, count in ((side * NEAR, 0, NEAR), (2 * NEAR + side * FAR, NEAR_ROWS, FAR)):
            for j in range(0, count, 2):
                row = begin + j // 2 * CH
                tile = near[row : row + CH, :]
                planes[2 * slots + start + j] = tile
                planes[2 * slots + start + j + 1] = pltpu.roll(tile.astype(F32), 64, 1).astype(BF)
        row, at = NEAR // 2 * CH, 2 * slots + side * EDGE
        strips[at] = near[row : row + CH, :]
        tile = near[row + CH : row + 2 * CH, :]
        strips[at + 1] = tile
        strips[at + 2] = pltpu.roll(tile.astype(F32), TILE - 32, 1).astype(BF)
    nothing = 2 * slots + 2 * NEAR + 2 * FAR
    planes[nothing] = jnp.zeros((CH, TILE), BF)
    for copy in copies:
        copy.wait()
    base = slot_ref[0]
    low_side = odd.astype(jnp.int32)
    high_side = 1 - low_side
    low_count = jnp.where(odd, counts[1], counts[0])
    high_count = jnp.where(odd, counts[0], counts[1])
    mate_first = jnp.where(odd, base - other, base + mine)
    chip_low = jnp.where(odd, base - other, base)
    chip_high = jnp.where(odd, base + mine, base + mine + other)

    def on_chip(brick):
        own = (brick >= base) & (brick < base + mine)
        return jnp.where(own, brick - base, slots + brick - mate_first)

    def find_strip(brick):
        low = 2 * slots + low_side * EDGE + (chip_low - 1 - brick)
        high = 2 * slots + high_side * EDGE + (brick - chip_high)
        at = jnp.where(brick < chip_low, low, jnp.where(brick >= chip_high, high, on_chip(brick)))
        return jnp.clip(at, 0, 2 * slots + 2 * EDGE - 1)

    def outside(distance, count, side):
        near = 2 * slots + side * NEAR + distance
        far = 2 * slots + 2 * NEAR + side * FAR + distance - count
        return jnp.where(distance < count, near, far)

    def find_plane(brick, exists):
        low = outside(chip_low - 1 - brick, low_count, low_side)
        high = outside(brick - chip_high, high_count, high_side)
        at = jnp.where(brick < chip_low, low, jnp.where(brick >= chip_high, high, on_chip(brick)))
        return jnp.clip(jnp.where(exists, at, nothing), 0, nothing)

    return base, mine, find_strip, find_plane


def convolve_pair(
    pair, base, find_strip, find_plane, link_ref, field_ref, planes, strips,
    spread_ref, ends_ref, shifts_ref, weight_ref, mixed, taps, sums,
):
    slots = (2 * pair, 2 * pair + 1)
    kinds, outers, besides = [], [], []
    of_y = lax.broadcasted_iota(jnp.int32, (CH, TILE), 1) % 64 < 32
    for s in slots:
        brick = base + s
        kind = brick & 3
        step_y = 2 - 2 * (kind & 2)
        step_z = 1 - 2 * (kind & 1)
        sides = (brick + step_y, brick + step_z, brick + step_y + step_z)
        has_low = link_ref[s, 0] >= 0
        has_high = link_ref[s, 1] >= 0

        def outer(near):
            high = planes[find_plane(near + 4, has_high)]
            low = planes[find_plane(near - 4, has_low)]
            return join_halves(high, low)

        beside_y, beside_z, beside_yz = [strips[find_strip(m)] for m in sides]
        beside = jnp.where(of_y, beside_y.astype(F32), beside_z.astype(F32)).astype(BF)
        besides.append(jnp.concatenate([beside, beside_yz], axis=1))
        kinds.append(kind)
        outers.append((outer(brick), jnp.concatenate([outer(m) for m in sides], axis=1)))
    halos = dot(jnp.concatenate(besides, axis=0), spread_ref[...]).astype(BF)
    for e, s in enumerate(slots):
        for i in range(4):
            rows = slice(i * CH, (i + 1) * CH)
            mixed[e, rows, 0:TILE] = field_ref[s, :, i * TILE : (i + 1) * TILE]
            mixed[e, rows, TILE:] = halos[e * CH : (e + 1) * CH, i * TILE : (i + 1) * TILE]
        mixed[e, 4 * CH :, 0:TILE] = outers[e][0]
        mixed[e, 4 * CH :, TILE:] = dot(outers[e][1], ends_ref[kinds[e]]).astype(BF)

    def put_taps(e, bc, values):
        for i in range(5):
            lanes = slice((5 * e + i) * TILE, (5 * e + i + 1) * TILE)
            for p in range(PARTS):
                taps[p, bc * PART : (bc + 1) * PART, lanes] = values[
                    i * CH + p * PART : i * CH + (p + 1) * PART, :
                ]

    for e in range(2):
        for k in range(0, 8, 2):
            part = dot(mixed[e], shifts_ref[kinds[e], :, k * TILE : (k + 2) * TILE]).astype(BF)
            put_taps(e, SIDES[k], part[:, 0:TILE])
            put_taps(e, SIDES[k + 1], part[:, TILE:])
        put_taps(e, 4, mixed[e, :, 0:TILE])
    for p in range(PARTS):
        part = dot(weight_ref[p], taps[p, 0 : 9 * PART, :])
        for a in range(3):
            at = a * CH + p * PART
            sums[at : at + PART, :] = part[a * PART : (a + 1) * PART, :]
    left = left_half((CH, TILE))
    results = []
    for e in range(2):
        first = 5 * e
        turned = []
        for a in (0, 2):
            rows = slice(a * CH, (a + 1) * CH)
            turned.append(
                [
                    pltpu.roll(sums[rows, (first + i) * TILE : (first + i + 1) * TILE], 64, 1)
                    for i in range(5)
                ]
            )
        tiles = []
        for i in range(4):
            lower = jnp.where(left, turned[0][(i - 1) % 5], turned[0][i])
            upper = jnp.where(left, turned[1][i], turned[1][i + 1])
            lanes = slice((first + i) * TILE, (first + i + 1) * TILE)
            tiles.append(sums[CH : 2 * CH, lanes] + lower + upper)
        results.append(tiles)
    return results


def forward_kernel(
    slot_hbm, link_hbm, field_ref, own_ref, mate_ref, first_ref, second_ref, weight_ref, bias_ref, cortex_ref, upstream_ref, strips_ref, spread_ref,
    ends_ref, shifts_ref, fold_ref, out_ref, dpre_ref, msg_ref,
    planes, strips, mixed, taps, sums, slot_ref, link_ref, sems, spots, grads,
):
    slots = field_ref.shape[0]
    base, mine, find_strip, find_plane = make_finder(
        slot_hbm, link_hbm, own_ref, mate_ref, first_ref, second_ref,
        planes, strips, slot_ref, link_ref, sems,
    )
    for pair in range(slots // 2):
        taps[pair, :, 9 * PART :, :] = jnp.ones((PARTS, PART, 10 * TILE), BF)

    square = (CH, CH)
    diagonal = lax.broadcasted_iota(jnp.int32, square, 0) == lax.broadcasted_iota(jnp.int32, square, 1)
    bias = jnp.sum(jnp.where(diagonal, bias_ref[...], 0.0), axis=1, keepdims=True)
    left = left_half((CH, TILE))
    zero = jnp.zeros((CH, TILE), F32)

    def put_spots(pair, a, i, values):
        for p in range(PARTS):
            spots[pair, p, a * PART : (a + 1) * PART, i * TILE : (i + 1) * TILE] = values[
                p * PART : (p + 1) * PART, :
            ]

    for pair in range(slots // 2):
        results = convolve_pair(
            pair, base, find_strip, find_plane, link_ref, field_ref, planes, strips,
            spread_ref, ends_ref, shifts_ref, weight_ref, mixed.at[pair], taps.at[pair], sums.at[pair],
        )
        for e, tiles in enumerate(results):
            s = 2 * pair + e
            present = jnp.where(s < mine, 1.0, 0.0)
            turned = []
            for i in range(4):
                lanes = slice(i * TILE, (i + 1) * TILE)
                pre = tiles[i] + bias
                keep = cortex_ref[s : s + 1, lanes].astype(F32) * present
                sigma = 1.0 / (1.0 + jnp.exp(-pre))
                out_ref[s, :, lanes] = (pre * sigma * keep).astype(BF)
                slope = sigma * (1.0 + pre * (1.0 - sigma))
                dpre = (upstream_ref[s, :, lanes].astype(F32) * keep * slope).astype(BF)
                dpre_ref[s, :, lanes] = dpre
                put_spots(pair, 1, 5 * e + i, dpre)
                turned.append(pltpu.roll(dpre.astype(F32), 64, 1))
            put_spots(pair, 1, 5 * e + 4, zero.astype(BF))
            turned.append(zero)
            for i in range(4):
                here = jnp.where(left, turned[i], turned[i + 1])
                put_spots(pair, 0, 5 * e + i, here.astype(BF))
                here = jnp.where(left, turned[i - 1] if i else zero, turned[i])
                put_spots(pair, 2, 5 * e + i, here.astype(BF))
            put_spots(pair, 0, 5 * e + 4, jnp.where(left, 0.0, turned[0]).astype(BF))
            put_spots(pair, 2, 5 * e + 4, jnp.where(left, turned[3], 0.0).astype(BF))
        for p in range(PARTS):
            term = lax.dot_general(
                spots[pair, p], taps[pair, p], (((1,), (1,)), ((), ())), preferred_element_type=F32
            )
            grads[p] = grads[p] + term if pair else term

    pack_bricks(slot_ref, dpre_ref, strips_ref, msg_ref)
    high = slots * 2 * CH + HEAD
    low = high + SUM_ROWS
    rows = jnp.concatenate(
        [grads[p, a * PART : (a + 1) * PART, :] for a in range(3) for p in range(PARTS)], axis=0
    )
    group = lax.broadcasted_iota(jnp.int32, rows.shape, 0) // GC % 2
    column = lax.broadcasted_iota(jnp.int32, rows.shape, 1)
    same = (column // GC % 2 == group) | (column >= 9 * PART)
    full = jnp.dot(
        jnp.where(same, rows, 0.0), fold_ref[...],
        precision=lax.Precision.HIGHEST, preferred_element_type=F32,
    ).T
    last = jnp.concatenate([full[:, TILE:], jnp.zeros((2 * GC, CH), F32)], axis=0)
    half = SUM_ROWS - 10 * GC
    last = jnp.concatenate([last[0:half], last[half:]], axis=1)
    for at, values in ((0, full[:, 0:TILE]), (10 * GC, last)):
        rounded = values.astype(BF)
        size = values.shape[0]
        msg_ref[high + at : high + at + size, :] = rounded
        msg_ref[low + at : low + at + size, :] = (values - rounded.astype(F32)).astype(BF)


def backward_kernel(pairs, *refs):
    if pairs[0] == 0:
        backward_body(pairs, *refs)
        return
    last_ref, out_ref = refs[11], refs[12]
    for s in range(2 * pairs[0]):
        out_ref[s] = last_ref[s]
    backward_body(pairs, *refs[:11], *refs[12:])


def backward_body(
    pairs, slot_hbm, link_hbm, field_ref, own_ref, mate_ref, first_ref, second_ref, weight_ref, spread_ref, ends_ref, shifts_ref, out_ref,
    planes, strips, mixed, taps, sums, slot_ref, link_ref, sems,
):
    base, mine, find_strip, find_plane = make_finder(
        slot_hbm, link_hbm, own_ref, mate_ref, first_ref, second_ref,
        planes, strips, slot_ref, link_ref, sems,
    )
    for pair in pairs:
        results = convolve_pair(
            pair, base, find_strip, find_plane, link_ref, field_ref, planes, strips,
            spread_ref, ends_ref, shifts_ref, weight_ref, mixed.at[pair], taps.at[pair], sums.at[pair],
        )
        for e, tiles in enumerate(results):
            s = 2 * pair + e
            present = jnp.where(s < mine, 1.0, 0.0)
            for i in range(4):
                out_ref[s, :, i * TILE : (i + 1) * TILE] = (tiles[i] * present).astype(BF)


def finish_kernel(a_ref, b_ref, kernel_ref, bias_ref):
    total = a_ref[...] + b_ref[...]
    first, last = total[0 : 10 * GC, :], total[10 * GC :, :]
    turned = pltpu.roll(first, 64, 1)
    parts = (first, turned, jnp.concatenate([last, pltpu.roll(last, 64, 1)], axis=0))
    for a, part in enumerate(parts):
        kernel_ref[a * 9 * GC : (a + 1) * 9 * GC, :] = part[0 : 9 * GC, 0:CH]
    bias_ref[...] = turned[9 * GC : 9 * GC + 1, 0:CH]


VMEM = pl.BlockSpec(memory_space=pltpu.VMEM)
HBM = pl.BlockSpec(memory_space=pltpu.HBM)


def call(kernel, ins, outs, scratch=(), flops=0, size=400000, limit=24):
    return pl.pallas_call(
        kernel,
        in_specs=ins,
        out_specs=tuple(VMEM for _ in outs),
        out_shape=tuple(outs),
        scratch_shapes=list(scratch),
        compiler_params=pltpu.CompilerParams(vmem_limit_bytes=limit * 2**20),
        cost_estimate=pl.CostEstimate(flops=flops, bytes_accessed=size, transcendentals=0),
    )


def sent(block, route):
    return lax.ppermute(block, "bricks", route)


def shards(voxels, kernel, bias, cortex, slot_to_brick, neighbors, cotangent):
    slots = voxels.shape[0]
    devices = lax.axis_size("bricks")
    strips, spread, ends, shifts, fold = (jnp.asarray(t, BF) for t in tables())
    fold = fold.astype(F32)
    shape = jax.ShapeDtypeStruct
    pack_rows = slots * 2 * CH + HEAD
    near_shape = shape((NEAR_ROWS, TILE), BF)
    far_shape = shape((FAR // 2 * CH, TILE), BF)

    def routed(block, chips):
        pairs = []
        for d in range(devices):
            to = d + 2 * chips - 1 if d % 2 else d - 2 * chips + 1
            if 0 <= to < devices:
                pairs.append((d, to))
        return sent(block, pairs)

    def swapped(block, mask):
        return sent(block, [(d, d ^ mask) for d in range(devices)])

    def merged(near, far):
        rows = near.shape[0] + far.shape[0]
        return call(merge_kernel, [VMEM] * 2, [shape((rows, TILE), BF)])(near, far)[0]

    box = [pltpu.VMEM((4 * slots, CH, TILE), BF)]
    work = [
        pltpu.VMEM((2 * slots + 2 * NEAR + 2 * FAR + 1, CH, TILE), BF),
        pltpu.VMEM((2 * slots + 2 * EDGE, CH, TILE), BF),
        pltpu.VMEM((slots // 2, 2, 5 * CH, 2 * TILE), BF),
        pltpu.VMEM((slots // 2, PARTS, 10 * PART, 10 * TILE), BF),
        pltpu.VMEM((slots // 2, 3 * CH, 10 * TILE), F32),
        pltpu.SMEM(slot_to_brick.shape, jnp.int32),
        pltpu.SMEM(neighbors.shape, jnp.int32),
        pltpu.SemaphoreType.DMA((2,)),
    ]
    field = shape(voxels.shape, BF)

    (own,) = call(
        pack_kernel,
        [HBM] * 3,
        [shape((pack_rows, TILE), BF)],
        [pltpu.VMEM(voxels.shape, BF), pltpu.VMEM(strips.shape, BF), pltpu.SMEM(slot_to_brick.shape, jnp.int32), pltpu.SemaphoreType.DMA((3,))],
        limit=60,
    )(slot_to_brick, voxels, strips)
    mate = swapped(own, 1)
    weight_shape = shape((PARTS, 3 * PART, 9 * PART), BF)
    taps = jnp.transpose(kernel, (2, 3, 4, 1, 0)).reshape(27 * GC, CH)
    staged = call(
        weight_kernel, [VMEM], [weight_shape] * 2, [pltpu.VMEM((2 * TILE, 3 * TILE), F32)], flops=BUSY
    )(taps)
    near, far = call(
        functools.partial(route_kernel, slots), [VMEM, VMEM], [near_shape, far_shape], box,
        flops=BUSY,
    )(own, mate)
    near, far = routed(near, 1), routed(far, 2)
    near, far, staged = lax.optimization_barrier((near, far, staged))
    forward, backward = staged
    first = merged(near, far)
    second = swapped(first, 1)
    activated, dpre, own = call(
        forward_kernel,
        [HBM, HBM] + [VMEM] * 14,
        [field, field, shape((pack_rows + 2 * SUM_ROWS, TILE), BF)],
        work
        + [
            pltpu.VMEM((slots // 2, PARTS, 3 * PART, 10 * TILE), BF),
            pltpu.VMEM((PARTS, 3 * PART, 10 * PART), F32),
        ],
        flops=4 * 10**9,
    )(
        slot_to_brick, neighbors, voxels, own, mate, first, second, forward, bias.reshape(1, CH),
        cortex, cotangent, strips, spread, ends, shifts, fold,
    )
    mate = swapped(own, 1)
    near, far, total = call(
        functools.partial(route_sum_kernel, slots),
        [VMEM, VMEM],
        [near_shape, far_shape, shape((SUM_ROWS, TILE), F32)],
        box,
    )(own, mate)
    state = {}

    def part_backward(pair):
        last = [state["grad"]] if pair else []
        (state["grad"],) = call(
            functools.partial(backward_kernel, (pair,)),
            [HBM, HBM] + [VMEM] * (9 + len(last)),
            [field],
            work,
            flops=10**9,
        )(
            slot_to_brick, neighbors, dpre, own, mate, state["first"], state["second"], backward,
            spread, ends, shifts, *last,
        )

    pairs = list(range(slots // 2))
    masks = [2**p for p in range(1, devices.bit_length() - 1)]
    for mask in masks:
        other = swapped(total, mask)
        if mask == masks[0]:
            state["near"], state["far"] = routed(near, 1), routed(far, 2)
        elif pairs:
            if mask == masks[1]:
                state["first"] = merged(state.pop("near"), state.pop("far"))
                state["second"] = swapped(state["first"], 1)
            part_backward(pairs.pop(0))
        if mask != masks[-1]:
            total, other, state = lax.optimization_barrier((total, other, state))
            total = total + other
    for pair in pairs:
        part_backward(pair)
    input_grad = state["grad"]
    kernel_sum, bias_sum = call(
        finish_kernel, [VMEM, VMEM], [shape((27 * GC, CH), F32), shape((1, CH), F32)]
    )(total, other)
    kernel_grad = jnp.transpose(kernel_sum.reshape(3, 3, 3, GC, CH), (4, 3, 0, 1, 2))
    return (activated, input_grad, kernel_grad, bias_sum.reshape(CH))


def solution(mesh):
    devices = mesh.shape["bricks"]
    assert devices & (devices - 1) == 0
    return jax.shard_map(
        shards,
        mesh=mesh,
        in_specs=(
            P("bricks", None, None),
            P(),
            P(),
            P("bricks", None),
            P("bricks"),
            P("bricks", None),
            P("bricks", None, None),
        ),
        out_specs=(P("bricks", None, None), P("bricks", None, None), P(), P()),
        check_vma=False,
    )
```

```python
import functools

import jax
import jax.numpy as jnp
import numpy as np
from jax import lax
from jax.experimental import pallas as pl
from jax.experimental.pallas import tpu as pltpu
from jax.sharding import PartitionSpec as P

CH = 64
GC = 8
PART = 16
PARTS = CH // PART
SIDES = (0, 1, 2, 3, 5, 6, 7, 8)
TILE = 128
NEAR = 8
FAR = 4
EDGE = 3
BUSY = 10**10
HEAD = 16
NEAR_ROWS = (NEAR // 2 + 2) * CH + HEAD
SUM_ROWS = 128
BF = jnp.bfloat16
F32 = jnp.float32


@functools.cache
def tables():
    strips = np.zeros((4, 512, TILE), np.float32)
    spread = np.zeros((256, 4 * TILE), np.float32)
    ends = np.zeros((4, 384, TILE), np.float32)
    shifts = np.zeros((4, 256, 8 * TILE), np.float32)
    fold = np.zeros((10 * PART, 10 * GC), np.float32)
    for bc in range(9):
        for i in range(PART):
            fold[bc * PART + i, bc * GC + i % GC] = 1
    fold[9 * PART, 9 * GC] = 1
    for half in range(2):
        for xx in range(4):
            for w in range(8):
                i, xp = 2 * half + xx // 2, xx % 2
                spread[half * 64 + xx * 8 + w, i * TILE + xp * 8 + w] = 1
                spread[half * 64 + 32 + xx * 8 + w, i * TILE + 32 + xp * 8 + w] = 1
                spread[128 + half * 64 + xx * 8 + w, i * TILE + 64 + xp * 8 + w] = 1
    for t in range(4):
        q, r = t // 2, t % 2
        own_y, own_z = (0 if q else 7), (0 if r else 7)
        far_y, far_z = 7 - own_y, 7 - own_z
        for half in range(2):
            for xx in range(4):
                for w in range(8):
                    plane = (4 * half + xx) * 64
                    strips[t, plane + own_y * 8 + w, half * 64 + xx * 8 + w] = 1
                    strips[t, plane + w * 8 + own_z, half * 64 + 32 + xx * 8 + w] = 1
        for xp in range(2):
            for w in range(8):
                ends[t, xp * 64 + far_y * 8 + w, xp * 8 + w] = 1
                ends[t, 128 + xp * 64 + w * 8 + far_z, 32 + xp * 8 + w] = 1
                ends[t, 256 + xp * 64 + far_y * 8 + w, 64 + xp * 8 + w] = 1
        out_y, out_z = (-1 if q else 8), (-1 if r else 8)
        for b in range(3):
            for c in range(3):
                if b == 1 and c == 1:
                    continue
                column = SIDES.index(b * 3 + c)
                for xp in range(2):
                    for y in range(8):
                        for z in range(8):
                            yy, zz = y + b - 1, z + c - 1
                            in_y, in_z = 0 <= yy < 8, 0 <= zz < 8
                            if in_y and in_z:
                                k = xp * 64 + yy * 8 + zz
                            elif in_z and yy == out_y:
                                k = 128 + xp * 8 + zz
                            elif in_y and zz == out_z:
                                k = 160 + xp * 8 + yy
                            elif yy == out_y and zz == out_z:
                                k = 192 + xp * 8 + far_z
                            else:
                                continue
                            shifts[t, k, column * TILE + xp * 64 + y * 8 + z] = 1
    return strips, spread, ends, shifts, fold


def left_half(shape):
    return lax.broadcasted_iota(jnp.int32, shape, len(shape) - 1) % TILE < 64


def join_halves(left, right):
    mixed = jnp.where(left_half(left.shape), left.astype(F32), right.astype(F32))
    return mixed.astype(left.dtype)


def dot(a, b):
    return jnp.dot(a, b, preferred_element_type=F32)


def count_own(slot_ref):
    total = jnp.int32(0)
    for s in range(slot_ref.shape[0]):
        total = total + (slot_ref[s] >= 0).astype(jnp.int32)
    return total


def count_sent(head):
    return jnp.max(head.astype(F32)).astype(jnp.int32)


def kind_of(brick):
    return jnp.maximum(brick, 0) & 3


def pack_bricks(slot_ref, field_ref, strips_ref, msg_ref):
    slots = field_ref.shape[0]
    for s in range(slots):
        table = strips_ref[kind_of(slot_ref[s])]
        row = s * 2 * CH
        msg_ref[row : row + CH, :] = dot(field_ref[s], table).astype(BF)
        msg_ref[row + CH : row + 2 * CH, :] = join_halves(
            field_ref[s, :, 0:TILE], field_ref[s, :, 3 * TILE : 4 * TILE]
        )
    row = slots * 2 * CH
    count = count_own(slot_ref).astype(F32)
    msg_ref[row : row + HEAD, :] = jnp.full((HEAD, TILE), count, F32).astype(BF)


def bring(pairs, sems):
    copies = [pltpu.make_async_copy(a, b, sems.at[i]) for i, (a, b) in enumerate(pairs)]
    for copy in copies:
        copy.start()
    return copies


def pack_kernel(slot_hbm, field_hbm, strips_hbm, msg_ref, field_ref, strips_ref, slot_ref, sems):
    pairs = ((slot_hbm, slot_ref), (field_hbm, field_ref), (strips_hbm, strips_ref))
    for copy in bring(pairs, sems):
        copy.wait()
    pack_bricks(slot_ref, field_ref, strips_ref, msg_ref)


def route_body(slots, own_ref, mate_ref, near_ref, far_ref, box):
    odd = (lax.axis_index("bricks") & 1) == 1
    head = slots * 2 * CH
    mine = count_sent(own_ref[head : head + HEAD, :])
    other = count_sent(mate_ref[head : head + HEAD, :])
    for s in range(2 * slots):
        box[s] = own_ref[s * CH : (s + 1) * CH, :]
        box[2 * slots + s] = mate_ref[s * CH : (s + 1) * CH, :]

    def place(j):
        up = jnp.where(j < mine, mine - 1 - j, slots + other - 1 - (j - mine))
        down = jnp.where(j < mine, j, slots + j - mine)
        return jnp.clip(jnp.where(odd, up, down), 0, 2 * slots - 1)

    half = lax.broadcasted_iota(jnp.int32, (CH, TILE), 1) // 64
    counts_here = half == odd.astype(jnp.int32)
    for j in range(0, NEAR, 2):
        first, second = [box[2 * place(j + e) + 1].astype(F32) for e in range(2)]
        both = jnp.where(counts_here, first, pltpu.roll(second, 64, 1)).astype(BF)
        near_ref[j // 2 * CH : (j // 2 + 1) * CH, :] = both
        if j < FAR:
            far_ref[j // 2 * CH : (j // 2 + 1) * CH, :] = both
    of_y = lax.broadcasted_iota(jnp.int32, (CH, TILE), 1) % 64 < 32
    row = NEAR // 2 * CH
    near_ref[row : row + CH, :] = box[2 * place(0)]
    first, second = [box[2 * place(j)].astype(F32) for j in (1, 2)]
    near_ref[row + CH : row + 2 * CH, :] = jnp.where(of_y, first, pltpu.roll(second, 32, 1)).astype(BF)
    row = (NEAR // 2 + 2) * CH
    both = (mine + other).astype(F32)
    near_ref[row : row + HEAD, :] = jnp.full((HEAD, TILE), both, F32).astype(BF)


def route_kernel(slots, own_ref, mate_ref, near_ref, far_ref, box):
    route_body(slots, own_ref, mate_ref, near_ref, far_ref, box)


def merge_kernel(near_ref, far_ref, out_ref):
    out_ref[0:NEAR_ROWS, :] = near_ref[...]
    out_ref[NEAR_ROWS:, :] = far_ref[...]


def weight_kernel(taps_ref, forward_ref, backward_ref, work):
    values = taps_ref[...].astype(F32)
    lanes = lax.broadcasted_iota(jnp.int32, (GC, CH), 1) // GC

    def block(tap, part):
        tile = values[tap * GC : (tap + 1) * GC, :]
        groups = (2 * part, 2 * part + 1)
        return jnp.concatenate([jnp.where(lanes == g, tile, 0.0) for g in groups], axis=0)

    work[...] = jnp.zeros_like(work)
    for part in range(PARTS):
        out = slice(part * PART, (part + 1) * PART)
        for bc in range(9):
            for a in range(3):
                work[bc * PART : (bc + 1) * PART, a * TILE : a * TILE + CH] = block(a * 9 + bc, part)
        for a in range(3):
            turned = work[:, a * TILE : (a + 1) * TILE].T
            forward_ref[part, a * PART : (a + 1) * PART, :] = turned[out, 0 : 9 * PART].astype(BF)
    for part in range(PARTS):
        out = slice(part * PART, (part + 1) * PART)
        for a in range(3):
            blocks = [block((2 - a) * 9 + 8 - bc, part)[:, out] for bc in range(9)]
            backward_ref[part, a * PART : (a + 1) * PART, :] = jnp.concatenate(blocks, axis=1).astype(BF)


def make_finder(
    slot_hbm, link_hbm, own_ref, mate_ref, first_ref, second_ref,
    planes, strips, slot_ref, link_ref, sems,
):
    copies = bring(((slot_hbm, slot_ref), (link_hbm, link_ref)), sems)
    slots = slot_ref.shape[0]
    odd = (lax.axis_index("bricks") & 1) == 1
    head = slots * 2 * CH
    mine = count_sent(own_ref[head : head + HEAD, :])
    other = count_sent(mate_ref[head : head + HEAD, :])
    row = (NEAR // 2 + 2) * CH
    counts = [count_sent(ref[row : row + HEAD, :]) for ref in (first_ref, second_ref)]
    for k, ref in enumerate((own_ref, mate_ref)):
        for s in range(slots):
            strips[k * slots + s] = ref[s * 2 * CH : s * 2 * CH + CH, :]
            planes[k * slots + s] = ref[s * 2 * CH + CH : (s + 1) * 2 * CH, :]
    for side, near in enumerate((first_ref, second_ref)):
        for start, begin, count in ((side * NEAR, 0, NEAR), (2 * NEAR + side * FAR, NEAR_ROWS, FAR)):
            for j in range(0, count, 2):
                row = begin + j // 2 * CH
                tile = near[row : row + CH, :]
                planes[2 * slots + start + j] = tile
                planes[2 * slots + start + j + 1] = pltpu.roll(tile.astype(F32), 64, 1).astype(BF)
        row, at = NEAR // 2 * CH, 2 * slots + side * EDGE
        strips[at] = near[row : row + CH, :]
        tile = near[row + CH : row + 2 * CH, :]
        strips[at + 1] = tile
        strips[at + 2] = pltpu.roll(tile.astype(F32), TILE - 32, 1).astype(BF)
    nothing = 2 * slots + 2 * NEAR + 2 * FAR
    planes[nothing] = jnp.zeros((CH, TILE), BF)
    for copy in copies:
        copy.wait()
    base = slot_ref[0]
    low_side = odd.astype(jnp.int32)
    high_side = 1 - low_side
    low_count = jnp.where(odd, counts[1], counts[0])
    high_count = jnp.where(odd, counts[0], counts[1])
    mate_first = jnp.where(odd, base - other, base + mine)
    chip_low = jnp.where(odd, base - other, base)
    chip_high = jnp.where(odd, base + mine, base + mine + other)

    def on_chip(brick):
        own = (brick >= base) & (brick < base + mine)
        return jnp.where(own, brick - base, slots + brick - mate_first)

    def find_strip(brick):
        low = 2 * slots + low_side * EDGE + (chip_low - 1 - brick)
        high = 2 * slots + high_side * EDGE + (brick - chip_high)
        at = jnp.where(brick < chip_low, low, jnp.where(brick >= chip_high, high, on_chip(brick)))
        return jnp.clip(at, 0, 2 * slots + 2 * EDGE - 1)

    def outside(distance, count, side):
        near = 2 * slots + side * NEAR + distance
        far = 2 * slots + 2 * NEAR + side * FAR + distance - count
        return jnp.where(distance < count, near, far)

    def find_plane(brick, exists):
        low = outside(chip_low - 1 - brick, low_count, low_side)
        high = outside(brick - chip_high, high_count, high_side)
        at = jnp.where(brick < chip_low, low, jnp.where(brick >= chip_high, high, on_chip(brick)))
        return jnp.clip(jnp.where(exists, at, nothing), 0, nothing)

    return base, mine, find_strip, find_plane


def convolve_pair(
    pair, base, find_strip, find_plane, link_ref, field_ref, planes, strips,
    spread_ref, ends_ref, shifts_ref, weight_ref, mixed, taps, sums,
):
    slots = (2 * pair, 2 * pair + 1)
    kinds, outers, besides = [], [], []
    of_y = lax.broadcasted_iota(jnp.int32, (CH, TILE), 1) % 64 < 32
    for s in slots:
        brick = base + s
        kind = brick & 3
        step_y = 2 - 2 * (kind & 2)
        step_z = 1 - 2 * (kind & 1)
        sides = (brick + step_y, brick + step_z, brick + step_y + step_z)
        has_low = link_ref[s, 0] >= 0
        has_high = link_ref[s, 1] >= 0

        def outer(near):
            high = planes[find_plane(near + 4, has_high)]
            low = planes[find_plane(near - 4, has_low)]
            return join_halves(high, low)

        beside_y, beside_z, beside_yz = [strips[find_strip(m)] for m in sides]
        beside = jnp.where(of_y, beside_y.astype(F32), beside_z.astype(F32)).astype(BF)
        besides.append(jnp.concatenate([beside, beside_yz], axis=1))
        kinds.append(kind)
        outers.append((outer(brick), jnp.concatenate([outer(m) for m in sides], axis=1)))
    halos = dot(jnp.concatenate(besides, axis=0), spread_ref[...]).astype(BF)
    for e, s in enumerate(slots):
        for i in range(4):
            rows = slice(i * CH, (i + 1) * CH)
            mixed[e, rows, 0:TILE] = field_ref[s, :, i * TILE : (i + 1) * TILE]
            mixed[e, rows, TILE:] = halos[e * CH : (e + 1) * CH, i * TILE : (i + 1) * TILE]
        mixed[e, 4 * CH :, 0:TILE] = outers[e][0]
        mixed[e, 4 * CH :, TILE:] = dot(outers[e][1], ends_ref[kinds[e]]).astype(BF)

    def put_taps(e, bc, values):
        for i in range(5):
            lanes = slice((5 * e + i) * TILE, (5 * e + i + 1) * TILE)
            for p in range(PARTS):
                taps[p, bc * PART : (bc + 1) * PART, lanes] = values[
                    i * CH + p * PART : i * CH + (p + 1) * PART, :
                ]

    for e in range(2):
        for k in range(0, 8, 2):
            part = dot(mixed[e], shifts_ref[kinds[e], :, k * TILE : (k + 2) * TILE]).astype(BF)
            put_taps(e, SIDES[k], part[:, 0:TILE])
            put_taps(e, SIDES[k + 1], part[:, TILE:])
        put_taps(e, 4, mixed[e, :, 0:TILE])
    for p in range(PARTS):
        part = dot(weight_ref[p], taps[p, 0 : 9 * PART, :])
        for a in range(3):
            at = a * CH + p * PART
            sums[at : at + PART, :] = part[a * PART : (a + 1) * PART, :]
    left = left_half((CH, TILE))
    results = []
    for e in range(2):
        first = 5 * e
        turned = []
        for a in (0, 2):
            rows = slice(a * CH, (a + 1) * CH)
            turned.append(
                [
                    pltpu.roll(sums[rows, (first + i) * TILE : (first + i + 1) * TILE], 64, 1)
                    for i in range(5)
                ]
            )
        tiles = []
        for i in range(4):
            lower = jnp.where(left, turned[0][(i - 1) % 5], turned[0][i])
            upper = jnp.where(left, turned[1][i], turned[1][i + 1])
            lanes = slice((first + i) * TILE, (first + i + 1) * TILE)
            tiles.append(sums[CH : 2 * CH, lanes] + lower + upper)
        results.append(tiles)
    return results


def forward_kernel(
    slot_hbm, link_hbm, field_ref, own_ref, mate_ref, first_ref, second_ref, weight_ref, bias_ref, cortex_ref, upstream_ref, strips_ref, spread_ref,
    ends_ref, shifts_ref, fold_ref, out_ref, dpre_ref, msg_ref, sum_ref,
    planes, strips, mixed, taps, sums, slot_ref, link_ref, sems, spots, grads,
):
    slots = field_ref.shape[0]
    base, mine, find_strip, find_plane = make_finder(
        slot_hbm, link_hbm, own_ref, mate_ref, first_ref, second_ref,
        planes, strips, slot_ref, link_ref, sems,
    )
    for pair in range(slots // 2):
        taps[pair, :, 9 * PART :, :] = jnp.ones((PARTS, PART, 10 * TILE), BF)

    square = (CH, CH)
    diagonal = lax.broadcasted_iota(jnp.int32, square, 0) == lax.broadcasted_iota(jnp.int32, square, 1)
    bias = jnp.sum(jnp.where(diagonal, bias_ref[...], 0.0), axis=1, keepdims=True)
    left = left_half((CH, TILE))
    zero = jnp.zeros((CH, TILE), F32)

    def put_spots(pair, a, i, values):
        for p in range(PARTS):
            spots[pair, p, a * PART : (a + 1) * PART, i * TILE : (i + 1) * TILE] = values[
                p * PART : (p + 1) * PART, :
            ]

    for pair in range(slots // 2):
        results = convolve_pair(
            pair, base, find_strip, find_plane, link_ref, field_ref, planes, strips,
            spread_ref, ends_ref, shifts_ref, weight_ref, mixed.at[pair], taps.at[pair], sums.at[pair],
        )
        for e, tiles in enumerate(results):
            s = 2 * pair + e
            present = jnp.where(s < mine, 1.0, 0.0)
            turned = []
            for i in range(4):
                lanes = slice(i * TILE, (i + 1) * TILE)
                pre = tiles[i] + bias
                keep = cortex_ref[s : s + 1, lanes].astype(F32) * present
                sigma = 1.0 / (1.0 + jnp.exp(-pre))
                out_ref[s, :, lanes] = (pre * sigma * keep).astype(BF)
                slope = sigma * (1.0 + pre * (1.0 - sigma))
                dpre = (upstream_ref[s, :, lanes].astype(F32) * keep * slope).astype(BF)
                dpre_ref[s, :, lanes] = dpre
                put_spots(pair, 1, 5 * e + i, dpre)
                turned.append(pltpu.roll(dpre.astype(F32), 64, 1))
            put_spots(pair, 1, 5 * e + 4, zero.astype(BF))
            turned.append(zero)
            for i in range(4):
                here = jnp.where(left, turned[i], turned[i + 1])
                put_spots(pair, 0, 5 * e + i, here.astype(BF))
                here = jnp.where(left, turned[i - 1] if i else zero, turned[i])
                put_spots(pair, 2, 5 * e + i, here.astype(BF))
            put_spots(pair, 0, 5 * e + 4, jnp.where(left, 0.0, turned[0]).astype(BF))
            put_spots(pair, 2, 5 * e + 4, jnp.where(left, turned[3], 0.0).astype(BF))
        for p in range(PARTS):
            term = lax.dot_general(
                spots[pair, p], taps[pair, p], (((1,), (1,)), ((), ())), preferred_element_type=F32
            )
            grads[p] = grads[p] + term if pair else term

    pack_bricks(slot_ref, dpre_ref, strips_ref, msg_ref)
    rows = jnp.concatenate(
        [grads[p, a * PART : (a + 1) * PART, :] for a in range(3) for p in range(PARTS)], axis=0
    )
    group = lax.broadcasted_iota(jnp.int32, rows.shape, 0) // GC % 2
    column = lax.broadcasted_iota(jnp.int32, rows.shape, 1)
    same = (column // GC % 2 == group) | (column >= 9 * PART)
    full = jnp.dot(
        jnp.where(same, rows, 0.0), fold_ref[...],
        precision=lax.Precision.HIGHEST, preferred_element_type=F32,
    ).T
    last = jnp.concatenate([full[:, TILE:], jnp.zeros((2 * GC, CH), F32)], axis=0)
    half = SUM_ROWS - 10 * GC
    last = jnp.concatenate([last[0:half], last[half:]], axis=1)
    sum_ref[0 : 10 * GC, :] = full[:, 0:TILE]
    sum_ref[10 * GC :, :] = last


def backward_kernel(pairs, *refs):
    if pairs[0] == 0:
        backward_body(pairs, *refs)
        return
    last_ref, out_ref = refs[11], refs[12]
    for s in range(2 * pairs[0]):
        out_ref[s] = last_ref[s]
    backward_body(pairs, *refs[:11], *refs[12:])


def backward_body(
    pairs, slot_hbm, link_hbm, field_ref, own_ref, mate_ref, first_ref, second_ref, weight_ref, spread_ref, ends_ref, shifts_ref, out_ref,
    planes, strips, mixed, taps, sums, slot_ref, link_ref, sems,
):
    base, mine, find_strip, find_plane = make_finder(
        slot_hbm, link_hbm, own_ref, mate_ref, first_ref, second_ref,
        planes, strips, slot_ref, link_ref, sems,
    )
    for pair in pairs:
        results = convolve_pair(
            pair, base, find_strip, find_plane, link_ref, field_ref, planes, strips,
            spread_ref, ends_ref, shifts_ref, weight_ref, mixed.at[pair], taps.at[pair], sums.at[pair],
        )
        for e, tiles in enumerate(results):
            s = 2 * pair + e
            present = jnp.where(s < mine, 1.0, 0.0)
            for i in range(4):
                out_ref[s, :, i * TILE : (i + 1) * TILE] = (tiles[i] * present).astype(BF)


def finish_kernel(total_ref, kernel_ref, bias_ref):
    total = total_ref[...]
    first, last = total[0 : 10 * GC, :], total[10 * GC :, :]
    turned = pltpu.roll(first, 64, 1)
    parts = (first, turned, jnp.concatenate([last, pltpu.roll(last, 64, 1)], axis=0))
    for a, part in enumerate(parts):
        kernel_ref[a * 9 * GC : (a + 1) * 9 * GC, :] = part[0 : 9 * GC, 0:CH]
    bias_ref[...] = turned[9 * GC : 9 * GC + 1, 0:CH]


VMEM = pl.BlockSpec(memory_space=pltpu.VMEM)
HBM = pl.BlockSpec(memory_space=pltpu.HBM)


def call(kernel, ins, outs, scratch=(), flops=0, size=400000, limit=24):
    return pl.pallas_call(
        kernel,
        in_specs=ins,
        out_specs=tuple(VMEM for _ in outs),
        out_shape=tuple(outs),
        scratch_shapes=list(scratch),
        compiler_params=pltpu.CompilerParams(vmem_limit_bytes=limit * 2**20),
        cost_estimate=pl.CostEstimate(flops=flops, bytes_accessed=size, transcendentals=0),
    )


def sent(block, route):
    return lax.ppermute(block, "bricks", route)


def shards(voxels, kernel, bias, cortex, slot_to_brick, neighbors, cotangent):
    slots = voxels.shape[0]
    devices = lax.axis_size("bricks")
    strips, spread, ends, shifts, fold = (jnp.asarray(t, BF) for t in tables())
    fold = fold.astype(F32)
    shape = jax.ShapeDtypeStruct
    pack_rows = slots * 2 * CH + HEAD
    near_shape = shape((NEAR_ROWS, TILE), BF)
    far_shape = shape((FAR // 2 * CH, TILE), BF)

    def routed(block, chips):
        pairs = []
        for d in range(devices):
            to = d + 2 * chips - 1 if d % 2 else d - 2 * chips + 1
            if 0 <= to < devices:
                pairs.append((d, to))
        return sent(block, pairs)

    def swapped(block, mask):
        return sent(block, [(d, d ^ mask) for d in range(devices)])

    def merged(near, far):
        rows = near.shape[0] + far.shape[0]
        return call(merge_kernel, [VMEM] * 2, [shape((rows, TILE), BF)])(near, far)[0]

    box = [pltpu.VMEM((4 * slots, CH, TILE), BF)]
    work = [
        pltpu.VMEM((2 * slots + 2 * NEAR + 2 * FAR + 1, CH, TILE), BF),
        pltpu.VMEM((2 * slots + 2 * EDGE, CH, TILE), BF),
        pltpu.VMEM((slots // 2, 2, 5 * CH, 2 * TILE), BF),
        pltpu.VMEM((slots // 2, PARTS, 10 * PART, 10 * TILE), BF),
        pltpu.VMEM((slots // 2, 3 * CH, 10 * TILE), F32),
        pltpu.SMEM(slot_to_brick.shape, jnp.int32),
        pltpu.SMEM(neighbors.shape, jnp.int32),
        pltpu.SemaphoreType.DMA((2,)),
    ]
    field = shape(voxels.shape, BF)

    (own,) = call(
        pack_kernel,
        [HBM] * 3,
        [shape((pack_rows, TILE), BF)],
        [pltpu.VMEM(voxels.shape, BF), pltpu.VMEM(strips.shape, BF), pltpu.SMEM(slot_to_brick.shape, jnp.int32), pltpu.SemaphoreType.DMA((3,))],
        limit=60,
    )(slot_to_brick, voxels, strips)
    mate = swapped(own, 1)
    weight_shape = shape((PARTS, 3 * PART, 9 * PART), BF)
    taps = jnp.transpose(kernel, (2, 3, 4, 1, 0)).reshape(27 * GC, CH)
    staged = call(
        weight_kernel, [VMEM], [weight_shape] * 2, [pltpu.VMEM((2 * TILE, 3 * TILE), F32)], flops=BUSY
    )(taps)
    near, far = call(
        functools.partial(route_kernel, slots), [VMEM, VMEM], [near_shape, far_shape], box,
        flops=BUSY,
    )(own, mate)
    near, far = routed(near, 1), routed(far, 2)
    near, far, staged = lax.optimization_barrier((near, far, staged))
    forward, backward = staged
    first = merged(near, far)
    second = swapped(first, 1)
    activated, dpre, own, terms = call(
        forward_kernel,
        [HBM, HBM] + [VMEM] * 14,
        [field, field, shape((pack_rows, TILE), BF), shape((SUM_ROWS, TILE), F32)],
        work
        + [
            pltpu.VMEM((slots // 2, PARTS, 3 * PART, 10 * TILE), BF),
            pltpu.VMEM((PARTS, 3 * PART, 10 * PART), F32),
        ],
        flops=4 * 10**9,
    )(
        slot_to_brick, neighbors, voxels, own, mate, first, second, forward, bias.reshape(1, CH),
        cortex, cotangent, strips, spread, ends, shifts, fold,
    )
    pieces = terms.reshape(devices, -1, min(TILE, SUM_ROWS * TILE // devices))
    pieces = lax.all_to_all(pieces, "bricks", 0, 0)
    mate = swapped(own, 1)
    near, far = call(
        functools.partial(route_kernel, slots), [VMEM, VMEM], [near_shape, far_shape], box,
        flops=BUSY,
    )(own, mate)
    near, far = routed(near, 1), routed(far, 2)
    near, far, pieces = lax.optimization_barrier((near, far, pieces))
    mine = jnp.sum(pieces, axis=0, keepdims=True)
    total = lax.all_to_all(jnp.broadcast_to(mine, pieces.shape), "bricks", 0, 0)
    first = merged(near, far)
    second = swapped(first, 1)
    state = {}

    def part_backward(pair):
        last = [state["grad"]] if pair else []
        (state["grad"],) = call(
            functools.partial(backward_kernel, tuple(range(slots // 2))),
            [HBM, HBM] + [VMEM] * (9 + len(last)),
            [field],
            work,
            flops=10**9,
        )(
            slot_to_brick, neighbors, dpre, own, mate, first, second, backward,
            spread, ends, shifts, *last,
        )

    part_backward(0)
    input_grad = state["grad"]
    kernel_sum, bias_sum = call(
        finish_kernel, [VMEM], [shape((27 * GC, CH), F32), shape((1, CH), F32)]
    )(total.reshape(SUM_ROWS, TILE))
    kernel_grad = jnp.transpose(kernel_sum.reshape(3, 3, 3, GC, CH), (4, 3, 0, 1, 2))
    return (activated, input_grad, kernel_grad, bias_sum.reshape(CH))


def solution(mesh):
    devices = mesh.shape["bricks"]
    assert devices & (devices - 1) == 0
    return jax.shard_map(
        shards,
        mesh=mesh,
        in_specs=(
            P("bricks", None, None),
            P(),
            P(),
            P("bricks", None),
            P("bricks"),
            P("bricks", None),
            P("bricks", None, None),
        ),
        out_specs=(P("bricks", None, None), P("bricks", None, None), P(), P()),
        check_vma=False,
    )
```

```python
import functools

import jax
import jax.numpy as jnp
import numpy as np
from jax import lax
from jax.experimental import pallas as pl
from jax.experimental.pallas import tpu as pltpu
from jax.sharding import PartitionSpec as P

CH = 64
GC = 8
PART = 16
PARTS = CH // PART
SIDES = (0, 1, 2, 3, 5, 6, 7, 8)
TILE = 128
NEAR = 8
FAR = 4
EDGE = 3
BUSY = 10**10
HEAD = 16
NEAR_ROWS = (NEAR // 2 + 2) * CH + HEAD
SUM_ROWS = 128
BF = jnp.bfloat16
F32 = jnp.float32


@functools.cache
def tables():
    strips = np.zeros((4, 512, TILE), np.float32)
    spread = np.zeros((256, 4 * TILE), np.float32)
    ends = np.zeros((4, 384, TILE), np.float32)
    shifts = np.zeros((4, 256, 8 * TILE), np.float32)
    fold = np.zeros((10 * PART, 10 * GC), np.float32)
    for bc in range(9):
        for i in range(PART):
            fold[bc * PART + i, bc * GC + i % GC] = 1
    fold[9 * PART, 9 * GC] = 1
    for half in range(2):
        for xx in range(4):
            for w in range(8):
                i, xp = 2 * half + xx // 2, xx % 2
                spread[half * 64 + xx * 8 + w, i * TILE + xp * 8 + w] = 1
                spread[half * 64 + 32 + xx * 8 + w, i * TILE + 32 + xp * 8 + w] = 1
                spread[128 + half * 64 + xx * 8 + w, i * TILE + 64 + xp * 8 + w] = 1
    for t in range(4):
        q, r = t // 2, t % 2
        own_y, own_z = (0 if q else 7), (0 if r else 7)
        far_y, far_z = 7 - own_y, 7 - own_z
        for half in range(2):
            for xx in range(4):
                for w in range(8):
                    plane = (4 * half + xx) * 64
                    strips[t, plane + own_y * 8 + w, half * 64 + xx * 8 + w] = 1
                    strips[t, plane + w * 8 + own_z, half * 64 + 32 + xx * 8 + w] = 1
        for xp in range(2):
            for w in range(8):
                ends[t, xp * 64 + far_y * 8 + w, xp * 8 + w] = 1
                ends[t, 128 + xp * 64 + w * 8 + far_z, 32 + xp * 8 + w] = 1
                ends[t, 256 + xp * 64 + far_y * 8 + w, 64 + xp * 8 + w] = 1
        out_y, out_z = (-1 if q else 8), (-1 if r else 8)
        for b in range(3):
            for c in range(3):
                if b == 1 and c == 1:
                    continue
                column = SIDES.index(b * 3 + c)
                for xp in range(2):
                    for y in range(8):
                        for z in range(8):
                            yy, zz = y + b - 1, z + c - 1
                            in_y, in_z = 0 <= yy < 8, 0 <= zz < 8
                            if in_y and in_z:
                                k = xp * 64 + yy * 8 + zz
                            elif in_z and yy == out_y:
                                k = 128 + xp * 8 + zz
                            elif in_y and zz == out_z:
                                k = 160 + xp * 8 + yy
                            elif yy == out_y and zz == out_z:
                                k = 192 + xp * 8 + far_z
                            else:
                                continue
                            shifts[t, k, column * TILE + xp * 64 + y * 8 + z] = 1
    return strips, spread, ends, shifts, fold


def left_half(shape):
    return lax.broadcasted_iota(jnp.int32, shape, len(shape) - 1) % TILE < 64


def join_halves(left, right):
    mixed = jnp.where(left_half(left.shape), left.astype(F32), right.astype(F32))
    return mixed.astype(left.dtype)


def dot(a, b):
    return jnp.dot(a, b, preferred_element_type=F32)


def count_own(slot_ref):
    total = jnp.int32(0)
    for s in range(slot_ref.shape[0]):
        total = total + (slot_ref[s] >= 0).astype(jnp.int32)
    return total


def count_sent(head):
    return jnp.max(head.astype(F32)).astype(jnp.int32)


def kind_of(brick):
    return jnp.maximum(brick, 0) & 3


def pack_bricks(slot_ref, field_ref, strips_ref, msg_ref):
    slots = field_ref.shape[0]
    for s in range(slots):
        table = strips_ref[kind_of(slot_ref[s])]
        row = s * 2 * CH
        msg_ref[row : row + CH, :] = dot(field_ref[s], table).astype(BF)
        msg_ref[row + CH : row + 2 * CH, :] = join_halves(
            field_ref[s, :, 0:TILE], field_ref[s, :, 3 * TILE : 4 * TILE]
        )
    row = slots * 2 * CH
    count = count_own(slot_ref).astype(F32)
    msg_ref[row : row + HEAD, :] = jnp.full((HEAD, TILE), count, F32).astype(BF)


def bring(pairs, sems):
    copies = [pltpu.make_async_copy(a, b, sems.at[i]) for i, (a, b) in enumerate(pairs)]
    for copy in copies:
        copy.start()
    return copies


def pack_kernel(slot_hbm, field_hbm, strips_hbm, msg_ref, field_ref, strips_ref, slot_ref, sems):
    pairs = ((slot_hbm, slot_ref), (field_hbm, field_ref), (strips_hbm, strips_ref))
    for copy in bring(pairs, sems):
        copy.wait()
    pack_bricks(slot_ref, field_ref, strips_ref, msg_ref)


def route_body(slots, own_ref, mate_ref, near_ref, far_ref, box):
    odd = (lax.axis_index("bricks") & 1) == 1
    head = slots * 2 * CH
    mine = count_sent(own_ref[head : head + HEAD, :])
    other = count_sent(mate_ref[head : head + HEAD, :])
    for s in range(2 * slots):
        box[s] = own_ref[s * CH : (s + 1) * CH, :]
        box[2 * slots + s] = mate_ref[s * CH : (s + 1) * CH, :]

    def place(j):
        up = jnp.where(j < mine, mine - 1 - j, slots + other - 1 - (j - mine))
        down = jnp.where(j < mine, j, slots + j - mine)
        return jnp.clip(jnp.where(odd, up, down), 0, 2 * slots - 1)

    half = lax.broadcasted_iota(jnp.int32, (CH, TILE), 1) // 64
    counts_here = half == odd.astype(jnp.int32)
    for j in range(0, NEAR, 2):
        first, second = [box[2 * place(j + e) + 1].astype(F32) for e in range(2)]
        both = jnp.where(counts_here, first, pltpu.roll(second, 64, 1)).astype(BF)
        near_ref[j // 2 * CH : (j // 2 + 1) * CH, :] = both
        if j < FAR:
            far_ref[j // 2 * CH : (j // 2 + 1) * CH, :] = both
    of_y = lax.broadcasted_iota(jnp.int32, (CH, TILE), 1) % 64 < 32
    row = NEAR // 2 * CH
    near_ref[row : row + CH, :] = box[2 * place(0)]
    first, second = [box[2 * place(j)].astype(F32) for j in (1, 2)]
    near_ref[row + CH : row + 2 * CH, :] = jnp.where(of_y, first, pltpu.roll(second, 32, 1)).astype(BF)
    row = (NEAR // 2 + 2) * CH
    both = (mine + other).astype(F32)
    near_ref[row : row + HEAD, :] = jnp.full((HEAD, TILE), both, F32).astype(BF)


def route_kernel(slots, own_ref, mate_ref, near_ref, far_ref, box):
    route_body(slots, own_ref, mate_ref, near_ref, far_ref, box)


def merge_kernel(near_ref, far_ref, out_ref):
    out_ref[0:NEAR_ROWS, :] = near_ref[...]
    out_ref[NEAR_ROWS:, :] = far_ref[...]


def weight_kernel(taps_ref, forward_ref, backward_ref, work):
    values = taps_ref[...].astype(F32)
    lanes = lax.broadcasted_iota(jnp.int32, (GC, CH), 1) // GC

    def block(tap, part):
        tile = values[tap * GC : (tap + 1) * GC, :]
        groups = (2 * part, 2 * part + 1)
        return jnp.concatenate([jnp.where(lanes == g, tile, 0.0) for g in groups], axis=0)

    work[...] = jnp.zeros_like(work)
    for part in range(PARTS):
        out = slice(part * PART, (part + 1) * PART)
        for bc in range(9):
            for a in range(3):
                work[bc * PART : (bc + 1) * PART, a * TILE : a * TILE + CH] = block(a * 9 + bc, part)
        for a in range(3):
            turned = work[:, a * TILE : (a + 1) * TILE].T
            forward_ref[part, a * PART : (a + 1) * PART, :] = turned[out, 0 : 9 * PART].astype(BF)
    for part in range(PARTS):
        out = slice(part * PART, (part + 1) * PART)
        for a in range(3):
            blocks = [block((2 - a) * 9 + 8 - bc, part)[:, out] for bc in range(9)]
            backward_ref[part, a * PART : (a + 1) * PART, :] = jnp.concatenate(blocks, axis=1).astype(BF)


def make_finder(
    slot_hbm, link_hbm, own_ref, mate_ref, first_ref, second_ref,
    planes, strips, slot_ref, link_ref, sems,
):
    copies = bring(((slot_hbm, slot_ref), (link_hbm, link_ref)), sems)
    slots = slot_ref.shape[0]
    odd = (lax.axis_index("bricks") & 1) == 1
    head = slots * 2 * CH
    mine = count_sent(own_ref[head : head + HEAD, :])
    other = count_sent(mate_ref[head : head + HEAD, :])
    row = (NEAR // 2 + 2) * CH
    counts = [count_sent(ref[row : row + HEAD, :]) for ref in (first_ref, second_ref)]
    for k, ref in enumerate((own_ref, mate_ref)):
        for s in range(slots):
            strips[k * slots + s] = ref[s * 2 * CH : s * 2 * CH + CH, :]
            planes[k * slots + s] = ref[s * 2 * CH + CH : (s + 1) * 2 * CH, :]
    for side, near in enumerate((first_ref, second_ref)):
        for start, begin, count in ((side * NEAR, 0, NEAR), (2 * NEAR + side * FAR, NEAR_ROWS, FAR)):
            for j in range(0, count, 2):
                row = begin + j // 2 * CH
                tile = near[row : row + CH, :]
                planes[2 * slots + start + j] = tile
                planes[2 * slots + start + j + 1] = pltpu.roll(tile.astype(F32), 64, 1).astype(BF)
        row, at = NEAR // 2 * CH, 2 * slots + side * EDGE
        strips[at] = near[row : row + CH, :]
        tile = near[row + CH : row + 2 * CH, :]
        strips[at + 1] = tile
        strips[at + 2] = pltpu.roll(tile.astype(F32), TILE - 32, 1).astype(BF)
    nothing = 2 * slots + 2 * NEAR + 2 * FAR
    planes[nothing] = jnp.zeros((CH, TILE), BF)
    for copy in copies:
        copy.wait()
    base = slot_ref[0]
    low_side = odd.astype(jnp.int32)
    high_side = 1 - low_side
    low_count = jnp.where(odd, counts[1], counts[0])
    high_count = jnp.where(odd, counts[0], counts[1])
    mate_first = jnp.where(odd, base - other, base + mine)
    chip_low = jnp.where(odd, base - other, base)
    chip_high = jnp.where(odd, base + mine, base + mine + other)

    def on_chip(brick):
        own = (brick >= base) & (brick < base + mine)
        return jnp.where(own, brick - base, slots + brick - mate_first)

    def find_strip(brick):
        low = 2 * slots + low_side * EDGE + (chip_low - 1 - brick)
        high = 2 * slots + high_side * EDGE + (brick - chip_high)
        at = jnp.where(brick < chip_low, low, jnp.where(brick >= chip_high, high, on_chip(brick)))
        return jnp.clip(at, 0, 2 * slots + 2 * EDGE - 1)

    def outside(distance, count, side):
        near = 2 * slots + side * NEAR + distance
        far = 2 * slots + 2 * NEAR + side * FAR + distance - count
        return jnp.where(distance < count, near, far)

    def find_plane(brick, exists):
        low = outside(chip_low - 1 - brick, low_count, low_side)
        high = outside(brick - chip_high, high_count, high_side)
        at = jnp.where(brick < chip_low, low, jnp.where(brick >= chip_high, high, on_chip(brick)))
        return jnp.clip(jnp.where(exists, at, nothing), 0, nothing)

    return base, mine, find_strip, find_plane


def convolve_pair(
    pair, base, find_strip, find_plane, link_ref, field_ref, planes, strips,
    spread_ref, ends_ref, shifts_ref, weight_ref, mixed, taps, sums,
):
    slots = (2 * pair, 2 * pair + 1)
    kinds, outers, besides = [], [], []
    of_y = lax.broadcasted_iota(jnp.int32, (CH, TILE), 1) % 64 < 32
    for s in slots:
        brick = base + s
        kind = brick & 3
        step_y = 2 - 2 * (kind & 2)
        step_z = 1 - 2 * (kind & 1)
        sides = (brick + step_y, brick + step_z, brick + step_y + step_z)
        has_low = link_ref[s, 0] >= 0
        has_high = link_ref[s, 1] >= 0

        def outer(near):
            high = planes[find_plane(near + 4, has_high)]
            low = planes[find_plane(near - 4, has_low)]
            return join_halves(high, low)

        beside_y, beside_z, beside_yz = [strips[find_strip(m)] for m in sides]
        beside = jnp.where(of_y, beside_y.astype(F32), beside_z.astype(F32)).astype(BF)
        besides.append(jnp.concatenate([beside, beside_yz], axis=1))
        kinds.append(kind)
        outers.append((outer(brick), jnp.concatenate([outer(m) for m in sides], axis=1)))
    halos = dot(jnp.concatenate(besides, axis=0), spread_ref[...]).astype(BF)
    for e, s in enumerate(slots):
        for i in range(4):
            rows = slice(i * CH, (i + 1) * CH)
            mixed[e, rows, 0:TILE] = field_ref[s, :, i * TILE : (i + 1) * TILE]
            mixed[e, rows, TILE:] = halos[e * CH : (e + 1) * CH, i * TILE : (i + 1) * TILE]
        mixed[e, 4 * CH :, 0:TILE] = outers[e][0]
        mixed[e, 4 * CH :, TILE:] = dot(outers[e][1], ends_ref[kinds[e]]).astype(BF)

    def put_taps(e, bc, values):
        for i in range(5):
            lanes = slice((5 * e + i) * TILE, (5 * e + i + 1) * TILE)
            for p in range(PARTS):
                taps[p, bc * PART : (bc + 1) * PART, lanes] = values[
                    i * CH + p * PART : i * CH + (p + 1) * PART, :
                ]

    for e in range(2):
        for k in range(0, 8, 2):
            part = dot(mixed[e], shifts_ref[kinds[e], :, k * TILE : (k + 2) * TILE]).astype(BF)
            put_taps(e, SIDES[k], part[:, 0:TILE])
            put_taps(e, SIDES[k + 1], part[:, TILE:])
        put_taps(e, 4, mixed[e, :, 0:TILE])
    for p in range(PARTS):
        part = dot(weight_ref[p], taps[p, 0 : 9 * PART, :])
        for a in range(3):
            at = a * CH + p * PART
            sums[at : at + PART, :] = part[a * PART : (a + 1) * PART, :]
    left = left_half((CH, TILE))
    results = []
    for e in range(2):
        first = 5 * e
        turned = []
        for a in (0, 2):
            rows = slice(a * CH, (a + 1) * CH)
            turned.append(
                [
                    pltpu.roll(sums[rows, (first + i) * TILE : (first + i + 1) * TILE], 64, 1)
                    for i in range(5)
                ]
            )
        tiles = []
        for i in range(4):
            lower = jnp.where(left, turned[0][(i - 1) % 5], turned[0][i])
            upper = jnp.where(left, turned[1][i], turned[1][i + 1])
            lanes = slice((first + i) * TILE, (first + i + 1) * TILE)
            tiles.append(sums[CH : 2 * CH, lanes] + lower + upper)
        results.append(tiles)
    return results


def forward_kernel(
    slot_hbm, link_hbm, field_ref, own_ref, mate_ref, first_ref, second_ref, weight_ref, bias_ref, cortex_ref, upstream_ref, strips_ref, spread_ref,
    ends_ref, shifts_ref, fold_ref, out_ref, dpre_ref, msg_ref, sum_ref,
    planes, strips, mixed, taps, sums, slot_ref, link_ref, sems, spots, grads,
):
    slots = field_ref.shape[0]
    base, mine, find_strip, find_plane = make_finder(
        slot_hbm, link_hbm, own_ref, mate_ref, first_ref, second_ref,
        planes, strips, slot_ref, link_ref, sems,
    )
    for pair in range(slots // 2):
        taps[pair, :, 9 * PART :, :] = jnp.ones((PARTS, PART, 10 * TILE), BF)

    square = (CH, CH)
    diagonal = lax.broadcasted_iota(jnp.int32, square, 0) == lax.broadcasted_iota(jnp.int32, square, 1)
    bias = jnp.sum(jnp.where(diagonal, bias_ref[...], 0.0), axis=1, keepdims=True)
    left = left_half((CH, TILE))
    zero = jnp.zeros((CH, TILE), F32)

    def put_spots(pair, a, i, values):
        for p in range(PARTS):
            spots[pair, p, a * PART : (a + 1) * PART, i * TILE : (i + 1) * TILE] = values[
                p * PART : (p + 1) * PART, :
            ]

    for pair in range(slots // 2):
        results = convolve_pair(
            pair, base, find_strip, find_plane, link_ref, field_ref, planes, strips,
            spread_ref, ends_ref, shifts_ref, weight_ref, mixed.at[pair], taps.at[pair], sums.at[pair],
        )
        for e, tiles in enumerate(results):
            s = 2 * pair + e
            present = jnp.where(s < mine, 1.0, 0.0)
            turned = []
            for i in range(4):
                lanes = slice(i * TILE, (i + 1) * TILE)
                pre = tiles[i] + bias
                keep = cortex_ref[s : s + 1, lanes].astype(F32) * present
                sigma = 1.0 / (1.0 + jnp.exp(-pre))
                out_ref[s, :, lanes] = (pre * sigma * keep).astype(BF)
                slope = sigma * (1.0 + pre * (1.0 - sigma))
                dpre = (upstream_ref[s, :, lanes].astype(F32) * keep * slope).astype(BF)
                dpre_ref[s, :, lanes] = dpre
                put_spots(pair, 1, 5 * e + i, dpre)
                turned.append(pltpu.roll(dpre.astype(F32), 64, 1))
            put_spots(pair, 1, 5 * e + 4, zero.astype(BF))
            turned.append(zero)
            for i in range(4):
                here = jnp.where(left, turned[i], turned[i + 1])
                put_spots(pair, 0, 5 * e + i, here.astype(BF))
                here = jnp.where(left, turned[i - 1] if i else zero, turned[i])
                put_spots(pair, 2, 5 * e + i, here.astype(BF))
            put_spots(pair, 0, 5 * e + 4, jnp.where(left, 0.0, turned[0]).astype(BF))
            put_spots(pair, 2, 5 * e + 4, jnp.where(left, turned[3], 0.0).astype(BF))
        for p in range(PARTS):
            term = lax.dot_general(
                taps[pair, p], spots[pair, p], (((1,), (1,)), ((), ())), preferred_element_type=F32
            )
            grads[p] = grads[p] + term if pair else term

    pack_bricks(slot_ref, dpre_ref, strips_ref, msg_ref)
    turned = [grads[p].T for p in range(PARTS)]
    rows = jnp.concatenate(
        [turned[p][a * PART : (a + 1) * PART, :] for a in range(3) for p in range(PARTS)], axis=0
    )
    group = lax.broadcasted_iota(jnp.int32, rows.shape, 0) // GC % 2
    column = lax.broadcasted_iota(jnp.int32, rows.shape, 1)
    same = (column // GC % 2 == group) | (column >= 9 * PART)
    full = jnp.dot(
        jnp.where(same, rows, 0.0), fold_ref[...],
        precision=lax.Precision.HIGHEST, preferred_element_type=F32,
    ).T
    last = jnp.concatenate([full[:, TILE:], jnp.zeros((2 * GC, CH), F32)], axis=0)
    half = SUM_ROWS - 10 * GC
    last = jnp.concatenate([last[0:half], last[half:]], axis=1)
    sum_ref[0 : 10 * GC, :] = full[:, 0:TILE]
    sum_ref[10 * GC :, :] = last


def backward_kernel(pairs, *refs):
    if pairs[0] == 0:
        backward_body(pairs, *refs)
        return
    last_ref, out_ref = refs[11], refs[12]
    for s in range(2 * pairs[0]):
        out_ref[s] = last_ref[s]
    backward_body(pairs, *refs[:11], *refs[12:])


def backward_body(
    pairs, slot_hbm, link_hbm, field_ref, own_ref, mate_ref, first_ref, second_ref, weight_ref, spread_ref, ends_ref, shifts_ref, out_ref,
    planes, strips, mixed, taps, sums, slot_ref, link_ref, sems,
):
    base, mine, find_strip, find_plane = make_finder(
        slot_hbm, link_hbm, own_ref, mate_ref, first_ref, second_ref,
        planes, strips, slot_ref, link_ref, sems,
    )
    for pair in pairs:
        results = convolve_pair(
            pair, base, find_strip, find_plane, link_ref, field_ref, planes, strips,
            spread_ref, ends_ref, shifts_ref, weight_ref, mixed.at[pair], taps.at[pair], sums.at[pair],
        )
        for e, tiles in enumerate(results):
            s = 2 * pair + e
            present = jnp.where(s < mine, 1.0, 0.0)
            for i in range(4):
                out_ref[s, :, i * TILE : (i + 1) * TILE] = (tiles[i] * present).astype(BF)


def finish_kernel(total_ref, kernel_ref, bias_ref):
    total = total_ref[...]
    first, last = total[0 : 10 * GC, :], total[10 * GC :, :]
    turned = pltpu.roll(first, 64, 1)
    parts = (first, turned, jnp.concatenate([last, pltpu.roll(last, 64, 1)], axis=0))
    for a, part in enumerate(parts):
        kernel_ref[a * 9 * GC : (a + 1) * 9 * GC, :] = part[0 : 9 * GC, 0:CH]
    bias_ref[...] = turned[9 * GC : 9 * GC + 1, 0:CH]


VMEM = pl.BlockSpec(memory_space=pltpu.VMEM)
HBM = pl.BlockSpec(memory_space=pltpu.HBM)


def call(kernel, ins, outs, scratch=(), flops=0, size=400000, limit=24):
    return pl.pallas_call(
        kernel,
        in_specs=ins,
        out_specs=tuple(VMEM for _ in outs),
        out_shape=tuple(outs),
        scratch_shapes=list(scratch),
        compiler_params=pltpu.CompilerParams(vmem_limit_bytes=limit * 2**20),
        cost_estimate=pl.CostEstimate(flops=flops, bytes_accessed=size, transcendentals=0),
    )


def sent(block, route):
    return lax.ppermute(block, "bricks", route)


def shards(voxels, kernel, bias, cortex, slot_to_brick, neighbors, cotangent):
    slots = voxels.shape[0]
    devices = lax.axis_size("bricks")
    strips, spread, ends, shifts, fold = (jnp.asarray(t, BF) for t in tables())
    fold = fold.astype(F32)
    shape = jax.ShapeDtypeStruct
    pack_rows = slots * 2 * CH + HEAD
    near_shape = shape((NEAR_ROWS, TILE), BF)
    far_shape = shape((FAR // 2 * CH, TILE), BF)

    def routed(block, chips):
        pairs = []
        for d in range(devices):
            to = d + 2 * chips - 1 if d % 2 else d - 2 * chips + 1
            if 0 <= to < devices:
                pairs.append((d, to))
        return sent(block, pairs)

    def swapped(block, mask):
        return sent(block, [(d, d ^ mask) for d in range(devices)])

    def merged(near, far):
        rows = near.shape[0] + far.shape[0]
        return call(merge_kernel, [VMEM] * 2, [shape((rows, TILE), BF)])(near, far)[0]

    box = [pltpu.VMEM((4 * slots, CH, TILE), BF)]
    work = [
        pltpu.VMEM((2 * slots + 2 * NEAR + 2 * FAR + 1, CH, TILE), BF),
        pltpu.VMEM((2 * slots + 2 * EDGE, CH, TILE), BF),
        pltpu.VMEM((slots // 2, 2, 5 * CH, 2 * TILE), BF),
        pltpu.VMEM((slots // 2, PARTS, 10 * PART, 10 * TILE), BF),
        pltpu.VMEM((slots // 2, 3 * CH, 10 * TILE), F32),
        pltpu.SMEM(slot_to_brick.shape, jnp.int32),
        pltpu.SMEM(neighbors.shape, jnp.int32),
        pltpu.SemaphoreType.DMA((2,)),
    ]
    field = shape(voxels.shape, BF)

    (own,) = call(
        pack_kernel,
        [HBM] * 3,
        [shape((pack_rows, TILE), BF)],
        [pltpu.VMEM(voxels.shape, BF), pltpu.VMEM(strips.shape, BF), pltpu.SMEM(slot_to_brick.shape, jnp.int32), pltpu.SemaphoreType.DMA((3,))],
        limit=60,
    )(slot_to_brick, voxels, strips)
    mate = swapped(own, 1)
    weight_shape = shape((PARTS, 3 * PART, 9 * PART), BF)
    taps = jnp.transpose(kernel, (2, 3, 4, 1, 0)).reshape(27 * GC, CH)
    staged = call(
        weight_kernel, [VMEM], [weight_shape] * 2, [pltpu.VMEM((2 * TILE, 3 * TILE), F32)], flops=BUSY
    )(taps)
    near, far = call(
        functools.partial(route_kernel, slots), [VMEM, VMEM], [near_shape, far_shape], box,
        flops=BUSY,
    )(own, mate)
    near, far = routed(near, 1), routed(far, 2)
    near, far, staged = lax.optimization_barrier((near, far, staged))
    forward, backward = staged
    first = merged(near, far)
    second = swapped(first, 1)
    activated, dpre, own, terms = call(
        forward_kernel,
        [HBM, HBM] + [VMEM] * 14,
        [field, field, shape((pack_rows, TILE), BF), shape((SUM_ROWS, TILE), F32)],
        work
        + [
            pltpu.VMEM((slots // 2, PARTS, 3 * PART, 10 * TILE), BF),
            pltpu.VMEM((PARTS, 10 * PART, 3 * PART), F32),
        ],
        flops=4 * 10**9,
    )(
        slot_to_brick, neighbors, voxels, own, mate, first, second, forward, bias.reshape(1, CH),
        cortex, cotangent, strips, spread, ends, shifts, fold,
    )
    pieces = terms.reshape(devices, -1, min(TILE, SUM_ROWS * TILE // devices))
    pieces = lax.all_to_all(pieces, "bricks", 0, 0)
    mate = swapped(own, 1)
    near, far = call(
        functools.partial(route_kernel, slots), [VMEM, VMEM], [near_shape, far_shape], box,
        flops=BUSY,
    )(own, mate)
    near, far = routed(near, 1), routed(far, 2)
    near, far, pieces = lax.optimization_barrier((near, far, pieces))
    mine = jnp.sum(pieces, axis=0, keepdims=True)
    total = lax.all_to_all(jnp.broadcast_to(mine, pieces.shape), "bricks", 0, 0)
    first = merged(near, far)
    second = swapped(first, 1)
    state = {}

    def part_backward(pair):
        last = [state["grad"]] if pair else []
        (state["grad"],) = call(
            functools.partial(backward_kernel, tuple(range(slots // 2))),
            [HBM, HBM] + [VMEM] * (9 + len(last)),
            [field],
            work,
            flops=10**9,
        )(
            slot_to_brick, neighbors, dpre, own, mate, first, second, backward,
            spread, ends, shifts, *last,
        )

    part_backward(0)
    input_grad = state["grad"]
    total, input_grad = lax.optimization_barrier((total, input_grad))
    kernel_sum, bias_sum = call(
        finish_kernel, [VMEM], [shape((27 * GC, CH), F32), shape((1, CH), F32)]
    )(total.reshape(SUM_ROWS, TILE))
    kernel_grad = jnp.transpose(kernel_sum.reshape(3, 3, 3, GC, CH), (4, 3, 0, 1, 2))
    return (activated, input_grad, kernel_grad, bias_sum.reshape(CH))


def solution(mesh):
    devices = mesh.shape["bricks"]
    assert devices & (devices - 1) == 0
    return jax.shard_map(
        shards,
        mesh=mesh,
        in_specs=(
            P("bricks", None, None),
            P(),
            P(),
            P("bricks", None),
            P("bricks"),
            P("bricks", None),
            P("bricks", None, None),
        ),
        out_specs=(P("bricks", None, None), P("bricks", None, None), P(), P()),
        check_vma=False,
    )
```

```python
import functools

import jax
import jax.numpy as jnp
import numpy as np
from jax import lax
from jax.experimental import pallas as pl
from jax.experimental.pallas import tpu as pltpu
from jax.sharding import PartitionSpec as P

CH = 64
GC = 8
PART = 16
PARTS = CH // PART
SIDES = (0, 1, 2, 3, 5, 6, 7, 8)
TILE = 128
NEAR = 8
FAR = 4
EDGE = 3
BUSY = 10**10
HEAD = 16
NEAR_ROWS = (NEAR // 2 + 2) * CH + HEAD
MESSAGE_ROWS = NEAR_ROWS + FAR // 2 * CH
SUM_ROWS = 128
BF = jnp.bfloat16
F32 = jnp.float32


@functools.cache
def tables():
    strips = np.zeros((4, 512, TILE), np.float32)
    spread = np.zeros((256, 4 * TILE), np.float32)
    ends = np.zeros((4, 384, TILE), np.float32)
    shifts = np.zeros((4, 256, 8 * TILE), np.float32)
    fold = np.zeros((10 * PART, 10 * GC), np.float32)
    for bc in range(9):
        for i in range(PART):
            fold[bc * PART + i, bc * GC + i % GC] = 1
    fold[9 * PART, 9 * GC] = 1
    for half in range(2):
        for xx in range(4):
            for w in range(8):
                i, xp = 2 * half + xx // 2, xx % 2
                spread[half * 64 + xx * 8 + w, i * TILE + xp * 8 + w] = 1
                spread[half * 64 + 32 + xx * 8 + w, i * TILE + 32 + xp * 8 + w] = 1
                spread[128 + half * 64 + xx * 8 + w, i * TILE + 64 + xp * 8 + w] = 1
    for t in range(4):
        q, r = t // 2, t % 2
        own_y, own_z = (0 if q else 7), (0 if r else 7)
        far_y, far_z = 7 - own_y, 7 - own_z
        for half in range(2):
            for xx in range(4):
                for w in range(8):
                    plane = (4 * half + xx) * 64
                    strips[t, plane + own_y * 8 + w, half * 64 + xx * 8 + w] = 1
                    strips[t, plane + w * 8 + own_z, half * 64 + 32 + xx * 8 + w] = 1
        for xp in range(2):
            for w in range(8):
                ends[t, xp * 64 + far_y * 8 + w, xp * 8 + w] = 1
                ends[t, 128 + xp * 64 + w * 8 + far_z, 32 + xp * 8 + w] = 1
                ends[t, 256 + xp * 64 + far_y * 8 + w, 64 + xp * 8 + w] = 1
        out_y, out_z = (-1 if q else 8), (-1 if r else 8)
        for b in range(3):
            for c in range(3):
                if b == 1 and c == 1:
                    continue
                column = SIDES.index(b * 3 + c)
                for xp in range(2):
                    for y in range(8):
                        for z in range(8):
                            yy, zz = y + b - 1, z + c - 1
                            in_y, in_z = 0 <= yy < 8, 0 <= zz < 8
                            if in_y and in_z:
                                k = xp * 64 + yy * 8 + zz
                            elif in_z and yy == out_y:
                                k = 128 + xp * 8 + zz
                            elif in_y and zz == out_z:
                                k = 160 + xp * 8 + yy
                            elif yy == out_y and zz == out_z:
                                k = 192 + xp * 8 + far_z
                            else:
                                continue
                            shifts[t, k, column * TILE + xp * 64 + y * 8 + z] = 1
    return strips, spread, ends, shifts, fold


def left_half(shape):
    return lax.broadcasted_iota(jnp.int32, shape, len(shape) - 1) % TILE < 64


def join_halves(left, right):
    mixed = jnp.where(left_half(left.shape), left.astype(F32), right.astype(F32))
    return mixed.astype(left.dtype)


def dot(a, b):
    return jnp.dot(a, b, preferred_element_type=F32)


def count_own(slot_ref):
    total = jnp.int32(0)
    for s in range(slot_ref.shape[0]):
        total = total + (slot_ref[s] >= 0).astype(jnp.int32)
    return total


def count_sent(head):
    return jnp.max(head.astype(F32)).astype(jnp.int32)


def kind_of(brick):
    return jnp.maximum(brick, 0) & 3


def pack_bricks(slot_ref, field_ref, strips_ref, msg_ref):
    slots = field_ref.shape[0]
    for s in range(slots):
        table = strips_ref[kind_of(slot_ref[s])]
        row = s * 2 * CH
        msg_ref[row : row + CH, :] = dot(field_ref[s], table).astype(BF)
        msg_ref[row + CH : row + 2 * CH, :] = join_halves(
            field_ref[s, :, 0:TILE], field_ref[s, :, 3 * TILE : 4 * TILE]
        )
    row = slots * 2 * CH
    count = count_own(slot_ref).astype(F32)
    msg_ref[row : row + HEAD, :] = jnp.full((HEAD, TILE), count, F32).astype(BF)


def bring(pairs, sems):
    copies = [pltpu.make_async_copy(a, b, sems.at[i]) for i, (a, b) in enumerate(pairs)]
    for copy in copies:
        copy.start()
    return copies


def pack_kernel(slot_hbm, field_hbm, strips_hbm, msg_ref, field_ref, strips_ref, slot_ref, sems):
    pairs = ((slot_hbm, slot_ref), (field_hbm, field_ref), (strips_hbm, strips_ref))
    for copy in bring(pairs, sems):
        copy.wait()
    pack_bricks(slot_ref, field_ref, strips_ref, msg_ref)


def unpack(slots, own_ref, mate_ref, box):
    head = slots * 2 * CH
    for s in range(2 * slots):
        box[s] = own_ref[s * CH : (s + 1) * CH, :]
        box[2 * slots + s] = mate_ref[s * CH : (s + 1) * CH, :]
    return [count_sent(ref[head : head + HEAD, :]) for ref in (own_ref, mate_ref)]


def write_message(place, up, count, box, near_ref, far_ref):
    last = box.shape[0] // 2 - 1

    def at(j):
        return jnp.clip(place(j), 0, last)

    half = lax.broadcasted_iota(jnp.int32, (CH, TILE), 1) // 64
    counts_here = half == jnp.asarray(up).astype(jnp.int32)
    for j in range(0, NEAR, 2):
        first, second = [box[2 * at(j + e) + 1].astype(F32) for e in range(2)]
        both = jnp.where(counts_here, first, pltpu.roll(second, 64, 1)).astype(BF)
        near_ref[j // 2 * CH : (j // 2 + 1) * CH, :] = both
        if j < FAR:
            far_ref[j // 2 * CH : (j // 2 + 1) * CH, :] = both
    of_y = lax.broadcasted_iota(jnp.int32, (CH, TILE), 1) % 64 < 32
    row = NEAR // 2 * CH
    near_ref[row : row + CH, :] = box[2 * at(0)]
    first, second = [box[2 * at(j)].astype(F32) for j in (1, 2)]
    near_ref[row + CH : row + 2 * CH, :] = jnp.where(of_y, first, pltpu.roll(second, 32, 1)).astype(BF)
    row = (NEAR // 2 + 2) * CH
    near_ref[row : row + HEAD, :] = jnp.full((HEAD, TILE), count.astype(F32), F32).astype(BF)


def route_kernel(slots, own_ref, mate_ref, near_ref, far_ref, box):
    odd = (lax.axis_index("bricks") & 1) == 1
    mine, other = unpack(slots, own_ref, mate_ref, box)

    def place(j):
        up = jnp.where(j < mine, mine - 1 - j, slots + other - 1 - (j - mine))
        down = jnp.where(j < mine, j, slots + j - mine)
        return jnp.where(odd, up, down)

    write_message(place, odd, mine + other, box, near_ref, far_ref)


def route_sum_kernel(
    slots, own_ref, mate_ref, up_near_ref, up_far_ref, down_near_ref, down_far_ref, sum_ref, box
):
    mine, other = unpack(slots, own_ref, mate_ref, box)

    def from_end(j):
        return jnp.where(j < mine, mine - 1 - j, slots + other - 1 - (j - mine))

    def from_start(j):
        return jnp.where(j < other, slots + j, j - other)

    write_message(from_end, True, mine + other, box, up_near_ref, up_far_ref)
    write_message(from_start, False, mine + other, box, down_near_ref, down_far_ref)
    high = slots * 2 * CH + HEAD
    low = high + SUM_ROWS
    parts = []
    for ref in (own_ref, mate_ref):
        parts.append(
            ref[high : high + SUM_ROWS, :].astype(F32) + ref[low : low + SUM_ROWS, :].astype(F32)
        )
    sum_ref[...] = parts[0] + parts[1]


def merge_kernel(*refs):
    out_ref, row = refs[-1], 0
    for ref in refs[:-1]:
        out_ref[row : row + ref.shape[0], :] = ref[...]
        row += ref.shape[0]


def weight_kernel(taps_ref, forward_ref, backward_ref, work):
    values = taps_ref[...].astype(F32)
    lanes = lax.broadcasted_iota(jnp.int32, (GC, CH), 1) // GC

    def block(tap, part):
        tile = values[tap * GC : (tap + 1) * GC, :]
        groups = (2 * part, 2 * part + 1)
        return jnp.concatenate([jnp.where(lanes == g, tile, 0.0) for g in groups], axis=0)

    work[...] = jnp.zeros_like(work)
    for part in range(PARTS):
        out = slice(part * PART, (part + 1) * PART)
        for bc in range(9):
            for a in range(3):
                work[bc * PART : (bc + 1) * PART, a * TILE : a * TILE + CH] = block(a * 9 + bc, part)
        for a in range(3):
            turned = work[:, a * TILE : (a + 1) * TILE].T
            forward_ref[part, a * PART : (a + 1) * PART, :] = turned[out, 0 : 9 * PART].astype(BF)
    for part in range(PARTS):
        out = slice(part * PART, (part + 1) * PART)
        for a in range(3):
            blocks = [block((2 - a) * 9 + 8 - bc, part)[:, out] for bc in range(9)]
            backward_ref[part, a * PART : (a + 1) * PART, :] = jnp.concatenate(blocks, axis=1).astype(BF)


def make_finder(
    slot_hbm, link_hbm, own_ref, mate_ref, first_ref, second_ref,
    planes, strips, slot_ref, link_ref, sems, shared,
):
    copies = bring(((slot_hbm, slot_ref), (link_hbm, link_ref)), sems)
    slots = slot_ref.shape[0]
    odd = (lax.axis_index("bricks") & 1) == 1
    head = slots * 2 * CH
    mine = count_sent(own_ref[head : head + HEAD, :])
    other = count_sent(mate_ref[head : head + HEAD, :])
    for k, ref in enumerate((own_ref, mate_ref)):
        for s in range(slots):
            strips[k * slots + s] = ref[s * 2 * CH : s * 2 * CH + CH, :]
            planes[k * slots + s] = ref[s * 2 * CH + CH : (s + 1) * 2 * CH, :]

    def take(near, top, side):
        for start, begin, count in ((side * NEAR, 0, NEAR), (2 * NEAR + side * FAR, NEAR_ROWS, FAR)):
            for j in range(0, count, 2):
                row = top + begin + j // 2 * CH
                tile = near[row : row + CH, :]
                planes[2 * slots + start + j] = tile
                planes[2 * slots + start + j + 1] = pltpu.roll(tile.astype(F32), 64, 1).astype(BF)
        row, at = top + NEAR // 2 * CH, 2 * slots + side * EDGE
        strips[at] = near[row : row + CH, :]
        tile = near[row + CH : row + 2 * CH, :]
        strips[at + 1] = tile
        strips[at + 2] = pltpu.roll(tile.astype(F32), TILE - 32, 1).astype(BF)

    def count_of(ref, top):
        row = top + (NEAR // 2 + 2) * CH
        return count_sent(ref[row : row + HEAD, :])

    if shared:
        for here, ref in ((odd, first_ref), (jnp.logical_not(odd), second_ref)):

            @pl.when(here)
            def _():
                take(ref, 0, 0)
                take(ref, MESSAGE_ROWS, 1)

        low_count, high_count = [
            jnp.where(odd, count_of(first_ref, top), count_of(second_ref, top))
            for top in (0, MESSAGE_ROWS)
        ]
        low_side, high_side = 0, 1
    else:
        take(first_ref, 0, 0)
        take(second_ref, 0, 1)
        counts = count_of(first_ref, 0), count_of(second_ref, 0)
        low_count = jnp.where(odd, counts[1], counts[0])
        high_count = jnp.where(odd, counts[0], counts[1])
        low_side = odd.astype(jnp.int32)
        high_side = 1 - low_side
    nothing = 2 * slots + 2 * NEAR + 2 * FAR
    planes[nothing] = jnp.zeros((CH, TILE), BF)
    for copy in copies:
        copy.wait()
    base = slot_ref[0]
    mate_first = jnp.where(odd, base - other, base + mine)
    chip_low = jnp.where(odd, base - other, base)
    chip_high = jnp.where(odd, base + mine, base + mine + other)

    def on_chip(brick):
        own = (brick >= base) & (brick < base + mine)
        return jnp.where(own, brick - base, slots + brick - mate_first)

    def find_strip(brick):
        low = 2 * slots + low_side * EDGE + (chip_low - 1 - brick)
        high = 2 * slots + high_side * EDGE + (brick - chip_high)
        at = jnp.where(brick < chip_low, low, jnp.where(brick >= chip_high, high, on_chip(brick)))
        return jnp.clip(at, 0, 2 * slots + 2 * EDGE - 1)

    def outside(distance, count, side):
        near = 2 * slots + side * NEAR + distance
        far = 2 * slots + 2 * NEAR + side * FAR + distance - count
        return jnp.where(distance < count, near, far)

    def find_plane(brick, exists):
        low = outside(chip_low - 1 - brick, low_count, low_side)
        high = outside(brick - chip_high, high_count, high_side)
        at = jnp.where(brick < chip_low, low, jnp.where(brick >= chip_high, high, on_chip(brick)))
        return jnp.clip(jnp.where(exists, at, nothing), 0, nothing)

    return base, mine, find_strip, find_plane


def convolve_pair(
    pair, base, find_strip, find_plane, link_ref, field_ref, planes, strips,
    spread_ref, ends_ref, shifts_ref, weight_ref, mixed, taps, sums,
):
    slots = (2 * pair, 2 * pair + 1)
    kinds, outers, besides = [], [], []
    of_y = lax.broadcasted_iota(jnp.int32, (CH, TILE), 1) % 64 < 32
    for s in slots:
        brick = base + s
        kind = brick & 3
        step_y = 2 - 2 * (kind & 2)
        step_z = 1 - 2 * (kind & 1)
        sides = (brick + step_y, brick + step_z, brick + step_y + step_z)
        has_low = link_ref[s, 0] >= 0
        has_high = link_ref[s, 1] >= 0

        def outer(near):
            high = planes[find_plane(near + 4, has_high)]
            low = planes[find_plane(near - 4, has_low)]
            return join_halves(high, low)

        beside_y, beside_z, beside_yz = [strips[find_strip(m)] for m in sides]
        beside = jnp.where(of_y, beside_y.astype(F32), beside_z.astype(F32)).astype(BF)
        besides.append(jnp.concatenate([beside, beside_yz], axis=1))
        kinds.append(kind)
        outers.append((outer(brick), jnp.concatenate([outer(m) for m in sides], axis=1)))
    halos = dot(jnp.concatenate(besides, axis=0), spread_ref[...]).astype(BF)
    for e, s in enumerate(slots):
        for i in range(4):
            rows = slice(i * CH, (i + 1) * CH)
            mixed[e, rows, 0:TILE] = field_ref[s, :, i * TILE : (i + 1) * TILE]
            mixed[e, rows, TILE:] = halos[e * CH : (e + 1) * CH, i * TILE : (i + 1) * TILE]
        mixed[e, 4 * CH :, 0:TILE] = outers[e][0]
        mixed[e, 4 * CH :, TILE:] = dot(outers[e][1], ends_ref[kinds[e]]).astype(BF)

    def put_taps(e, bc, values):
        for i in range(5):
            lanes = slice((5 * e + i) * TILE, (5 * e + i + 1) * TILE)
            for p in range(PARTS):
                taps[p, bc * PART : (bc + 1) * PART, lanes] = values[
                    i * CH + p * PART : i * CH + (p + 1) * PART, :
                ]

    for e in range(2):
        for k in range(0, 8, 2):
            part = dot(mixed[e], shifts_ref[kinds[e], :, k * TILE : (k + 2) * TILE]).astype(BF)
            put_taps(e, SIDES[k], part[:, 0:TILE])
            put_taps(e, SIDES[k + 1], part[:, TILE:])
        put_taps(e, 4, mixed[e, :, 0:TILE])
    for p in range(PARTS):
        part = dot(weight_ref[p], taps[p, 0 : 9 * PART, :])
        for a in range(3):
            at = a * CH + p * PART
            sums[at : at + PART, :] = part[a * PART : (a + 1) * PART, :]
    left = left_half((CH, TILE))
    results = []
    for e in range(2):
        first = 5 * e
        turned = []
        for a in (0, 2):
            rows = slice(a * CH, (a + 1) * CH)
            turned.append(
                [
                    pltpu.roll(sums[rows, (first + i) * TILE : (first + i + 1) * TILE], 64, 1)
                    for i in range(5)
                ]
            )
        tiles = []
        for i in range(4):
            lower = jnp.where(left, turned[0][(i - 1) % 5], turned[0][i])
            upper = jnp.where(left, turned[1][i], turned[1][i + 1])
            lanes = slice((first + i) * TILE, (first + i + 1) * TILE)
            tiles.append(sums[CH : 2 * CH, lanes] + lower + upper)
        results.append(tiles)
    return results


def forward_kernel(
    slot_hbm, link_hbm, field_ref, own_ref, mate_ref, first_ref, second_ref, weight_ref, bias_ref, cortex_ref, upstream_ref, strips_ref, spread_ref,
    ends_ref, shifts_ref, fold_ref, out_ref, dpre_ref, msg_ref,
    planes, strips, mixed, taps, sums, slot_ref, link_ref, sems, spots, grads,
):
    slots = field_ref.shape[0]
    base, mine, find_strip, find_plane = make_finder(
        slot_hbm, link_hbm, own_ref, mate_ref, first_ref, second_ref,
        planes, strips, slot_ref, link_ref, sems, False,
    )
    for pair in range(slots // 2):
        taps[pair, :, 9 * PART :, :] = jnp.ones((PARTS, PART, 10 * TILE), BF)

    square = (CH, CH)
    diagonal = lax.broadcasted_iota(jnp.int32, square, 0) == lax.broadcasted_iota(jnp.int32, square, 1)
    bias = jnp.sum(jnp.where(diagonal, bias_ref[...], 0.0), axis=1, keepdims=True)
    left = left_half((CH, TILE))
    zero = jnp.zeros((CH, TILE), F32)

    def put_spots(pair, a, i, values):
        for p in range(PARTS):
            spots[pair, p, a * PART : (a + 1) * PART, i * TILE : (i + 1) * TILE] = values[
                p * PART : (p + 1) * PART, :
            ]

    for pair in range(slots // 2):
        results = convolve_pair(
            pair, base, find_strip, find_plane, link_ref, field_ref, planes, strips,
            spread_ref, ends_ref, shifts_ref, weight_ref, mixed.at[pair], taps.at[pair], sums.at[pair],
        )
        for e, tiles in enumerate(results):
            s = 2 * pair + e
            present = jnp.where(s < mine, 1.0, 0.0)
            turned = []
            for i in range(4):
                lanes = slice(i * TILE, (i + 1) * TILE)
                pre = tiles[i] + bias
                keep = cortex_ref[s : s + 1, lanes].astype(F32) * present
                sigma = 1.0 / (1.0 + jnp.exp(-pre))
                out_ref[s, :, lanes] = (pre * sigma * keep).astype(BF)
                slope = sigma * (1.0 + pre * (1.0 - sigma))
                dpre = (upstream_ref[s, :, lanes].astype(F32) * keep * slope).astype(BF)
                dpre_ref[s, :, lanes] = dpre
                put_spots(pair, 1, 5 * e + i, dpre)
                turned.append(pltpu.roll(dpre.astype(F32), 64, 1))
            put_spots(pair, 1, 5 * e + 4, zero.astype(BF))
            turned.append(zero)
            for i in range(4):
                here = jnp.where(left, turned[i], turned[i + 1])
                put_spots(pair, 0, 5 * e + i, here.astype(BF))
                here = jnp.where(left, turned[i - 1] if i else zero, turned[i])
                put_spots(pair, 2, 5 * e + i, here.astype(BF))
            put_spots(pair, 0, 5 * e + 4, jnp.where(left, 0.0, turned[0]).astype(BF))
            put_spots(pair, 2, 5 * e + 4, jnp.where(left, turned[3], 0.0).astype(BF))
        for p in range(PARTS):
            term = lax.dot_general(
                spots[pair, p], taps[pair, p], (((1,), (1,)), ((), ())), preferred_element_type=F32
            )
            grads[p] = grads[p] + term if pair else term

    pack_bricks(slot_ref, dpre_ref, strips_ref, msg_ref)
    high = slots * 2 * CH + HEAD
    low = high + SUM_ROWS
    rows = jnp.concatenate(
        [grads[p, a * PART : (a + 1) * PART, :] for a in range(3) for p in range(PARTS)], axis=0
    )
    group = lax.broadcasted_iota(jnp.int32, rows.shape, 0) // GC % 2
    column = lax.broadcasted_iota(jnp.int32, rows.shape, 1)
    same = (column // GC % 2 == group) | (column >= 9 * PART)
    full = jnp.dot(
        jnp.where(same, rows, 0.0), fold_ref[...],
        precision=lax.Precision.HIGHEST, preferred_element_type=F32,
    ).T
    last = jnp.concatenate([full[:, TILE:], jnp.zeros((2 * GC, CH), F32)], axis=0)
    half = SUM_ROWS - 10 * GC
    last = jnp.concatenate([last[0:half], last[half:]], axis=1)
    for at, values in ((0, full[:, 0:TILE]), (10 * GC, last)):
        rounded = values.astype(BF)
        size = values.shape[0]
        msg_ref[high + at : high + at + size, :] = rounded
        msg_ref[low + at : low + at + size, :] = (values - rounded.astype(F32)).astype(BF)


def backward_kernel(pairs, *refs):
    if pairs[0] == 0:
        backward_body(pairs, *refs)
        return
    last_ref, out_ref = refs[11], refs[12]
    for s in range(2 * pairs[0]):
        out_ref[s] = last_ref[s]
    backward_body(pairs, *refs[:11], *refs[12:])


def backward_body(
    pairs, slot_hbm, link_hbm, field_ref, own_ref, mate_ref, first_ref, second_ref, weight_ref, spread_ref, ends_ref, shifts_ref, out_ref,
    planes, strips, mixed, taps, sums, slot_ref, link_ref, sems,
):
    base, mine, find_strip, find_plane = make_finder(
        slot_hbm, link_hbm, own_ref, mate_ref, first_ref, second_ref,
        planes, strips, slot_ref, link_ref, sems, True,
    )
    for pair in pairs:
        results = convolve_pair(
            pair, base, find_strip, find_plane, link_ref, field_ref, planes, strips,
            spread_ref, ends_ref, shifts_ref, weight_ref, mixed.at[pair], taps.at[pair], sums.at[pair],
        )
        for e, tiles in enumerate(results):
            s = 2 * pair + e
            present = jnp.where(s < mine, 1.0, 0.0)
            for i in range(4):
                out_ref[s, :, i * TILE : (i + 1) * TILE] = (tiles[i] * present).astype(BF)


def finish_kernel(own_ref, mate_ref, kernel_ref, bias_ref):
    odd = (lax.axis_index("bricks") & 1) == 1
    total = jnp.where(odd, mate_ref[...], own_ref[...])
    first, last = total[0 : 10 * GC, :], total[10 * GC :, :]
    turned = pltpu.roll(first, 64, 1)
    parts = (first, turned, jnp.concatenate([last, pltpu.roll(last, 64, 1)], axis=0))
    for a, part in enumerate(parts):
        kernel_ref[a * 9 * GC : (a + 1) * 9 * GC, :] = part[0 : 9 * GC, 0:CH]
    bias_ref[...] = turned[9 * GC : 9 * GC + 1, 0:CH]


VMEM = pl.BlockSpec(memory_space=pltpu.VMEM)
HBM = pl.BlockSpec(memory_space=pltpu.HBM)


def call(kernel, ins, outs, scratch=(), flops=0, size=400000, limit=24):
    return pl.pallas_call(
        kernel,
        in_specs=ins,
        out_specs=tuple(VMEM for _ in outs),
        out_shape=tuple(outs),
        scratch_shapes=list(scratch),
        compiler_params=pltpu.CompilerParams(vmem_limit_bytes=limit * 2**20),
        cost_estimate=pl.CostEstimate(flops=flops, bytes_accessed=size, transcendentals=0),
    )


def sent(block, route):
    return lax.ppermute(block, "bricks", route)


def shards(voxels, kernel, bias, cortex, slot_to_brick, neighbors, cotangent):
    slots = voxels.shape[0]
    devices = lax.axis_size("bricks")
    strips, spread, ends, shifts, fold = (jnp.asarray(t, BF) for t in tables())
    fold = fold.astype(F32)
    shape = jax.ShapeDtypeStruct
    pack_rows = slots * 2 * CH + HEAD
    near_shape = shape((NEAR_ROWS, TILE), BF)
    far_shape = shape((FAR // 2 * CH, TILE), BF)

    def routed(block, chips):
        pairs = []
        for d in range(devices):
            to = d + 2 * chips - 1 if d % 2 else d - 2 * chips + 1
            if 0 <= to < devices:
                pairs.append((d, to))
        return sent(block, pairs)

    def swapped(block, mask):
        return sent(block, [(d, d ^ mask) for d in range(devices)])

    def merged(*parts):
        rows = sum(part.shape[0] for part in parts)
        return call(merge_kernel, [VMEM] * len(parts), [shape((rows, TILE), BF)])(*parts)[0]

    def among_odd(block, step):
        return sent(block, [(d, d + step) for d in range(1, devices, 2) if 0 <= d + step < devices])

    def among_even(block, mask):
        return sent(block, [(d, d ^ mask) for d in range(0, devices, 2)])

    box = [pltpu.VMEM((4 * slots, CH, TILE), BF)]
    work = [
        pltpu.VMEM((2 * slots + 2 * NEAR + 2 * FAR + 1, CH, TILE), BF),
        pltpu.VMEM((2 * slots + 2 * EDGE, CH, TILE), BF),
        pltpu.VMEM((slots // 2, 2, 5 * CH, 2 * TILE), BF),
        pltpu.VMEM((slots // 2, PARTS, 10 * PART, 10 * TILE), BF),
        pltpu.VMEM((slots // 2, 3 * CH, 10 * TILE), F32),
        pltpu.SMEM(slot_to_brick.shape, jnp.int32),
        pltpu.SMEM(neighbors.shape, jnp.int32),
        pltpu.SemaphoreType.DMA((2,)),
    ]
    field = shape(voxels.shape, BF)

    (own,) = call(
        pack_kernel,
        [HBM] * 3,
        [shape((pack_rows, TILE), BF)],
        [pltpu.VMEM(voxels.shape, BF), pltpu.VMEM(strips.shape, BF), pltpu.SMEM(slot_to_brick.shape, jnp.int32), pltpu.SemaphoreType.DMA((3,))],
        limit=60,
    )(slot_to_brick, voxels, strips)
    mate = swapped(own, 1)
    weight_shape = shape((PARTS, 3 * PART, 9 * PART), BF)
    taps = jnp.transpose(kernel, (2, 3, 4, 1, 0)).reshape(27 * GC, CH)
    staged = call(
        weight_kernel, [VMEM], [weight_shape] * 2, [pltpu.VMEM((2 * TILE, 3 * TILE), F32)], flops=BUSY
    )(taps)
    near, far = call(
        functools.partial(route_kernel, slots), [VMEM, VMEM], [near_shape, far_shape], box,
        flops=BUSY,
    )(own, mate)
    near, far = routed(near, 1), routed(far, 2)
    near, far, staged = lax.optimization_barrier((near, far, staged))
    forward, backward = staged
    first = merged(near, far)
    second = swapped(first, 1)
    activated, dpre, own = call(
        forward_kernel,
        [HBM, HBM] + [VMEM] * 14,
        [field, field, shape((pack_rows + 2 * SUM_ROWS, TILE), BF)],
        work
        + [
            pltpu.VMEM((slots // 2, PARTS, 3 * PART, 10 * TILE), BF),
            pltpu.VMEM((PARTS, 3 * PART, 10 * PART), F32),
        ],
        flops=4 * 10**9,
    )(
        slot_to_brick, neighbors, voxels, own, mate, first, second, forward, bias.reshape(1, CH),
        cortex, cotangent, strips, spread, ends, shifts, fold,
    )
    mate = swapped(own, 1)
    *halos, total = call(
        functools.partial(route_sum_kernel, slots),
        [VMEM, VMEM],
        [near_shape, far_shape] * 2 + [shape((SUM_ROWS, TILE), F32)],
        box,
    )(own, mate)
    state = {}

    def part_backward(*pairs):
        last = [state["grad"]] if pairs[0] else []
        (state["grad"],) = call(
            functools.partial(backward_kernel, pairs),
            [HBM, HBM] + [VMEM] * (9 + len(last)),
            [field],
            work,
            flops=10**9,
        )(
            slot_to_brick, neighbors, dpre, own, mate, state["first"], state["second"], backward,
            spread, ends, shifts, *last,
        )

    pairs = list(range(slots // 2))
    masks = [2**p for p in range(1, devices.bit_length() - 1)]
    for at, mask in enumerate(masks):
        other = among_even(total, mask)
        if at == 0:
            halos = [among_odd(block, step) for block, step in zip(halos, (2, 4, -2, -4))]
        elif at == 1:
            total, other, halos = lax.optimization_barrier((total, other, halos))
        elif at == 2:
            state["first"] = merged(*halos)
            state["second"] = sent(state["first"], [(d, d - 1) for d in range(1, devices, 2)])
        elif at == 3:
            part_backward(*pairs[:-1])
        total, other, state = lax.optimization_barrier((total, other, state))
        total = total + other
    other = sent(total, [(d, d + 1) for d in range(0, devices, 2)])
    part_backward(pairs[-1])
    input_grad = state["grad"]
    kernel_sum, bias_sum = call(
        finish_kernel, [VMEM, VMEM], [shape((27 * GC, CH), F32), shape((1, CH), F32)]
    )(total, other)
    kernel_grad = jnp.transpose(kernel_sum.reshape(3, 3, 3, GC, CH), (4, 3, 0, 1, 2))
    return (activated, input_grad, kernel_grad, bias_sum.reshape(CH))


def solution(mesh):
    devices = mesh.shape["bricks"]
    assert devices & (devices - 1) == 0
    return jax.shard_map(
        shards,
        mesh=mesh,
        in_specs=(
            P("bricks", None, None),
            P(),
            P(),
            P("bricks", None),
            P("bricks"),
            P("bricks", None),
            P("bricks", None, None),
        ),
        out_specs=(P("bricks", None, None), P("bricks", None, None), P(), P()),
        check_vma=False,
    )
```

```python
import functools

import jax
import jax.numpy as jnp
import numpy as np
from jax import lax
from jax.experimental import pallas as pl
from jax.experimental.pallas import tpu as pltpu
from jax.sharding import PartitionSpec as P

CH = 64
GC = 8
PART = 16
PARTS = CH // PART
SIDES = (0, 1, 2, 3, 5, 6, 7, 8)
TILE = 128
NEAR = 8
FAR = 4
EDGE = 3
BUSY = 10**10
HEAD = 16
NEAR_ROWS = (NEAR // 2 + 2) * CH + HEAD
SUM_ROWS = 128
BF = jnp.bfloat16
F32 = jnp.float32


@functools.cache
def tables():
    strips = np.zeros((4, 512, TILE), np.float32)
    spread = np.zeros((256, 4 * TILE), np.float32)
    ends = np.zeros((4, 384, TILE), np.float32)
    shifts = np.zeros((4, 256, 8 * TILE), np.float32)
    fold = np.zeros((10 * PART, 10 * GC), np.float32)
    for bc in range(9):
        for i in range(PART):
            fold[bc * PART + i, bc * GC + i % GC] = 1
    fold[9 * PART, 9 * GC] = 1
    for half in range(2):
        for xx in range(4):
            for w in range(8):
                i, xp = 2 * half + xx // 2, xx % 2
                spread[half * 64 + xx * 8 + w, i * TILE + xp * 8 + w] = 1
                spread[half * 64 + 32 + xx * 8 + w, i * TILE + 32 + xp * 8 + w] = 1
                spread[128 + half * 64 + xx * 8 + w, i * TILE + 64 + xp * 8 + w] = 1
    for t in range(4):
        q, r = t // 2, t % 2
        own_y, own_z = (0 if q else 7), (0 if r else 7)
        far_y, far_z = 7 - own_y, 7 - own_z
        for half in range(2):
            for xx in range(4):
                for w in range(8):
                    plane = (4 * half + xx) * 64
                    strips[t, plane + own_y * 8 + w, half * 64 + xx * 8 + w] = 1
                    strips[t, plane + w * 8 + own_z, half * 64 + 32 + xx * 8 + w] = 1
        for xp in range(2):
            for w in range(8):
                ends[t, xp * 64 + far_y * 8 + w, xp * 8 + w] = 1
                ends[t, 128 + xp * 64 + w * 8 + far_z, 32 + xp * 8 + w] = 1
                ends[t, 256 + xp * 64 + far_y * 8 + w, 64 + xp * 8 + w] = 1
        out_y, out_z = (-1 if q else 8), (-1 if r else 8)
        for b in range(3):
            for c in range(3):
                if b == 1 and c == 1:
                    continue
                column = SIDES.index(b * 3 + c)
                for xp in range(2):
                    for y in range(8):
                        for z in range(8):
                            yy, zz = y + b - 1, z + c - 1
                            in_y, in_z = 0 <= yy < 8, 0 <= zz < 8
                            if in_y and in_z:
                                k = xp * 64 + yy * 8 + zz
                            elif in_z and yy == out_y:
                                k = 128 + xp * 8 + zz
                            elif in_y and zz == out_z:
                                k = 160 + xp * 8 + yy
                            elif yy == out_y and zz == out_z:
                                k = 192 + xp * 8 + far_z
                            else:
                                continue
                            shifts[t, k, column * TILE + xp * 64 + y * 8 + z] = 1
    return strips, spread, ends, shifts, fold


def left_half(shape):
    return lax.broadcasted_iota(jnp.int32, shape, len(shape) - 1) % TILE < 64


def join_halves(left, right):
    mixed = jnp.where(left_half(left.shape), left.astype(F32), right.astype(F32))
    return mixed.astype(left.dtype)


def dot(a, b):
    return jnp.dot(a, b, preferred_element_type=F32)


def count_own(slot_ref):
    total = jnp.int32(0)
    for s in range(slot_ref.shape[0]):
        total = total + (slot_ref[s] >= 0).astype(jnp.int32)
    return total


def count_sent(head):
    return jnp.max(head.astype(F32)).astype(jnp.int32)


def kind_of(brick):
    return jnp.maximum(brick, 0) & 3


def pack_bricks(slot_ref, field_ref, strips_ref, msg_ref):
    slots = field_ref.shape[0]
    for s in range(slots):
        table = strips_ref[kind_of(slot_ref[s])]
        row = s * 2 * CH
        msg_ref[row : row + CH, :] = dot(field_ref[s], table).astype(BF)
        msg_ref[row + CH : row + 2 * CH, :] = join_halves(
            field_ref[s, :, 0:TILE], field_ref[s, :, 3 * TILE : 4 * TILE]
        )
    row = slots * 2 * CH
    count = count_own(slot_ref).astype(F32)
    msg_ref[row : row + HEAD, :] = jnp.full((HEAD, TILE), count, F32).astype(BF)


def bring(pairs, sems):
    copies = [pltpu.make_async_copy(a, b, sems.at[i]) for i, (a, b) in enumerate(pairs)]
    for copy in copies:
        copy.start()
    return copies


def pack_kernel(slot_hbm, field_hbm, strips_hbm, msg_ref, field_ref, strips_ref, slot_ref, sems):
    pairs = ((slot_hbm, slot_ref), (field_hbm, field_ref), (strips_hbm, strips_ref))
    for copy in bring(pairs, sems):
        copy.wait()
    pack_bricks(slot_ref, field_ref, strips_ref, msg_ref)


def route_body(slots, own_ref, mate_ref, near_ref, far_ref, box):
    odd = (lax.axis_index("bricks") & 1) == 1
    head = slots * 2 * CH
    mine = count_sent(own_ref[head : head + HEAD, :])
    other = count_sent(mate_ref[head : head + HEAD, :])
    for s in range(2 * slots):
        box[s] = own_ref[s * CH : (s + 1) * CH, :]
        box[2 * slots + s] = mate_ref[s * CH : (s + 1) * CH, :]

    def place(j):
        up = jnp.where(j < mine, mine - 1 - j, slots + other - 1 - (j - mine))
        down = jnp.where(j < mine, j, slots + j - mine)
        return jnp.clip(jnp.where(odd, up, down), 0, 2 * slots - 1)

    half = lax.broadcasted_iota(jnp.int32, (CH, TILE), 1) // 64
    counts_here = half == odd.astype(jnp.int32)
    for j in range(0, NEAR, 2):
        first, second = [box[2 * place(j + e) + 1].astype(F32) for e in range(2)]
        both = jnp.where(counts_here, first, pltpu.roll(second, 64, 1)).astype(BF)
        near_ref[j // 2 * CH : (j // 2 + 1) * CH, :] = both
        if j < FAR:
            far_ref[j // 2 * CH : (j // 2 + 1) * CH, :] = both
    of_y = lax.broadcasted_iota(jnp.int32, (CH, TILE), 1) % 64 < 32
    row = NEAR // 2 * CH
    near_ref[row : row + CH, :] = box[2 * place(0)]
    first, second = [box[2 * place(j)].astype(F32) for j in (1, 2)]
    near_ref[row + CH : row + 2 * CH, :] = jnp.where(of_y, first, pltpu.roll(second, 32, 1)).astype(BF)
    row = (NEAR // 2 + 2) * CH
    both = (mine + other).astype(F32)
    near_ref[row : row + HEAD, :] = jnp.full((HEAD, TILE), both, F32).astype(BF)


def route_kernel(slots, own_ref, mate_ref, near_ref, far_ref, box):
    route_body(slots, own_ref, mate_ref, near_ref, far_ref, box)


def route_sum_kernel(slots, own_ref, mate_ref, near_ref, far_ref, sum_ref, box):
    route_body(slots, own_ref, mate_ref, near_ref, far_ref, box)
    high = slots * 2 * CH + HEAD
    low = high + SUM_ROWS
    parts = []
    for ref in (own_ref, mate_ref):
        parts.append(
            ref[high : high + SUM_ROWS, :].astype(F32) + ref[low : low + SUM_ROWS, :].astype(F32)
        )
    sum_ref[...] = parts[0] + parts[1]


def merge_kernel(near_ref, far_ref, out_ref):
    out_ref[0:NEAR_ROWS, :] = near_ref[...]
    out_ref[NEAR_ROWS:, :] = far_ref[...]


def weight_kernel(taps_ref, forward_ref, backward_ref, work):
    values = taps_ref[...].astype(F32)
    lanes = lax.broadcasted_iota(jnp.int32, (GC, CH), 1) // GC

    def block(tap, part):
        tile = values[tap * GC : (tap + 1) * GC, :]
        groups = (2 * part, 2 * part + 1)
        return jnp.concatenate([jnp.where(lanes == g, tile, 0.0) for g in groups], axis=0)

    work[...] = jnp.zeros_like(work)
    for part in range(PARTS):
        out = slice(part * PART, (part + 1) * PART)
        for bc in range(9):
            for a in range(3):
                work[bc * PART : (bc + 1) * PART, a * TILE : a * TILE + CH] = block(a * 9 + bc, part)
        for a in range(3):
            turned = work[:, a * TILE : (a + 1) * TILE].T
            forward_ref[part, a * PART : (a + 1) * PART, :] = turned[out, 0 : 9 * PART].astype(BF)
    for part in range(PARTS):
        out = slice(part * PART, (part + 1) * PART)
        for a in range(3):
            blocks = [block((2 - a) * 9 + 8 - bc, part)[:, out] for bc in range(9)]
            backward_ref[part, a * PART : (a + 1) * PART, :] = jnp.concatenate(blocks, axis=1).astype(BF)


def make_finder(
    slot_hbm, link_hbm, own_ref, mate_ref, first_ref, second_ref,
    planes, strips, slot_ref, link_ref, sems,
):
    copies = bring(((slot_hbm, slot_ref), (link_hbm, link_ref)), sems)
    slots = slot_ref.shape[0]
    odd = (lax.axis_index("bricks") & 1) == 1
    head = slots * 2 * CH
    mine = count_sent(own_ref[head : head + HEAD, :])
    other = count_sent(mate_ref[head : head + HEAD, :])
    row = (NEAR // 2 + 2) * CH
    counts = [count_sent(ref[row : row + HEAD, :]) for ref in (first_ref, second_ref)]
    for k, ref in enumerate((own_ref, mate_ref)):
        for s in range(slots):
            strips[k * slots + s] = ref[s * 2 * CH : s * 2 * CH + CH, :]
            planes[k * slots + s] = ref[s * 2 * CH + CH : (s + 1) * 2 * CH, :]
    for side, near in enumerate((first_ref, second_ref)):
        for start, begin, count in ((side * NEAR, 0, NEAR), (2 * NEAR + side * FAR, NEAR_ROWS, FAR)):
            for j in range(0, count, 2):
                row = begin + j // 2 * CH
                tile = near[row : row + CH, :]
                planes[2 * slots + start + j] = tile
                planes[2 * slots + start + j + 1] = pltpu.roll(tile.astype(F32), 64, 1).astype(BF)
        row, at = NEAR // 2 * CH, 2 * slots + side * EDGE
        strips[at] = near[row : row + CH, :]
        tile = near[row + CH : row + 2 * CH, :]
        strips[at + 1] = tile
        strips[at + 2] = pltpu.roll(tile.astype(F32), TILE - 32, 1).astype(BF)
    nothing = 2 * slots + 2 * NEAR + 2 * FAR
    planes[nothing] = jnp.zeros((CH, TILE), BF)
    for copy in copies:
        copy.wait()
    base = slot_ref[0]
    low_side = odd.astype(jnp.int32)
    high_side = 1 - low_side
    low_count = jnp.where(odd, counts[1], counts[0])
    high_count = jnp.where(odd, counts[0], counts[1])
    mate_first = jnp.where(odd, base - other, base + mine)
    chip_low = jnp.where(odd, base - other, base)
    chip_high = jnp.where(odd, base + mine, base + mine + other)

    def on_chip(brick):
        own = (brick >= base) & (brick < base + mine)
        return jnp.where(own, brick - base, slots + brick - mate_first)

    def find_strip(brick):
        low = 2 * slots + low_side * EDGE + (chip_low - 1 - brick)
        high = 2 * slots + high_side * EDGE + (brick - chip_high)
        at = jnp.where(brick < chip_low, low, jnp.where(brick >= chip_high, high, on_chip(brick)))
        return jnp.clip(at, 0, 2 * slots + 2 * EDGE - 1)

    def outside(distance, count, side):
        near = 2 * slots + side * NEAR + distance
        far = 2 * slots + 2 * NEAR + side * FAR + distance - count
        return jnp.where(distance < count, near, far)

    def find_plane(brick, exists):
        low = outside(chip_low - 1 - brick, low_count, low_side)
        high = outside(brick - chip_high, high_count, high_side)
        at = jnp.where(brick < chip_low, low, jnp.where(brick >= chip_high, high, on_chip(brick)))
        return jnp.clip(jnp.where(exists, at, nothing), 0, nothing)

    return base, mine, find_strip, find_plane


def convolve_pair(
    pair, base, find_strip, find_plane, link_ref, field_ref, planes, strips,
    spread_ref, ends_ref, shifts_ref, weight_ref, mixed, taps, sums,
):
    slots = (2 * pair, 2 * pair + 1)
    kinds, outers, besides = [], [], []
    of_y = lax.broadcasted_iota(jnp.int32, (CH, TILE), 1) % 64 < 32
    for s in slots:
        brick = base + s
        kind = brick & 3
        step_y = 2 - 2 * (kind & 2)
        step_z = 1 - 2 * (kind & 1)
        sides = (brick + step_y, brick + step_z, brick + step_y + step_z)
        has_low = link_ref[s, 0] >= 0
        has_high = link_ref[s, 1] >= 0

        def outer(near):
            high = planes[find_plane(near + 4, has_high)]
            low = planes[find_plane(near - 4, has_low)]
            return join_halves(high, low)

        beside_y, beside_z, beside_yz = [strips[find_strip(m)] for m in sides]
        beside = jnp.where(of_y, beside_y.astype(F32), beside_z.astype(F32)).astype(BF)
        besides.append(jnp.concatenate([beside, beside_yz], axis=1))
        kinds.append(kind)
        outers.append((outer(brick), jnp.concatenate([outer(m) for m in sides], axis=1)))
    halos = dot(jnp.concatenate(besides, axis=0), spread_ref[...]).astype(BF)
    for e, s in enumerate(slots):
        for i in range(4):
            rows = slice(i * CH, (i + 1) * CH)
            mixed[e, rows, 0:TILE] = field_ref[s, :, i * TILE : (i + 1) * TILE]
            mixed[e, rows, TILE:] = halos[e * CH : (e + 1) * CH, i * TILE : (i + 1) * TILE]
        mixed[e, 4 * CH :, 0:TILE] = outers[e][0]
        mixed[e, 4 * CH :, TILE:] = dot(outers[e][1], ends_ref[kinds[e]]).astype(BF)

    def put_taps(e, bc, values):
        for i in range(5):
            lanes = slice((5 * e + i) * TILE, (5 * e + i + 1) * TILE)
            for p in range(PARTS):
                taps[p, bc * PART : (bc + 1) * PART, lanes] = values[
                    i * CH + p * PART : i * CH + (p + 1) * PART, :
                ]

    for e in range(2):
        for k in range(0, 8, 2):
            part = dot(mixed[e], shifts_ref[kinds[e], :, k * TILE : (k + 2) * TILE]).astype(BF)
            put_taps(e, SIDES[k], part[:, 0:TILE])
            put_taps(e, SIDES[k + 1], part[:, TILE:])
        put_taps(e, 4, mixed[e, :, 0:TILE])
    for p in range(PARTS):
        part = dot(weight_ref[p], taps[p, 0 : 9 * PART, :])
        for a in range(3):
            at = a * CH + p * PART
            sums[at : at + PART, :] = part[a * PART : (a + 1) * PART, :]
    left = left_half((CH, TILE))
    results = []
    for e in range(2):
        first = 5 * e
        turned = []
        for a in (0, 2):
            rows = slice(a * CH, (a + 1) * CH)
            turned.append(
                [
                    pltpu.roll(sums[rows, (first + i) * TILE : (first + i + 1) * TILE], 64, 1)
                    for i in range(5)
                ]
            )
        tiles = []
        for i in range(4):
            lower = jnp.where(left, turned[0][(i - 1) % 5], turned[0][i])
            upper = jnp.where(left, turned[1][i], turned[1][i + 1])
            lanes = slice((first + i) * TILE, (first + i + 1) * TILE)
            tiles.append(sums[CH : 2 * CH, lanes] + lower + upper)
        results.append(tiles)
    return results


def forward_kernel(
    slot_hbm, link_hbm, field_ref, own_ref, mate_ref, first_ref, second_ref, weight_ref, bias_ref, cortex_ref, upstream_ref, strips_ref, spread_ref,
    ends_ref, shifts_ref, fold_ref, out_ref, dpre_ref, msg_ref,
    planes, strips, mixed, taps, sums, slot_ref, link_ref, sems, spots, grads,
):
    slots = field_ref.shape[0]
    base, mine, find_strip, find_plane = make_finder(
        slot_hbm, link_hbm, own_ref, mate_ref, first_ref, second_ref,
        planes, strips, slot_ref, link_ref, sems,
    )
    for pair in range(slots // 2):
        taps[pair, :, 9 * PART :, :] = jnp.ones((PARTS, PART, 10 * TILE), BF)

    square = (CH, CH)
    diagonal = lax.broadcasted_iota(jnp.int32, square, 0) == lax.broadcasted_iota(jnp.int32, square, 1)
    bias = jnp.sum(jnp.where(diagonal, bias_ref[...], 0.0), axis=1, keepdims=True)
    left = left_half((CH, TILE))
    zero = jnp.zeros((CH, TILE), F32)

    def put_spots(pair, a, i, values):
        for p in range(PARTS):
            spots[pair, p, a * PART : (a + 1) * PART, i * TILE : (i + 1) * TILE] = values[
                p * PART : (p + 1) * PART, :
            ]

    for pair in range(slots // 2):
        results = convolve_pair(
            pair, base, find_strip, find_plane, link_ref, field_ref, planes, strips,
            spread_ref, ends_ref, shifts_ref, weight_ref, mixed.at[pair], taps.at[pair], sums.at[pair],
        )
        for e, tiles in enumerate(results):
            s = 2 * pair + e
            present = jnp.where(s < mine, 1.0, 0.0)
            turned = []
            for i in range(4):
                lanes = slice(i * TILE, (i + 1) * TILE)
                pre = tiles[i] + bias
                keep = cortex_ref[s : s + 1, lanes].astype(F32) * present
                sigma = 1.0 / (1.0 + jnp.exp(-pre))
                out_ref[s, :, lanes] = (pre * sigma * keep).astype(BF)
                slope = sigma * (1.0 + pre * (1.0 - sigma))
                dpre = (upstream_ref[s, :, lanes].astype(F32) * keep * slope).astype(BF)
                dpre_ref[s, :, lanes] = dpre
                put_spots(pair, 1, 5 * e + i, dpre)
                turned.append(pltpu.roll(dpre.astype(F32), 64, 1))
            put_spots(pair, 1, 5 * e + 4, zero.astype(BF))
            turned.append(zero)
            for i in range(4):
                here = jnp.where(left, turned[i], turned[i + 1])
                put_spots(pair, 0, 5 * e + i, here.astype(BF))
                here = jnp.where(left, turned[i - 1] if i else zero, turned[i])
                put_spots(pair, 2, 5 * e + i, here.astype(BF))
            put_spots(pair, 0, 5 * e + 4, jnp.where(left, 0.0, turned[0]).astype(BF))
            put_spots(pair, 2, 5 * e + 4, jnp.where(left, turned[3], 0.0).astype(BF))
        for p in range(PARTS):
            term = lax.dot_general(
                spots[pair, p], taps[pair, p], (((1,), (1,)), ((), ())), preferred_element_type=F32
            )
            grads[p] = grads[p] + term if pair else term

    pack_bricks(slot_ref, dpre_ref, strips_ref, msg_ref)
    high = slots * 2 * CH + HEAD
    low = high + SUM_ROWS
    rows = jnp.concatenate(
        [grads[p, a * PART : (a + 1) * PART, :] for a in range(3) for p in range(PARTS)], axis=0
    )
    group = lax.broadcasted_iota(jnp.int32, rows.shape, 0) // GC % 2
    column = lax.broadcasted_iota(jnp.int32, rows.shape, 1)
    same = (column // GC % 2 == group) | (column >= 9 * PART)
    full = jnp.dot(
        jnp.where(same, rows, 0.0), fold_ref[...],
        precision=lax.Precision.HIGHEST, preferred_element_type=F32,
    ).T
    last = jnp.concatenate([full[:, TILE:], jnp.zeros((2 * GC, CH), F32)], axis=0)
    half = SUM_ROWS - 10 * GC
    last = jnp.concatenate([last[0:half], last[half:]], axis=1)
    for at, values in ((0, full[:, 0:TILE]), (10 * GC, last)):
        rounded = values.astype(BF)
        size = values.shape[0]
        msg_ref[high + at : high + at + size, :] = rounded
        msg_ref[low + at : low + at + size, :] = (values - rounded.astype(F32)).astype(BF)


def backward_kernel(pairs, *refs):
    if pairs[0] == 0:
        backward_body(pairs, *refs)
        return
    last_ref, out_ref = refs[11], refs[12]
    for s in range(2 * pairs[0]):
        out_ref[s] = last_ref[s]
    backward_body(pairs, *refs[:11], *refs[12:])


def backward_body(
    pairs, slot_hbm, link_hbm, field_ref, own_ref, mate_ref, first_ref, second_ref, weight_ref, spread_ref, ends_ref, shifts_ref, out_ref,
    planes, strips, mixed, taps, sums, slot_ref, link_ref, sems,
):
    base, mine, find_strip, find_plane = make_finder(
        slot_hbm, link_hbm, own_ref, mate_ref, first_ref, second_ref,
        planes, strips, slot_ref, link_ref, sems,
    )
    for pair in pairs:
        results = convolve_pair(
            pair, base, find_strip, find_plane, link_ref, field_ref, planes, strips,
            spread_ref, ends_ref, shifts_ref, weight_ref, mixed.at[pair], taps.at[pair], sums.at[pair],
        )
        for e, tiles in enumerate(results):
            s = 2 * pair + e
            present = jnp.where(s < mine, 1.0, 0.0)
            for i in range(4):
                out_ref[s, :, i * TILE : (i + 1) * TILE] = (tiles[i] * present).astype(BF)


def finish_kernel(a_ref, b_ref, kernel_ref, bias_ref):
    total = a_ref[...] + b_ref[...]
    first, last = total[0 : 10 * GC, :], total[10 * GC :, :]
    turned = pltpu.roll(first, 64, 1)
    parts = (first, turned, jnp.concatenate([last, pltpu.roll(last, 64, 1)], axis=0))
    for a, part in enumerate(parts):
        kernel_ref[a * 9 * GC : (a + 1) * 9 * GC, :] = part[0 : 9 * GC, 0:CH]
    bias_ref[...] = turned[9 * GC : 9 * GC + 1, 0:CH]


VMEM = pl.BlockSpec(memory_space=pltpu.VMEM)
HBM = pl.BlockSpec(memory_space=pltpu.HBM)


def call(kernel, ins, outs, scratch=(), flops=0, size=400000, limit=24):
    return pl.pallas_call(
        kernel,
        in_specs=ins,
        out_specs=tuple(VMEM for _ in outs),
        out_shape=tuple(outs),
        scratch_shapes=list(scratch),
        compiler_params=pltpu.CompilerParams(vmem_limit_bytes=int(limit * 2**20)),
        cost_estimate=pl.CostEstimate(flops=flops, bytes_accessed=size, transcendentals=0),
    )


def sent(block, route):
    return lax.ppermute(block, "bricks", route)


def shards(voxels, kernel, bias, cortex, slot_to_brick, neighbors, cotangent):
    slots = voxels.shape[0]
    devices = lax.axis_size("bricks")
    strips, spread, ends, shifts, fold = (jnp.asarray(t, BF) for t in tables())
    fold = fold.astype(F32)
    shape = jax.ShapeDtypeStruct
    pack_rows = slots * 2 * CH + HEAD
    near_shape = shape((NEAR_ROWS, TILE), BF)
    far_shape = shape((FAR // 2 * CH, TILE), BF)

    def routed(block, chips):
        pairs = []
        for d in range(devices):
            to = d + 2 * chips - 1 if d % 2 else d - 2 * chips + 1
            if 0 <= to < devices:
                pairs.append((d, to))
        return sent(block, pairs)

    def swapped(block, mask):
        return sent(block, [(d, d ^ mask) for d in range(devices)])

    def merged(near, far):
        rows = near.shape[0] + far.shape[0]
        return call(merge_kernel, [VMEM] * 2, [shape((rows, TILE), BF)])(near, far)[0]

    box = [pltpu.VMEM((4 * slots, CH, TILE), BF)]
    work = [
        pltpu.VMEM((2 * slots + 2 * NEAR + 2 * FAR + 1, CH, TILE), BF),
        pltpu.VMEM((2 * slots + 2 * EDGE, CH, TILE), BF),
        pltpu.VMEM((slots // 2, 2, 5 * CH, 2 * TILE), BF),
        pltpu.VMEM((slots // 2, PARTS, 10 * PART, 10 * TILE), BF),
        pltpu.VMEM((slots // 2, 3 * CH, 10 * TILE), F32),
        pltpu.SMEM(slot_to_brick.shape, jnp.int32),
        pltpu.SMEM(neighbors.shape, jnp.int32),
        pltpu.SemaphoreType.DMA((2,)),
    ]
    field = shape(voxels.shape, BF)

    (own,) = call(
        pack_kernel,
        [HBM] * 3,
        [shape((pack_rows, TILE), BF)],
        [pltpu.VMEM(voxels.shape, BF), pltpu.VMEM(strips.shape, BF), pltpu.SMEM(slot_to_brick.shape, jnp.int32), pltpu.SemaphoreType.DMA((3,))],
        limit=53.5,
    )(slot_to_brick, voxels, strips)
    mate = swapped(own, 1)
    weight_shape = shape((PARTS, 3 * PART, 9 * PART), BF)
    taps = jnp.transpose(kernel, (2, 3, 4, 1, 0)).reshape(27 * GC, CH)
    staged = call(
        weight_kernel, [VMEM], [weight_shape] * 2, [pltpu.VMEM((2 * TILE, 3 * TILE), F32)], flops=BUSY
    )(taps)
    near, far = call(
        functools.partial(route_kernel, slots), [VMEM, VMEM], [near_shape, far_shape], box,
        flops=BUSY,
    )(own, mate)
    near, far = routed(near, 1), routed(far, 2)
    near, far, staged = lax.optimization_barrier((near, far, staged))
    forward, backward = staged
    first = merged(near, far)
    second = merged(swapped(near, 1), swapped(far, 1))
    activated, dpre, own = call(
        forward_kernel,
        [HBM, HBM] + [VMEM] * 14,
        [field, field, shape((pack_rows + 2 * SUM_ROWS, TILE), BF)],
        work
        + [
            pltpu.VMEM((slots // 2, PARTS, 3 * PART, 10 * TILE), BF),
            pltpu.VMEM((PARTS, 3 * PART, 10 * PART), F32),
        ],
        flops=4 * 10**9,
    )(
        slot_to_brick, neighbors, voxels, own, mate, first, second, forward, bias.reshape(1, CH),
        cortex, cotangent, strips, spread, ends, shifts, fold,
    )
    mate = swapped(own, 1)
    near, far, total = call(
        functools.partial(route_sum_kernel, slots),
        [VMEM, VMEM],
        [near_shape, far_shape, shape((SUM_ROWS, TILE), F32)],
        box,
    )(own, mate)
    state = {}

    def part_backward(pair):
        last = [state["grad"]] if pair else []
        (state["grad"],) = call(
            functools.partial(backward_kernel, (pair,)),
            [HBM, HBM] + [VMEM] * (9 + len(last)),
            [field],
            work,
            flops=10**9,
        )(
            slot_to_brick, neighbors, dpre, own, mate, state["first"], state["second"], backward,
            spread, ends, shifts, *last,
        )

    pairs = list(range(slots // 2))
    masks = [2**p for p in range(1, devices.bit_length() - 1)]
    for mask in masks:
        other = swapped(total, mask)
        if mask == masks[0]:
            state["near"], state["far"] = routed(near, 1), routed(far, 2)
        elif pairs:
            if mask == masks[1]:
                state["first"] = merged(state.pop("near"), state.pop("far"))
                state["second"] = swapped(state["first"], 1)
            part_backward(pairs.pop(0))
        if mask != masks[-1]:
            total, other, state = lax.optimization_barrier((total, other, state))
            total = total + other
    for pair in pairs:
        part_backward(pair)
    input_grad = state["grad"]
    kernel_sum, bias_sum = call(
        finish_kernel, [VMEM, VMEM], [shape((27 * GC, CH), F32), shape((1, CH), F32)]
    )(total, other)
    kernel_grad = jnp.transpose(kernel_sum.reshape(3, 3, 3, GC, CH), (4, 3, 0, 1, 2))
    return (activated, input_grad, kernel_grad, bias_sum.reshape(CH))


def solution(mesh):
    devices = mesh.shape["bricks"]
    assert devices & (devices - 1) == 0
    return jax.shard_map(
        shards,
        mesh=mesh,
        in_specs=(
            P("bricks", None, None),
            P(),
            P(),
            P("bricks", None),
            P("bricks"),
            P("bricks", None),
            P("bricks", None, None),
        ),
        out_specs=(P("bricks", None, None), P("bricks", None, None), P(), P()),
        check_vma=False,
    )
```

```python
import functools

import jax
import jax.numpy as jnp
import numpy as np
from jax import lax
from jax.experimental import pallas as pl
from jax.experimental.pallas import tpu as pltpu
from jax.sharding import PartitionSpec as P

CH = 64
GC = 8
PART = 16
PARTS = CH // PART
SIDES = (0, 1, 2, 3, 5, 6, 7, 8)
TILE = 128
NEAR = 8
FAR = 4
EDGE = 3
BUSY = 10**10
HEAD = 16
NEAR_ROWS = (NEAR // 2 + 2) * CH + HEAD
SUM_ROWS = 128
BF = jnp.bfloat16
F32 = jnp.float32


@functools.cache
def tables():
    strips = np.zeros((4, 512, TILE), np.float32)
    spread = np.zeros((256, 4 * TILE), np.float32)
    ends = np.zeros((4, 384, TILE), np.float32)
    shifts = np.zeros((4, 256, 8 * TILE), np.float32)
    fold = np.zeros((10 * PART, 10 * GC), np.float32)
    for bc in range(9):
        for i in range(PART):
            fold[bc * PART + i, bc * GC + i % GC] = 1
    fold[9 * PART, 9 * GC] = 1
    for half in range(2):
        for xx in range(4):
            for w in range(8):
                i, xp = 2 * half + xx // 2, xx % 2
                spread[half * 64 + xx * 8 + w, i * TILE + xp * 8 + w] = 1
                spread[half * 64 + 32 + xx * 8 + w, i * TILE + 32 + xp * 8 + w] = 1
                spread[128 + half * 64 + xx * 8 + w, i * TILE + 64 + xp * 8 + w] = 1
    for t in range(4):
        q, r = t // 2, t % 2
        own_y, own_z = (0 if q else 7), (0 if r else 7)
        far_y, far_z = 7 - own_y, 7 - own_z
        for half in range(2):
            for xx in range(4):
                for w in range(8):
                    plane = (4 * half + xx) * 64
                    strips[t, plane + own_y * 8 + w, half * 64 + xx * 8 + w] = 1
                    strips[t, plane + w * 8 + own_z, half * 64 + 32 + xx * 8 + w] = 1
        for xp in range(2):
            for w in range(8):
                ends[t, xp * 64 + far_y * 8 + w, xp * 8 + w] = 1
                ends[t, 128 + xp * 64 + w * 8 + far_z, 32 + xp * 8 + w] = 1
                ends[t, 256 + xp * 64 + far_y * 8 + w, 64 + xp * 8 + w] = 1
        out_y, out_z = (-1 if q else 8), (-1 if r else 8)
        for b in range(3):
            for c in range(3):
                if b == 1 and c == 1:
                    continue
                column = SIDES.index(b * 3 + c)
                for xp in range(2):
                    for y in range(8):
                        for z in range(8):
                            yy, zz = y + b - 1, z + c - 1
                            in_y, in_z = 0 <= yy < 8, 0 <= zz < 8
                            if in_y and in_z:
                                k = xp * 64 + yy * 8 + zz
                            elif in_z and yy == out_y:
                                k = 128 + xp * 8 + zz
                            elif in_y and zz == out_z:
                                k = 160 + xp * 8 + yy
                            elif yy == out_y and zz == out_z:
                                k = 192 + xp * 8 + far_z
                            else:
                                continue
                            shifts[t, k, column * TILE + xp * 64 + y * 8 + z] = 1
    return strips, spread, ends, shifts, fold


def left_half(shape):
    return lax.broadcasted_iota(jnp.int32, shape, len(shape) - 1) % TILE < 64


def join_halves(left, right):
    mixed = jnp.where(left_half(left.shape), left.astype(F32), right.astype(F32))
    return mixed.astype(left.dtype)


def dot(a, b):
    return jnp.dot(a, b, preferred_element_type=F32)


def count_own(slot_ref):
    total = jnp.int32(0)
    for s in range(slot_ref.shape[0]):
        total = total + (slot_ref[s] >= 0).astype(jnp.int32)
    return total


def count_sent(head):
    return jnp.max(head.astype(F32)).astype(jnp.int32)


def kind_of(brick):
    return jnp.maximum(brick, 0) & 3


def pack_bricks(slot_ref, field_ref, strips_ref, msg_ref):
    slots = field_ref.shape[0]
    for s in range(slots):
        table = strips_ref[kind_of(slot_ref[s])]
        row = s * 2 * CH
        msg_ref[row : row + CH, :] = dot(field_ref[s], table).astype(BF)
        msg_ref[row + CH : row + 2 * CH, :] = join_halves(
            field_ref[s, :, 0:TILE], field_ref[s, :, 3 * TILE : 4 * TILE]
        )
    row = slots * 2 * CH
    count = count_own(slot_ref).astype(F32)
    msg_ref[row : row + HEAD, :] = jnp.full((HEAD, TILE), count, F32).astype(BF)


def bring(pairs, sems):
    copies = [pltpu.make_async_copy(a, b, sems.at[i]) for i, (a, b) in enumerate(pairs)]
    for copy in copies:
        copy.start()
    return copies


def pack_kernel(slot_hbm, field_hbm, strips_hbm, msg_ref, field_ref, strips_ref, slot_ref, sems):
    pairs = ((slot_hbm, slot_ref), (field_hbm, field_ref), (strips_hbm, strips_ref))
    for copy in bring(pairs, sems):
        copy.wait()
    pack_bricks(slot_ref, field_ref, strips_ref, msg_ref)


def route_body(slots, own_ref, mate_ref, near_ref, far_ref, box):
    odd = (lax.axis_index("bricks") & 1) == 1
    head = slots * 2 * CH
    mine = count_sent(own_ref[head : head + HEAD, :])
    other = count_sent(mate_ref[head : head + HEAD, :])
    for s in range(2 * slots):
        box[s] = own_ref[s * CH : (s + 1) * CH, :]
        box[2 * slots + s] = mate_ref[s * CH : (s + 1) * CH, :]

    def place(j):
        up = jnp.where(j < mine, mine - 1 - j, slots + other - 1 - (j - mine))
        down = jnp.where(j < mine, j, slots + j - mine)
        return jnp.clip(jnp.where(odd, up, down), 0, 2 * slots - 1)

    half = lax.broadcasted_iota(jnp.int32, (CH, TILE), 1) // 64
    counts_here = half == odd.astype(jnp.int32)
    for j in range(0, NEAR, 2):
        first, second = [box[2 * place(j + e) + 1].astype(F32) for e in range(2)]
        both = jnp.where(counts_here, first, pltpu.roll(second, 64, 1)).astype(BF)
        near_ref[j // 2 * CH : (j // 2 + 1) * CH, :] = both
        if j < FAR:
            far_ref[j // 2 * CH : (j // 2 + 1) * CH, :] = both
    of_y = lax.broadcasted_iota(jnp.int32, (CH, TILE), 1) % 64 < 32
    row = NEAR // 2 * CH
    near_ref[row : row + CH, :] = box[2 * place(0)]
    first, second = [box[2 * place(j)].astype(F32) for j in (1, 2)]
    near_ref[row + CH : row + 2 * CH, :] = jnp.where(of_y, first, pltpu.roll(second, 32, 1)).astype(BF)
    row = (NEAR // 2 + 2) * CH
    both = (mine + other).astype(F32)
    near_ref[row : row + HEAD, :] = jnp.full((HEAD, TILE), both, F32).astype(BF)


def route_kernel(slots, own_ref, mate_ref, near_ref, far_ref, box):
    route_body(slots, own_ref, mate_ref, near_ref, far_ref, box)


def route_sum_kernel(slots, own_ref, mate_ref, near_ref, far_ref, sum_ref, box):
    route_body(slots, own_ref, mate_ref, near_ref, far_ref, box)
    high = slots * 2 * CH + HEAD
    low = high + SUM_ROWS
    parts = []
    for ref in (own_ref, mate_ref):
        parts.append(
            ref[high : high + SUM_ROWS, :].astype(F32) + ref[low : low + SUM_ROWS, :].astype(F32)
        )
    sum_ref[...] = parts[0] + parts[1]


def merge_kernel(near_ref, far_ref, out_ref):
    out_ref[0:NEAR_ROWS, :] = near_ref[...]
    out_ref[NEAR_ROWS:, :] = far_ref[...]


def weight_kernel(taps_ref, forward_ref, backward_ref, work):
    values = taps_ref[...].astype(F32)
    lanes = lax.broadcasted_iota(jnp.int32, (GC, CH), 1) // GC

    def block(tap, part):
        tile = values[tap * GC : (tap + 1) * GC, :]
        groups = (2 * part, 2 * part + 1)
        return jnp.concatenate([jnp.where(lanes == g, tile, 0.0) for g in groups], axis=0)

    work[...] = jnp.zeros_like(work)
    for part in range(PARTS):
        out = slice(part * PART, (part + 1) * PART)
        for bc in range(9):
            for a in range(3):
                work[bc * PART : (bc + 1) * PART, a * TILE : a * TILE + CH] = block(a * 9 + bc, part)
        for a in range(3):
            turned = work[:, a * TILE : (a + 1) * TILE].T
            forward_ref[part, a * PART : (a + 1) * PART, :] = turned[out, 0 : 9 * PART].astype(BF)
    for part in range(PARTS):
        out = slice(part * PART, (part + 1) * PART)
        for a in range(3):
            blocks = [block((2 - a) * 9 + 8 - bc, part)[:, out] for bc in range(9)]
            backward_ref[part, a * PART : (a + 1) * PART, :] = jnp.concatenate(blocks, axis=1).astype(BF)


def make_finder(
    slot_hbm, link_hbm, own_ref, mate_ref, first_ref, second_ref,
    planes, strips, slot_ref, link_ref, sems,
):
    copies = bring(((slot_hbm, slot_ref), (link_hbm, link_ref)), sems)
    slots = slot_ref.shape[0]
    odd = (lax.axis_index("bricks") & 1) == 1
    head = slots * 2 * CH
    mine = count_sent(own_ref[head : head + HEAD, :])
    other = count_sent(mate_ref[head : head + HEAD, :])
    row = (NEAR // 2 + 2) * CH
    counts = [count_sent(ref[row : row + HEAD, :]) for ref in (first_ref, second_ref)]
    for k, ref in enumerate((own_ref, mate_ref)):
        for s in range(slots):
            strips[k * slots + s] = ref[s * 2 * CH : s * 2 * CH + CH, :]
            planes[k * slots + s] = ref[s * 2 * CH + CH : (s + 1) * 2 * CH, :]
    for side, near in enumerate((first_ref, second_ref)):
        for start, begin, count in ((side * NEAR, 0, NEAR), (2 * NEAR + side * FAR, NEAR_ROWS, FAR)):
            for j in range(0, count, 2):
                row = begin + j // 2 * CH
                tile = near[row : row + CH, :]
                planes[2 * slots + start + j] = tile
                planes[2 * slots + start + j + 1] = pltpu.roll(tile.astype(F32), 64, 1).astype(BF)
        row, at = NEAR // 2 * CH, 2 * slots + side * EDGE
        strips[at] = near[row : row + CH, :]
        tile = near[row + CH : row + 2 * CH, :]
        strips[at + 1] = tile
        strips[at + 2] = pltpu.roll(tile.astype(F32), TILE - 32, 1).astype(BF)
    nothing = 2 * slots + 2 * NEAR + 2 * FAR
    planes[nothing] = jnp.zeros((CH, TILE), BF)
    for copy in copies:
        copy.wait()
    base = slot_ref[0]
    low_side = odd.astype(jnp.int32)
    high_side = 1 - low_side
    low_count = jnp.where(odd, counts[1], counts[0])
    high_count = jnp.where(odd, counts[0], counts[1])
    mate_first = jnp.where(odd, base - other, base + mine)
    chip_low = jnp.where(odd, base - other, base)
    chip_high = jnp.where(odd, base + mine, base + mine + other)

    def on_chip(brick):
        own = (brick >= base) & (brick < base + mine)
        return jnp.where(own, brick - base, slots + brick - mate_first)

    def find_strip(brick):
        low = 2 * slots + low_side * EDGE + (chip_low - 1 - brick)
        high = 2 * slots + high_side * EDGE + (brick - chip_high)
        at = jnp.where(brick < chip_low, low, jnp.where(brick >= chip_high, high, on_chip(brick)))
        return jnp.clip(at, 0, 2 * slots + 2 * EDGE - 1)

    def outside(distance, count, side):
        near = 2 * slots + side * NEAR + distance
        far = 2 * slots + 2 * NEAR + side * FAR + distance - count
        return jnp.where(distance < count, near, far)

    def find_plane(brick, exists):
        low = outside(chip_low - 1 - brick, low_count, low_side)
        high = outside(brick - chip_high, high_count, high_side)
        at = jnp.where(brick < chip_low, low, jnp.where(brick >= chip_high, high, on_chip(brick)))
        return jnp.clip(jnp.where(exists, at, nothing), 0, nothing)

    return base, mine, find_strip, find_plane


def convolve_pair(
    pair, base, find_strip, find_plane, link_ref, field_ref, planes, strips,
    spread_ref, ends_ref, shifts_ref, weight_ref, mixed, taps, sums,
):
    slots = (2 * pair, 2 * pair + 1)
    kinds, outers, besides = [], [], []
    of_y = lax.broadcasted_iota(jnp.int32, (CH, TILE), 1) % 64 < 32
    for s in slots:
        brick = base + s
        kind = brick & 3
        step_y = 2 - 2 * (kind & 2)
        step_z = 1 - 2 * (kind & 1)
        sides = (brick + step_y, brick + step_z, brick + step_y + step_z)
        has_low = link_ref[s, 0] >= 0
        has_high = link_ref[s, 1] >= 0

        def outer(near):
            high = planes[find_plane(near + 4, has_high)]
            low = planes[find_plane(near - 4, has_low)]
            return join_halves(high, low)

        beside_y, beside_z, beside_yz = [strips[find_strip(m)] for m in sides]
        beside = jnp.where(of_y, beside_y.astype(F32), beside_z.astype(F32)).astype(BF)
        besides.append(jnp.concatenate([beside, beside_yz], axis=1))
        kinds.append(kind)
        outers.append((outer(brick), jnp.concatenate([outer(m) for m in sides], axis=1)))
    halos = dot(jnp.concatenate(besides, axis=0), spread_ref[...]).astype(BF)
    for e, s in enumerate(slots):
        for i in range(4):
            rows = slice(i * CH, (i + 1) * CH)
            mixed[e, rows, 0:TILE] = field_ref[s, :, i * TILE : (i + 1) * TILE]
            mixed[e, rows, TILE:] = halos[e * CH : (e + 1) * CH, i * TILE : (i + 1) * TILE]
        mixed[e, 4 * CH :, 0:TILE] = outers[e][0]
        mixed[e, 4 * CH :, TILE:] = dot(outers[e][1], ends_ref[kinds[e]]).astype(BF)

    def put_taps(e, bc, values):
        for i in range(5):
            lanes = slice((5 * e + i) * TILE, (5 * e + i + 1) * TILE)
            for p in range(PARTS):
                taps[p, bc * PART : (bc + 1) * PART, lanes] = values[
                    i * CH + p * PART : i * CH + (p + 1) * PART, :
                ]

    for e in range(2):
        for k in range(0, 8, 2):
            part = dot(mixed[e], shifts_ref[kinds[e], :, k * TILE : (k + 2) * TILE]).astype(BF)
            put_taps(e, SIDES[k], part[:, 0:TILE])
            put_taps(e, SIDES[k + 1], part[:, TILE:])
        put_taps(e, 4, mixed[e, :, 0:TILE])
    for p in range(PARTS):
        part = dot(weight_ref[p], taps[p, 0 : 9 * PART, :])
        for a in range(3):
            at = a * CH + p * PART
            sums[at : at + PART, :] = part[a * PART : (a + 1) * PART, :]
    left = left_half((CH, TILE))
    results = []
    for e in range(2):
        first = 5 * e
        turned = []
        for a in (0, 2):
            rows = slice(a * CH, (a + 1) * CH)
            turned.append(
                [
                    pltpu.roll(sums[rows, (first + i) * TILE : (first + i + 1) * TILE], 64, 1)
                    for i in range(5)
                ]
            )
        tiles = []
        for i in range(4):
            lower = jnp.where(left, turned[0][(i - 1) % 5], turned[0][i])
            upper = jnp.where(left, turned[1][i], turned[1][i + 1])
            lanes = slice((first + i) * TILE, (first + i + 1) * TILE)
            tiles.append(sums[CH : 2 * CH, lanes] + lower + upper)
        results.append(tiles)
    return results


def forward_kernel(
    slot_hbm, link_hbm, field_ref, own_ref, mate_ref, first_ref, second_ref, weight_ref, bias_ref, cortex_ref, upstream_ref, strips_ref, spread_ref,
    ends_ref, shifts_ref, fold_ref, out_ref, dpre_ref, msg_ref,
    planes, strips, mixed, taps, sums, slot_ref, link_ref, sems, spots, grads,
):
    slots = field_ref.shape[0]
    base, mine, find_strip, find_plane = make_finder(
        slot_hbm, link_hbm, own_ref, mate_ref, first_ref, second_ref,
        planes, strips, slot_ref, link_ref, sems,
    )
    for pair in range(slots // 2):
        taps[pair, :, 9 * PART :, :] = jnp.ones((PARTS, PART, 10 * TILE), BF)

    square = (CH, CH)
    diagonal = lax.broadcasted_iota(jnp.int32, square, 0) == lax.broadcasted_iota(jnp.int32, square, 1)
    bias = jnp.sum(jnp.where(diagonal, bias_ref[...], 0.0), axis=1, keepdims=True)
    left = left_half((CH, TILE))
    zero = jnp.zeros((CH, TILE), F32)

    def put_spots(pair, a, i, values):
        for p in range(PARTS):
            spots[pair, p, a * PART : (a + 1) * PART, i * TILE : (i + 1) * TILE] = values[
                p * PART : (p + 1) * PART, :
            ]

    for pair in range(slots // 2):
        results = convolve_pair(
            pair, base, find_strip, find_plane, link_ref, field_ref, planes, strips,
            spread_ref, ends_ref, shifts_ref, weight_ref, mixed.at[pair], taps.at[pair], sums.at[pair],
        )
        for e, tiles in enumerate(results):
            s = 2 * pair + e
            present = jnp.where(s < mine, 1.0, 0.0)
            turned = []
            for i in range(4):
                lanes = slice(i * TILE, (i + 1) * TILE)
                pre = tiles[i] + bias
                keep = cortex_ref[s : s + 1, lanes].astype(F32) * present
                sigma = 1.0 / (1.0 + jnp.exp(-pre))
                out_ref[s, :, lanes] = (pre * sigma * keep).astype(BF)
                slope = sigma * (1.0 + pre * (1.0 - sigma))
                dpre = (upstream_ref[s, :, lanes].astype(F32) * keep * slope).astype(BF)
                dpre_ref[s, :, lanes] = dpre
                put_spots(pair, 1, 5 * e + i, dpre)
                turned.append(pltpu.roll(dpre.astype(F32), 64, 1))
            put_spots(pair, 1, 5 * e + 4, zero.astype(BF))
            turned.append(zero)
            for i in range(4):
                here = jnp.where(left, turned[i], turned[i + 1])
                put_spots(pair, 0, 5 * e + i, here.astype(BF))
                here = jnp.where(left, turned[i - 1] if i else zero, turned[i])
                put_spots(pair, 2, 5 * e + i, here.astype(BF))
            put_spots(pair, 0, 5 * e + 4, jnp.where(left, 0.0, turned[0]).astype(BF))
            put_spots(pair, 2, 5 * e + 4, jnp.where(left, turned[3], 0.0).astype(BF))
        for p in range(PARTS):
            term = lax.dot_general(
                spots[pair, p], taps[pair, p], (((1,), (1,)), ((), ())), preferred_element_type=F32
            )
            grads[p] = grads[p] + term if pair else term

    pack_bricks(slot_ref, dpre_ref, strips_ref, msg_ref)
    high = slots * 2 * CH + HEAD
    low = high + SUM_ROWS
    rows = jnp.concatenate(
        [grads[p, a * PART : (a + 1) * PART, :] for a in range(3) for p in range(PARTS)], axis=0
    )
    group = lax.broadcasted_iota(jnp.int32, rows.shape, 0) // GC % 2
    column = lax.broadcasted_iota(jnp.int32, rows.shape, 1)
    same = (column // GC % 2 == group) | (column >= 9 * PART)
    full = jnp.dot(
        jnp.where(same, rows, 0.0), fold_ref[...],
        precision=lax.Precision.HIGHEST, preferred_element_type=F32,
    ).T
    last = jnp.concatenate([full[:, TILE:], jnp.zeros((2 * GC, CH), F32)], axis=0)
    half = SUM_ROWS - 10 * GC
    last = jnp.concatenate([last[0:half], last[half:]], axis=1)
    for at, values in ((0, full[:, 0:TILE]), (10 * GC, last)):
        rounded = values.astype(BF)
        size = values.shape[0]
        msg_ref[high + at : high + at + size, :] = rounded
        msg_ref[low + at : low + at + size, :] = (values - rounded.astype(F32)).astype(BF)


def backward_kernel(pairs, *refs):
    if pairs[0] == 0:
        backward_body(pairs, *refs)
        return
    last_ref, out_ref = refs[11], refs[12]
    for s in range(2 * pairs[0]):
        out_ref[s] = last_ref[s]
    backward_body(pairs, *refs[:11], *refs[12:])


def backward_body(
    pairs, slot_hbm, link_hbm, field_ref, own_ref, mate_ref, first_ref, second_ref, weight_ref, spread_ref, ends_ref, shifts_ref, out_ref,
    planes, strips, mixed, taps, sums, slot_ref, link_ref, sems,
):
    base, mine, find_strip, find_plane = make_finder(
        slot_hbm, link_hbm, own_ref, mate_ref, first_ref, second_ref,
        planes, strips, slot_ref, link_ref, sems,
    )
    for pair in pairs:
        results = convolve_pair(
            pair, base, find_strip, find_plane, link_ref, field_ref, planes, strips,
            spread_ref, ends_ref, shifts_ref, weight_ref, mixed.at[pair], taps.at[pair], sums.at[pair],
        )
        for e, tiles in enumerate(results):
            s = 2 * pair + e
            present = jnp.where(s < mine, 1.0, 0.0)
            for i in range(4):
                out_ref[s, :, i * TILE : (i + 1) * TILE] = (tiles[i] * present).astype(BF)


def finish_kernel(a_ref, b_ref, kernel_ref, bias_ref):
    total = a_ref[...] + b_ref[...]
    first, last = total[0 : 10 * GC, :], total[10 * GC :, :]
    turned = pltpu.roll(first, 64, 1)
    parts = (first, turned, jnp.concatenate([last, pltpu.roll(last, 64, 1)], axis=0))
    for a, part in enumerate(parts):
        kernel_ref[a * 9 * GC : (a + 1) * 9 * GC, :] = part[0 : 9 * GC, 0:CH]
    bias_ref[...] = turned[9 * GC : 9 * GC + 1, 0:CH]


VMEM = pl.BlockSpec(memory_space=pltpu.VMEM)
HBM = pl.BlockSpec(memory_space=pltpu.HBM)


def call(kernel, ins, outs, scratch=(), flops=0, size=400000, limit=24):
    return pl.pallas_call(
        kernel,
        in_specs=ins,
        out_specs=tuple(VMEM for _ in outs),
        out_shape=tuple(outs),
        scratch_shapes=list(scratch),
        compiler_params=pltpu.CompilerParams(vmem_limit_bytes=int(limit * 2**20)),
        cost_estimate=pl.CostEstimate(flops=flops, bytes_accessed=size, transcendentals=0),
    )


def sent(block, route):
    return lax.ppermute(block, "bricks", route)


def shards(voxels, kernel, bias, cortex, slot_to_brick, neighbors, cotangent):
    slots = voxels.shape[0]
    devices = lax.axis_size("bricks")
    strips, spread, ends, shifts, fold = (jnp.asarray(t, BF) for t in tables())
    fold = fold.astype(F32)
    shape = jax.ShapeDtypeStruct
    pack_rows = slots * 2 * CH + HEAD
    near_shape = shape((NEAR_ROWS, TILE), BF)
    far_shape = shape((FAR // 2 * CH, TILE), BF)

    def routed(block, chips):
        pairs = []
        for d in range(devices):
            to = d + 2 * chips - 1 if d % 2 else d - 2 * chips + 1
            if 0 <= to < devices:
                pairs.append((d, to))
        return sent(block, pairs)

    def swapped(block, mask):
        return sent(block, [(d, d ^ mask) for d in range(devices)])

    def merged(near, far):
        rows = near.shape[0] + far.shape[0]
        return call(merge_kernel, [VMEM] * 2, [shape((rows, TILE), BF)])(near, far)[0]

    box = [pltpu.VMEM((4 * slots, CH, TILE), BF)]
    work = [
        pltpu.VMEM((2 * slots + 2 * NEAR + 2 * FAR + 1, CH, TILE), BF),
        pltpu.VMEM((2 * slots + 2 * EDGE, CH, TILE), BF),
        pltpu.VMEM((slots // 2, 2, 5 * CH, 2 * TILE), BF),
        pltpu.VMEM((slots // 2, PARTS, 10 * PART, 10 * TILE), BF),
        pltpu.VMEM((slots // 2, 3 * CH, 10 * TILE), F32),
        pltpu.SMEM(slot_to_brick.shape, jnp.int32),
        pltpu.SMEM(neighbors.shape, jnp.int32),
        pltpu.SemaphoreType.DMA((2,)),
    ]
    field = shape(voxels.shape, BF)

    (own,) = call(
        pack_kernel,
        [HBM] * 3,
        [shape((pack_rows, TILE), BF)],
        [pltpu.VMEM(voxels.shape, BF), pltpu.VMEM(strips.shape, BF), pltpu.SMEM(slot_to_brick.shape, jnp.int32), pltpu.SemaphoreType.DMA((3,))],
        limit=53.5,
    )(slot_to_brick, voxels, strips)
    mate = swapped(own, 1)
    weight_shape = shape((PARTS, 3 * PART, 9 * PART), BF)
    taps = jnp.transpose(kernel, (2, 3, 4, 1, 0)).reshape(27 * GC, CH)
    staged = call(
        weight_kernel, [VMEM], [weight_shape] * 2, [pltpu.VMEM((2 * TILE, 3 * TILE), F32)], flops=BUSY
    )(taps)
    near, far = call(
        functools.partial(route_kernel, slots), [VMEM, VMEM], [near_shape, far_shape], box,
        flops=BUSY,
    )(own, mate)
    far, near = routed(far, 2), routed(near, 1)
    near, far, staged = lax.optimization_barrier((near, far, staged))
    forward, backward = staged
    first = merged(near, far)
    second = merged(swapped(near, 1), swapped(far, 1))
    activated, dpre, own = call(
        forward_kernel,
        [HBM, HBM] + [VMEM] * 14,
        [field, field, shape((pack_rows + 2 * SUM_ROWS, TILE), BF)],
        work
        + [
            pltpu.VMEM((slots // 2, PARTS, 3 * PART, 10 * TILE), BF),
            pltpu.VMEM((PARTS, 3 * PART, 10 * PART), F32),
        ],
        flops=4 * 10**9,
    )(
        slot_to_brick, neighbors, voxels, own, mate, first, second, forward, bias.reshape(1, CH),
        cortex, cotangent, strips, spread, ends, shifts, fold,
    )
    mate = swapped(own, 1)
    near, far, total = call(
        functools.partial(route_sum_kernel, slots),
        [VMEM, VMEM],
        [near_shape, far_shape, shape((SUM_ROWS, TILE), F32)],
        box,
    )(own, mate)
    state = {}

    def part_backward(pair):
        last = [state["grad"]] if pair else []
        (state["grad"],) = call(
            functools.partial(backward_kernel, (pair,)),
            [HBM, HBM] + [VMEM] * (9 + len(last)),
            [field],
            work,
            flops=10**9,
        )(
            slot_to_brick, neighbors, dpre, own, mate, state["first"], state["second"], backward,
            spread, ends, shifts, *last,
        )

    pairs = list(range(slots // 2))
    masks = [2**p for p in range(1, devices.bit_length() - 1)]
    for mask in masks:
        other = swapped(total, mask)
        if mask == masks[0]:
            state["near"], state["far"] = routed(near, 1), routed(far, 2)
        elif pairs:
            if mask == masks[1]:
                state["first"] = merged(state.pop("near"), state.pop("far"))
                state["second"] = swapped(state["first"], 1)
            part_backward(pairs.pop(0))
        if mask != masks[-1]:
            total, other, state = lax.optimization_barrier((total, other, state))
            total = total + other
    for pair in pairs:
        part_backward(pair)
    input_grad = state["grad"]
    kernel_sum, bias_sum = call(
        finish_kernel, [VMEM, VMEM], [shape((27 * GC, CH), F32), shape((1, CH), F32)]
    )(total, other)
    kernel_grad = jnp.transpose(kernel_sum.reshape(3, 3, 3, GC, CH), (4, 3, 0, 1, 2))
    return (activated, input_grad, kernel_grad, bias_sum.reshape(CH))


def solution(mesh):
    devices = mesh.shape["bricks"]
    assert devices & (devices - 1) == 0
    return jax.shard_map(
        shards,
        mesh=mesh,
        in_specs=(
            P("bricks", None, None),
            P(),
            P(),
            P("bricks", None),
            P("bricks"),
            P("bricks", None),
            P("bricks", None, None),
        ),
        out_specs=(P("bricks", None, None), P("bricks", None, None), P(), P()),
        check_vma=False,
    )
```
